32 devices in a mesh: seq: 4 (over y, x), dp: 8 (over z, core).
Axes of the slice: x: 2, y: 2, z: 4, core: 2. Of those that a mesh axis runs over, the one named last changes fastest.
Arguments:
- codes: int32 [16, 3072], P('dp', 'seq'), may hold values from 0 to 511
- actions: int32 [16, 3072], P('dp', 'seq'), may hold values from 0 to 17
- next_codes: int32 [16, 3072], P('dp', 'seq'), may hold values from 0 to 511
- lengths: int32 [16, 8], P('dp'), may hold values from 0 to 3072, as said below
- rewards: float32 [16, 3072], P('dp', 'seq'), may hold values from -6 to 6
- continues: float32 [16, 3072], P('dp', 'seq'), may hold values from 0 to 1
- target_values: float32 [16, 3072], P('dp', 'seq'), may hold values from -6 to 6
- table: float32 [530, 256], replicated, may hold values from -6 to 6
- table_m: float32 [530, 256], replicated, may hold values from -1.1444092e-05 to 1.1444092e-05
- table_v: float32 [530, 256], replicated, may hold values from 5.41632e-14 to 2.166528e-13
- attn_in: float32 [2, 256, 768], replicated, may hold values from -0.375 to 0.375
- attn_in_m: float32 [2, 256, 768], replicated, may hold values from -6.1035156e-05 to 6.1035156e-05
- attn_in_v: float32 [2, 256, 768], replicated, may hold values from 1.35408e-12 to 5.41632e-12
- attn_out: float32 [2, 256, 256], replicated, may hold values from -1 to 1
- attn_out_m: float32 [2, 256, 256], replicated, may hold values from -6.1035156e-05 to 6.1035156e-05
- attn_out_v: float32 [2, 256, 256], replicated, may hold values from 1.35408e-12 to 5.41632e-12
- ffn_in: float32 [2, 256, 1024], replicated, may hold values from -0.375 to 0.375
- ffn_in_m: float32 [2, 256, 1024], replicated, may hold values from -6.1035156e-05 to 6.1035156e-05
- ffn_in_v: float32 [2, 256, 1024], replicated, may hold values from 1.35408e-12 to 5.41632e-12
- ffn_out: float32 [2, 1024, 256], replicated, may hold values from -0.1875 to 0.1875
- ffn_out_m: float32 [2, 1024, 256], replicated, may hold values from -6.1035156e-05 to 6.1035156e-05
- ffn_out_v: float32 [2, 1024, 256], replicated, may hold values from 1.35408e-12 to 5.41632e-12
- gains: float32 [5, 256], replicated, may hold values from 0.5 to 1.5
- gains_m: float32 [5, 256], replicated, may hold values from -6.1035156e-05 to 6.1035156e-05
- gains_v: float32 [5, 256], replicated, may hold values from 1.35408e-12 to 5.41632e-12
- readout: float32 [256, 533], replicated, may hold values from -0.375 to 0.375
- readout_m: float32 [256, 533], replicated, may hold values from -6.1035156e-05 to 6.1035156e-05
- readout_v: float32 [256, 533], replicated, may hold values from 1.35408e-12 to 5.41632e-12
Outputs:
- table_new: float32 [530, 256], replicated
- table_m_new: float32 [530, 256], replicated
- table_v_new: float32 [530, 256], replicated
- attn_in_new: float32 [2, 256, 768], replicated
- attn_in_m_new: float32 [2, 256, 768], replicated
- attn_in_v_new: float32 [2, 256, 768], replicated
- attn_out_new: float32 [2, 256, 256], replicated
- attn_out_m_new: float32 [2, 256, 256], replicated
- attn_out_v_new: float32 [2, 256, 256], replicated
- ffn_in_new: float32 [2, 256, 1024], replicated
- ffn_in_m_new: float32 [2, 256, 1024], replicated
- ffn_in_v_new: float32 [2, 256, 1024], replicated
- ffn_out_new: float32 [2, 1024, 256], replicated
- ffn_out_m_new: float32 [2, 1024, 256], replicated
- ffn_out_v_new: float32 [2, 1024, 256], replicated
- gains_new: float32 [5, 256], replicated
- gains_m_new: float32 [5, 256], replicated
- gains_v_new: float32 [5, 256], replicated
- readout_new: float32 [256, 533], replicated
- readout_m_new: float32 [256, 533], replicated
- readout_v_new: float32 [256, 533], replicated
- loss_sum: float32 [], replicated
- step_count: float32 [], replicated
- grad_norm: float32 [], replicated
The draws below stay inside these ranges and needn't reach their ends.
Inputs may be any that keep to these rules, and one draw needn't show every extreme that they name: Each sequence's lengths sum to 3072; lengths may be 0; in each block of 2 sequences one sequence is a single episode.
All inputs are finite; a program needn't handle non-finite values.
Results may differ from the reference program's by a relative error of at most 0.0066.
Values may be sent and summed in bfloat16 or wider, within the bound.
A program may use at most 256 MiB of HBM per device.

```python
import math
import jax
import jax.numpy as jnp
import numpy as np
from jax import lax

D = 256
HEADS = 8
FF = 1024
VOCAB = 512
ACTIONS = 18
LAYERS = 2
SEG = 48
EPISODES = 8
STEP = 5
B_DEV = 2
SEQ_LEN = 3072
SEQS = 16
PARAMS = 1846272


def draw_lengths(key, part):
    key = jax.random.fold_in(key, 11)
    cut_key, pick_key = jax.random.split(key)
    cuts = jnp.sort(jax.random.randint(cut_key, (SEQS, EPISODES - 1), 1, SEQ_LEN), axis=-1)
    chosen_row = jax.random.randint(pick_key, (), 0, B_DEV)
    single = (jnp.arange(SEQS) % B_DEV == chosen_row)[:, None]
    cuts = jnp.where(single, SEQ_LEN, cuts)
    edges = jnp.concatenate([jnp.zeros((SEQS, 1), jnp.int32), cuts.astype(jnp.int32), jnp.full((SEQS, 1), SEQ_LEN, jnp.int32)], axis=1)
    return (edges[:, 1:] - edges[:, :-1]).astype(jnp.int32)


def draw_rewards(key, part):
    key = jax.random.fold_in(key, 23)
    noise = jax.random.normal(key, (SEQS, SEQ_LEN), jnp.float32)
    values = noise
    return jnp.clip(values, -6.0, 6.0)


def draw_continues(key, part):
    key = jax.random.fold_in(key, 29)
    spread = jax.random.uniform(key, (SEQS, SEQ_LEN), jnp.float32)
    values = spread
    return values


def plant(entries, rng, smallest, high):
    spot = [jax.random.randint(jax.random.fold_in(rng, axis), (), 0, length) for axis, length in enumerate(entries.shape)]
    widest = entries.shape.index(max(entries.shape))
    neighbour = spot[:widest] + [(spot[widest] + 1) % entries.shape[widest]] + spot[widest + 1:]
    return entries.at[tuple(spot)].set(smallest).at[tuple(neighbour)].set(high)


def level_of(rng, extent, cuts, smallest, high):
    factor_of, own = 1.0, jax.random.fold_in(rng, 6)
    for axis_at, shards_of in cuts:
        steps = jnp.exp(jax.random.uniform(jax.random.fold_in(own, axis_at), (shards_of,), jnp.float32, smallest / len(cuts), high / len(cuts)))
        factor_of = factor_of * jnp.repeat(steps, extent[axis_at] // shards_of).reshape([-1 if axis == axis_at else 1 for axis in range(len(extent))])
    return factor_of


def rank_bounds(number_of, lean):
    loads = [(1 << 20) // math.isqrt(rank ** lean) + 1 for rank in range(1, number_of + 1)]
    deviation = 1 + sum(loads) // (1 << 30)
    return np.cumsum(np.array([max(1, weight // deviation) for weight in loads]))


def ranked_ids(key, shape, number_of, skew):
    listing = rank_bounds(number_of, skew)
    ticket = jax.random.randint(jax.random.fold_in(key, 1), shape, 0, int(listing[number_of - 1]))
    grade = jnp.searchsorted(jnp.asarray(listing, jnp.int32), ticket, side="right")
    return jax.random.permutation(jax.random.fold_in(key, 2), number_of)[grade].astype(jnp.int32)


def centred(stream_key, shape, scale, reach, pieces=(), kind=jnp.bfloat16):
    gain = level_of(stream_key, shape, pieces, -0.22, 0.18) if pieces else 1.0
    entries = jax.random.normal(stream_key, shape, jnp.float32) * scale * gain
    return jnp.minimum(jnp.maximum(entries, -reach), reach).astype(kind)


def setup_inputs(seed: int = 0) -> dict:
    key_list = jax.random.split(jax.random.key(seed), 29)
    return {
        "codes": plant(ranked_ids(key_list[0], (SEQS, SEQ_LEN), VOCAB, 2), jax.random.fold_in(key_list[0], 3), 0, VOCAB - 1).astype(jnp.int32),
        "actions": plant(jax.random.randint(key_list[1], (SEQS, SEQ_LEN), 0, ACTIONS), jax.random.fold_in(key_list[1], 1), 0, ACTIONS - 1).astype(jnp.int32),
        "next_codes": plant(ranked_ids(key_list[2], (SEQS, SEQ_LEN), VOCAB, 2), jax.random.fold_in(key_list[2], 3), 0, VOCAB - 1).astype(jnp.int32),
        "lengths": draw_lengths(jax.random.fold_in(key_list[28], 71), 0),
        "rewards": draw_rewards(jax.random.fold_in(key_list[28], 71), 0),
        "continues": draw_continues(jax.random.fold_in(key_list[28], 71), 0),
        "target_values": centred(key_list[6], (SEQS, SEQ_LEN), 1.0, 6.0, ((0, 8), (1, 4)), jnp.float32),
        "table": centred(key_list[7], (VOCAB + ACTIONS, D), 1.0, 6.0, (), jnp.float32),
        "table_m": centred(key_list[8], (VOCAB + ACTIONS, D), (0.0222 * 0.05 / PARAMS ** 0.5), 1.1444091796875e-05, (), jnp.float32),
        "table_v": jnp.clip(jnp.exp(jax.random.uniform(key_list[9], (VOCAB + ACTIONS, D), jnp.float32, math.log(5.416319993965628e-14), math.log(2.1665279975862511e-13))), 5.416319993965628e-14, 2.1665279975862511e-13),
        "attn_in": centred(key_list[10], (LAYERS, D, 3 * D), D ** -0.5, 0.375, (), jnp.float32),
        "attn_in_m": centred(key_list[11], (LAYERS, D, 3 * D), (0.111 * 0.05 / PARAMS ** 0.5), 6.103515625e-05, (), jnp.float32),
        "attn_in_v": jnp.clip(jnp.exp(jax.random.uniform(key_list[12], (LAYERS, D, 3 * D), jnp.float32, math.log(1.3540800425371202e-12), math.log(5.416320170148481e-12))), 1.3540800425371202e-12, 5.416320170148481e-12),
        "attn_out": centred(key_list[13], (LAYERS, D, D), (D // 8) ** -0.5, 1.0, (), jnp.float32),
        "attn_out_m": centred(key_list[14], (LAYERS, D, D), (0.111 * 0.05 / PARAMS ** 0.5), 6.103515625e-05, (), jnp.float32),
        "attn_out_v": jnp.clip(jnp.exp(jax.random.uniform(key_list[15], (LAYERS, D, D), jnp.float32, math.log(1.3540800425371202e-12), math.log(5.416320170148481e-12))), 1.3540800425371202e-12, 5.416320170148481e-12),
        "ffn_in": centred(key_list[16], (LAYERS, D, FF), D ** -0.5, 0.375, (), jnp.float32),
        "ffn_in_m": centred(key_list[17], (LAYERS, D, FF), (0.111 * 0.05 / PARAMS ** 0.5), 6.103515625e-05, (), jnp.float32),
        "ffn_in_v": jnp.clip(jnp.exp(jax.random.uniform(key_list[18], (LAYERS, D, FF), jnp.float32, math.log(1.3540800425371202e-12), math.log(5.416320170148481e-12))), 1.3540800425371202e-12, 5.416320170148481e-12),
        "ffn_out": centred(key_list[19], (LAYERS, FF, D), FF ** -0.5, 0.1875, (), jnp.float32),
        "ffn_out_m": centred(key_list[20], (LAYERS, FF, D), (0.111 * 0.05 / PARAMS ** 0.5), 6.103515625e-05, (), jnp.float32),
        "ffn_out_v": jnp.clip(jnp.exp(jax.random.uniform(key_list[21], (LAYERS, FF, D), jnp.float32, math.log(1.3540800425371202e-12), math.log(5.416320170148481e-12))), 1.3540800425371202e-12, 5.416320170148481e-12),
        "gains": jnp.clip(1.0 + 0.1 * jax.random.normal(key_list[22], (2 * LAYERS + 1, D), jnp.float32), 0.5, 1.5),
        "gains_m": centred(key_list[23], (2 * LAYERS + 1, D), (0.111 * 0.05 / PARAMS ** 0.5), 6.103515625e-05, (), jnp.float32),
        "gains_v": jnp.clip(jnp.exp(jax.random.uniform(key_list[24], (2 * LAYERS + 1, D), jnp.float32, math.log(1.3540800425371202e-12), math.log(5.416320170148481e-12))), 1.3540800425371202e-12, 5.416320170148481e-12),
        "readout": centred(key_list[25], (D, VOCAB + 3 + ACTIONS), D ** -0.5, 0.375, (), jnp.float32),
        "readout_m": centred(key_list[26], (D, VOCAB + 3 + ACTIONS), (0.111 * 0.05 / PARAMS ** 0.5), 6.103515625e-05, (), jnp.float32),
        "readout_v": jnp.clip(jnp.exp(jax.random.uniform(key_list[27], (D, VOCAB + 3 + ACTIONS), jnp.float32, math.log(1.3540800425371202e-12), math.log(5.416320170148481e-12))), 1.3540800425371202e-12, 5.416320170148481e-12),
    }


EPS_NORM = 1e-06
BETA_ONE = 0.9
BETA_TWO = 0.999
RATES = (0.25, 0.02, 0.08, 0.02, 0.02, 0.25, 0.02)
DECAY = 0.01
ADAM_EPS = 1e-08
CLIP_NORM = 0.05
GAMMA = 0.985
LAMBDA_RET = 0.95
ENTROPY_COEF = 0.05
HI = lax.Precision.HIGHEST

@jax.custom_vjp
def low(v):
    return lax.optimization_barrier(v.astype(jnp.bfloat16)).astype(jnp.float32)

@jax.custom_vjp
def low_back(v):
    return v

def low_keep(v):
    return (low(v), None)

def low_pass(kept, grad):
    return (grad,)

def back_keep(v):
    return (v, None)

def back_low(kept, grad):
    return (low(grad),)
low.defvjp(low_keep, low_pass)
low_back.defvjp(back_keep, back_low)

def mat_hi(left, right):
    return jnp.dot(left, right, precision=HI)

def rms_norm(hidden, gain_vec):
    return hidden * lax.rsqrt(lax.optimization_barrier(jnp.mean(hidden * hidden, axis=-1, keepdims=True)) + EPS_NORM) * gain_vec

def gelu_tanh(values):
    return jax.nn.gelu(values, approximate=True)

def episode_marks(lengths, positions):
    ep_ends = jnp.cumsum(lengths, axis=-1)
    passed = positions[None, :, None] >= ep_ends[:, None, :]
    doc_ids = lax.optimization_barrier(jnp.sum(passed.astype(jnp.int32), axis=-1))
    doc_ids = jnp.where(positions[None, :] < 0, jnp.int32(-1), doc_ids).astype(jnp.int32)
    ep_start = lax.optimization_barrier(jnp.max(jnp.where(passed, ep_ends[:, None, :], 0), axis=-1))
    ep_final = jnp.any(positions[None, :, None] + 1 == ep_ends[:, None, :], axis=-1)
    return (doc_ids, positions[None, :] - ep_start, ep_final)

def tile_allowed(doc_ids, span_len):
    batch_rows = doc_ids.shape[0]
    tiles = span_len // SEG
    key_docs = jnp.concatenate([doc_ids[:, :span_len].reshape(batch_rows, tiles, SEG), doc_ids[:, SEG:].reshape(batch_rows, tiles, SEG)], axis=-1)
    query_docs = doc_ids[:, SEG:].reshape(batch_rows, tiles, SEG)
    causal = jnp.arange(2 * SEG)[None, :] <= SEG + jnp.arange(SEG)[:, None]
    return causal[None, None] & (key_docs[:, :, None, :] == query_docs[..., None])

def position_code(rel_pos, dims):
    frequency = jnp.exp(jnp.arange(dims // 2).astype(jnp.float32) * (-2.0 * math.log(10000.0) / dims))
    angles = rel_pos[..., None].astype(jnp.float32) * frequency
    return jnp.concatenate([jnp.sin(angles), jnp.cos(angles)], axis=-1)

def lambda_returns(rewards, continues, values):
    rew_steps = jnp.moveaxis(rewards, -1, 0)
    cont_steps = jnp.moveaxis(continues, -1, 0)
    value_steps = jnp.moveaxis(values, -1, 0)

    def back_step(later_ret, step_items):
        reward_now, cont_now, value_next = step_items
        now_ret = reward_now + GAMMA * cont_now * ((1.0 - LAMBDA_RET) * value_next + LAMBDA_RET * later_ret)
        return (now_ret, now_ret)
    last_ret = value_steps[-1]
    unused, early_ret = lax.scan(back_step, last_ret, (rew_steps[:-1], cont_steps[:-1], value_steps[1:]), reverse=True)
    full_ret = jnp.concatenate([early_ret, last_ret[None]], axis=0)
    return jnp.moveaxis(full_ret, 0, -1)

def token_losses(outputs, next_codes, actions, rewards, continues, target_values, returns):
    logits = outputs[..., :VOCAB]
    picked = jnp.take_along_axis(logits, next_codes[..., None], axis=-1)[..., 0]
    cross_ent = jax.nn.logsumexp(logits, axis=-1) - picked
    reward_err = 0.5 * jnp.square(outputs[..., VOCAB] - rewards)
    end_logit = outputs[..., VOCAB + 1]
    ending = jax.nn.softplus(end_logit) - continues * end_logit
    critic = outputs[..., VOCAB + 2]
    log_policy = jax.nn.log_softmax(outputs[..., VOCAB + 3:], axis=-1)
    chosen = jnp.take_along_axis(log_policy, actions[..., None], axis=-1)[..., 0]
    entropy = -lax.optimization_barrier(jnp.sum(jnp.exp(log_policy) * log_policy, axis=-1))
    policy = -(returns - target_values) * chosen - ENTROPY_COEF * entropy
    value_err = 0.5 * jnp.square(critic - returns)
    return cross_ent + reward_err + ending + policy + value_err

def adam_update(weight, first_mom, second_mom, clipped, rate):
    new_first = BETA_ONE * first_mom + (1.0 - BETA_ONE) * clipped
    new_second = BETA_TWO * second_mom + (1.0 - BETA_TWO) * clipped * clipped
    ratio = new_first / (1.0 - BETA_ONE ** STEP) / (jnp.sqrt(new_second / (1.0 - BETA_TWO ** STEP)) + ADAM_EPS)
    return (weight - rate * (ratio + DECAY * weight), new_first, new_second)

def tile_kv(new_part, seq_batch, seq_len):
    tiles = seq_len // SEG
    full = new_part.reshape(seq_batch, seq_len, D)
    blank = jnp.zeros((seq_batch, SEG, D), new_part.dtype)
    before = jnp.concatenate([blank, full[:, :seq_len - SEG]], axis=1).reshape(seq_batch, tiles, SEG, D)
    return jnp.concatenate([before, full.reshape(seq_batch, tiles, SEG, D)], axis=2).reshape(seq_batch, tiles, 2 * SEG, HEADS, D // HEADS)

def forward_loss(params, batch_items):
    table, attn_in, attn_out, ffn_in, ffn_out, gains, readout = params
    codes, actions, next_codes, rewards, continues, target_values, returns, is_valid, allowed, pos_codes = batch_items
    seq_batch, seq_len = codes.shape
    tok_rows = seq_batch * seq_len
    tiles = seq_len // SEG
    span = jnp.arange(table.shape[0])
    onehot = ((span == codes[..., None]) | (span == actions[..., None] + VOCAB)).astype(table.dtype)
    hidden = low_back(mat_hi(onehot.reshape(tok_rows, -1), low(table))) + pos_codes.reshape(tok_rows, D)
    head_dim = D // HEADS
    score_scale = head_dim ** (-0.5)
    for layer_idx in range(LAYERS):
        normed = low(rms_norm(hidden, gains[2 * layer_idx]))
        mixed = low(low_back(mat_hi(normed, low(attn_in[layer_idx]))))
        query_part, key_part, value_part = jnp.split(mixed, 3, axis=1)
        query_heads = query_part.reshape(seq_batch, tiles, SEG, HEADS, head_dim)
        key_heads = tile_kv(key_part, seq_batch, seq_len)
        value_heads = tile_kv(value_part, seq_batch, seq_len)
        scores = low_back(jnp.einsum('btqhe,btkhe->bthqk', query_heads, key_heads, precision=HI) * score_scale)
        scores = jnp.where(allowed[:, :, None], scores, -1000000000.0)
        attn_probs = low(jax.nn.softmax(scores, axis=-1))
        attn_mix = low(low_back(jnp.einsum('bthqk,btkhe->btqhe', attn_probs, value_heads, precision=HI))).reshape(tok_rows, D)
        hidden = hidden + low_back(mat_hi(attn_mix, low(attn_out[layer_idx])))
        normed = low(rms_norm(hidden, gains[2 * layer_idx + 1]))
        up_proj = low_back(mat_hi(normed, low(ffn_in[layer_idx])))
        hidden = hidden + low_back(mat_hi(low(gelu_tanh(up_proj)), low(ffn_out[layer_idx])))
    final_in = low(rms_norm(hidden, gains[2 * LAYERS]))
    outputs = low_back(mat_hi(final_in, low(readout)))
    losses = token_losses(outputs, next_codes.reshape(tok_rows), actions.reshape(tok_rows), rewards.reshape(tok_rows), continues.reshape(tok_rows), target_values.reshape(tok_rows), returns.reshape(tok_rows))
    return jnp.sum(is_valid.reshape(tok_rows) * losses)

def reference(codes, actions, next_codes, lengths, rewards, continues, target_values, table, table_m, table_v, attn_in, attn_in_m, attn_in_v, attn_out, attn_out_m, attn_out_v, ffn_in, ffn_in_m, ffn_in_v, ffn_out, ffn_out_m, ffn_out_v, gains, gains_m, gains_v, readout, readout_m, readout_v):
    params = (table, attn_in, attn_out, ffn_in, ffn_out, gains, readout)
    firsts = (table_m, attn_in_m, attn_out_m, ffn_in_m, ffn_out_m, gains_m, readout_m)
    seconds = (table_v, attn_in_v, attn_out_v, ffn_in_v, ffn_out_v, gains_v, readout_v)
    group_size = 1
    group_count = SEQS // group_size
    positions = jnp.arange(-SEG, SEQ_LEN).astype(jnp.int32)

    def regroup(values):
        return values.reshape((group_count, group_size) + values.shape[1:])

    def one_group(running, group_items):
        codes_g, actions_g, next_g, lengths_g, rewards_g, continues_g, values_g = group_items
        doc_ids, rel_pos, ep_final = episode_marks(lengths_g, positions)
        allowed = tile_allowed(doc_ids, SEQ_LEN)
        is_valid = jnp.logical_not(ep_final[:, SEG:]).astype(rewards_g.dtype)
        pos_codes = position_code(rel_pos[:, SEG:], D)
        returns = lambda_returns(rewards_g.reshape(group_size, SEQ_LEN // SEG, SEG), continues_g.reshape(group_size, SEQ_LEN // SEG, SEG), values_g.reshape(group_size, SEQ_LEN // SEG, SEG)).reshape(group_size, SEQ_LEN)
        batch_items = (codes_g, actions_g, next_g, rewards_g, continues_g, values_g, returns, is_valid, allowed, pos_codes)
        loss_val, pullback = jax.vjp(lambda weights: forward_loss(weights, batch_items), params)
        grad_list = pullback(jnp.ones((), loss_val.dtype))[0]
        grad_sums, loss_total, count_total = running
        return ((jax.tree.map(jnp.add, grad_sums, grad_list), loss_total + loss_val, count_total + jnp.sum(is_valid)), None)
    start_state = (jax.tree.map(jnp.zeros_like, params), jnp.zeros((), rewards.dtype), jnp.zeros((), rewards.dtype))
    group_inputs = (regroup(codes), regroup(actions), regroup(next_codes), regroup(lengths), regroup(rewards), regroup(continues), regroup(target_values))
    (grad_sums, loss_sum, step_count), unused = lax.scan(one_group, start_state, group_inputs)
    averaged = [grad / step_count for grad in grad_sums]
    grad_norm = jnp.sqrt(sum((jnp.sum(grad * grad) for grad in averaged)))
    factor = jnp.minimum(1.0, CLIP_NORM / grad_norm)
    updated = [adam_update(params[slot], firsts[slot], seconds[slot], averaged[slot] * factor, RATES[slot]) for slot in range(7)]
    return (updated[0][0], updated[0][1], updated[0][2], updated[1][0], updated[1][1], updated[1][2], updated[2][0], updated[2][1], updated[2][2], updated[3][0], updated[3][1], updated[3][2], updated[4][0], updated[4][1], updated[4][2], updated[5][0], updated[5][1], updated[5][2], updated[6][0], updated[6][1], updated[6][2], loss_sum, step_count, grad_norm)
```

```python
import functools
import math

import jax
import jax.numpy as jnp
from jax import lax
from jax.experimental import pallas as pl
from jax.experimental.pallas import tpu as pltpu
from jax.sharding import PartitionSpec as P

HEADS = 8
VOCAB = 512
SEG = 48
STEP = 5

EPS_NORM = 1e-06
BETA_ONE = 0.9
BETA_TWO = 0.999
RATES = (0.25, 0.02, 0.08, 0.02, 0.02, 0.25, 0.02)
DECAY = 0.01
ADAM_EPS = 1e-08
CLIP_NORM = 0.05
GAMMA = 0.985
LAMBDA_RET = 0.95
ENTROPY_COEF = 0.05

BF = jnp.bfloat16
F32 = jnp.float32
ROWS = 256
WIN = 128
OUTS = 544
NEG = -1e30
MESH = pl.DeviceIdType.MESH


def dot_nn(left, right):
    return jnp.dot(left, right, preferred_element_type=F32)


def dot_tn(left, right):
    return lax.dot_general(left, right, (((0,), (0,)), ((), ())), preferred_element_type=F32)


def dot_nt(left, right):
    return lax.dot_general(left, right, (((1,), (1,)), ((), ())), preferred_element_type=F32)


def iota(shape, dim):
    return lax.broadcasted_iota(jnp.int32, shape, dim)


def rms_apply(x, gain):
    inv = lax.rsqrt(jnp.mean(x * x, axis=-1, keepdims=True) + EPS_NORM)
    return (x * inv * gain).astype(BF)


def rms_pull(grad, x, gain):
    inv = lax.rsqrt(jnp.mean(x * x, axis=-1, keepdims=True) + EPS_NORM)
    unit = x * inv
    weighted = grad * gain
    grad_x = inv * (weighted - unit * jnp.mean(weighted * unit, axis=-1, keepdims=True))
    rows, dims = x.shape
    return grad_x, jnp.sum((grad * unit).reshape(rows // 8, 8, dims), axis=0)


def step_kernel(
    layers,
    seq_size,
    codes_ref,
    actions_ref,
    next_ref,
    lengths_ref,
    rewards_ref,
    continues_ref,
    values_ref,
    freq_ref,
    table_ref,
    attn_in_ref,
    attn_out_ref,
    ffn_in_ref,
    ffn_out_ref,
    gains_ref,
    readout_ref,
    grads_ref,
    scal_ref,
    wq,
    wo,
    wu,
    wd,
    rt,
    tb,
    xs,
    hs,
    qs,
    kvs,
    probs,
    acts,
    gds,
    mixes,
    bias,
    tokf,
    toki,
    gouts,
    gx,
    gl,
    dmix,
    dqkv,
    dkv,
    dgain,
    lossacc,
    lam,
    ang,
    bsend,
    brecv,
    send_sem,
    recv_sem,
    load_sem,
):
    batch, span = codes_ref.shape
    dims = gains_ref.shape[1]
    ff = ffn_in_ref.shape[2]
    tiles = span // SEG
    total = batch * span
    chunks = total // ROWS
    per_seq = span // ROWS
    vocab_all = table_ref.shape[0]
    outs_all = readout_ref.shape[1]
    head_dim = dims // HEADS
    scale = head_dim ** (-0.5)
    exp_scale = scale * math.log2(math.e)
    groups = HEADS // 2
    base = lax.axis_index("seq") * span
    me = lax.axis_index("seq")
    right = lax.rem(me + 1, seq_size)
    left = lax.rem(me + seq_size - 1, seq_size)

    barrier = pltpu.get_barrier_semaphore()
    for neighbour in (left, right):
        pl.semaphore_signal(barrier, inc=1, device_id={"seq": neighbour}, device_id_type=MESH)
    pl.semaphore_wait(barrier, 2)

    blocks = []
    for layer in range(layers):
        for j in range(3):
            blocks.append((attn_in_ref, wq, layer, slice(0, 256), slice(j * 256, j * 256 + 256)))
        blocks.append((attn_out_ref, wo, layer, slice(0, 256), slice(0, 256)))
        for j in range(ff // 256):
            blocks.append((ffn_in_ref, wu, layer, slice(0, 256), slice(j * 256, j * 256 + 256)))
        for j in range(ff // 256):
            blocks.append((ffn_out_ref, wd, layer, slice(j * 256, j * 256 + 256), slice(0, 256)))

    def block_copy(k):
        source, _, layer, rows, cols = blocks[k]
        at = 256 * (k % chunks)
        return pltpu.make_async_copy(
            source.at[layer, rows, cols], xs.at[1 + k // chunks, at : at + 256, :], load_sem.at[k]
        )

    for k in range(len(blocks)):
        block_copy(k).start()
    tb[...] = jnp.zeros_like(tb)
    tb[0:vocab_all, :] = table_ref[...].astype(BF)
    for part in range(VOCAB // 256):
        rt[part * 256 : part * 256 + 256, :] = readout_ref[:, part * 256 : part * 256 + 256].T.astype(BF)
    rest = outs_all - VOCAB
    tail = jnp.concatenate(
        [readout_ref[:, VOCAB:outs_all], jnp.zeros((dims, 128 - rest), F32)], axis=1
    ).T
    rt[VOCAB:OUTS, :] = tail[0 : OUTS - VOCAB].astype(BF)

    ends = []
    for b in range(batch):
        run = jnp.int32(0)
        row = []
        for e in range(lengths_ref.shape[1]):
            run = run + lengths_ref[b, e]
            row.append(run)
        ends.append(row)
    episodes = len(ends[0])

    lane = iota((8, span), 1)
    lam[...] = jnp.zeros_like(lam)
    lam[0, 0:batch, :] = rewards_ref[...]
    lam[1, 0:batch, :] = continues_ref[...]
    lam[2, 0:batch, :] = values_ref[...]
    last = lax.rem(lane, SEG) == SEG - 1
    decay = GAMMA * lam[1]
    value_next = pltpu.roll(lam[2], span - 1, 1)
    add = jnp.where(last, lam[2], lam[0] + decay * ((1.0 - LAMBDA_RET) * value_next))
    mul = jnp.where(last, 0.0, decay * LAMBDA_RET)
    step = 1
    while step < SEG:
        add = add + mul * pltpu.roll(add, span - step, 1)
        mul = mul * pltpu.roll(mul, span - step, 1)
        step *= 2
    lam[3] = add
    valid_rows = []
    for b in range(batch):
        after = iota((1, span), 1) + (base + 1)
        final = after == ends[b][0]
        for e in range(1, episodes):
            final = final | (after == ends[b][e])
        valid_rows.append(jnp.where(final, 0.0, 1.0))
    for c in range(chunks):
        b = c // per_seq
        lanes = slice((c % per_seq) * ROWS, (c % per_seq) * ROWS + ROWS)
        for row in range(4):
            tokf[c, row : row + 1, :] = lam[row, b : b + 1, lanes]
        tokf[c, 4:5, :] = valid_rows[b][:, lanes]
        toki[c, 0:1, :] = codes_ref[b : b + 1, lanes]
        toki[c, 1:2, :] = actions_ref[b : b + 1, lanes]
        toki[c, 2:3, :] = next_ref[b : b + 1, lanes]

    half = dims // 2
    freq = freq_ref[...]
    in_angle = iota((SEG, half), 0).astype(F32) * freq
    in_sin, in_cos = jnp.sin(in_angle), jnp.cos(in_angle)
    tile_angle = (iota((tiles, half), 0) * SEG + base).astype(F32) * freq
    all_sin, all_cos = jnp.sin(tile_angle), jnp.cos(tile_angle)
    for tile in range(tiles):
        ang[tile, 0:1, :] = all_sin[tile : tile + 1, :]
        ang[tile, 1:2, :] = all_cos[tile : tile + 1, :]
    end_row = iota((batch * episodes, half), 0)
    end_all = jnp.zeros((batch * episodes, half), jnp.int32)
    for b in range(batch):
        for e in range(episodes):
            end_all = jnp.where(end_row == b * episodes + e, ends[b][e], end_all)
    end_angle = end_all.astype(F32) * freq
    end_sin, end_cos = jnp.sin(end_angle), jnp.cos(end_angle)

    def marks(tile, carry):
        tile_sin = ang[tile, 0:1, :]
        tile_cos = ang[tile, 1:2, :]
        here_sin = in_sin * tile_cos + in_cos * tile_sin
        here_cos = in_cos * tile_cos - in_sin * tile_sin
        place = iota((SEG, half), 0) + (base + tile * SEG)
        key_place = iota((SEG, WIN), 1) + (base + tile * SEG - SEG)
        for b in range(batch):
            start = jnp.zeros((SEG, half), jnp.int32)
            start_sin = jnp.zeros((SEG, half), F32)
            start_cos = jnp.ones((SEG, half), F32)
            for e in range(episodes):
                passed = place >= ends[b][e]
                row = b * episodes + e
                start = jnp.where(passed, ends[b][e], start)
                start_sin = jnp.where(passed, end_sin[row : row + 1, :], start_sin)
                start_cos = jnp.where(passed, end_cos[row : row + 1, :], start_cos)
            rows = pl.ds(pl.multiple_of(b * span + tile * SEG, SEG), SEG)
            xs[0, rows, 0:half] = here_sin * start_cos - here_cos * start_sin
            xs[0, rows, half:dims] = here_cos * start_cos + here_sin * start_sin
            seen = (key_place <= place) & (key_place >= start)
            bias[rows, :] = jnp.where(seen, 0.0, NEG)
        return carry

    lax.fori_loop(0, tiles, marks, 0)

    for layer in range(layers):
        for b in range(batch):
            kvs[layer, b, SEG + span :, :] = jnp.zeros((kvs.shape[2] - SEG - span, 2 * dims), BF)

    def chunk_rows(c):
        return pl.ds(pl.multiple_of(c * ROWS, ROWS), ROWS)

    def kv_rows(c):
        return pl.ds(pl.multiple_of(lax.rem(c, per_seq) * ROWS + SEG, 16), ROWS)

    for k, (_, dest, layer, rows, cols) in enumerate(blocks):
        block_copy(k).wait()
        at = 256 * (k % chunks)
        dest[layer, rows, cols] = xs[1 + k // chunks, at : at + 256, :].astype(BF)

    def onehot(c):
        code = toki[c, 0:1, :]
        act = toki[c, 1:2, :] + VOCAB
        ids = iota((OUTS, ROWS), 0)
        return jnp.where((ids == code) | (ids == act), 1.0, 0.0).astype(BF)

    def embed(c, carry):
        rows = chunk_rows(c)
        xs[0, rows, :] += dot_tn(onehot(c), tb[...])
        return carry

    lax.fori_loop(0, chunks, embed, 0)

    lane_head = iota((1, dims), 1) // head_dim
    group_mask = [jnp.where(lane_head // 2 == g, 1.0, 0.0).astype(BF) for g in range(groups)]
    even_mask = jnp.where(lax.rem(lane_head, 2) == 0, 1.0, 0.0).astype(BF)
    odd_mask = jnp.where(lax.rem(lane_head, 2) == 1, 1.0, 0.0).astype(BF)
    even_f = lax.rem(lane_head, 2) == 0

    def spread(rows):
        return jnp.concatenate([rows * group_mask[g] for g in range(groups)], axis=0)

    def both(keys):
        return jnp.concatenate([keys * even_mask, keys * odd_mask], axis=0)

    def gather_heads(wide):
        out = wide[0:SEG]
        for g in range(1, groups):
            out = jnp.where(lane_head // 2 == g, wide[g * SEG : g * SEG + SEG], out)
        return out

    def forward_copy(layer):
        return pltpu.make_async_remote_copy(
            src_ref=kvs.at[layer, :, pl.ds(span, SEG), :],
            dst_ref=kvs.at[layer, :, pl.ds(0, SEG), :],
            send_sem=send_sem.at[layer],
            recv_sem=recv_sem.at[layer],
            device_id={"seq": right},
            device_id_type=MESH,
        )

    def backward_copy(layer):
        return pltpu.make_async_remote_copy(
            src_ref=bsend.at[layer],
            dst_ref=brecv.at[layer],
            send_sem=send_sem.at[layers + layer],
            recv_sem=recv_sem.at[layers + layer],
            device_id={"seq": left},
            device_id_type=MESH,
        )

    def project(layer):
        def body(c, carry):
            rows = chunk_rows(c)
            h = rms_apply(xs[2 * layer, rows, :], gains_ref[2 * layer : 2 * layer + 1, :])
            hs[2 * layer, rows, :] = h
            qkv = dot_nn(h, wq[layer]).astype(BF)
            qs[layer, rows, :] = qkv[:, 0:dims]
            kvs[layer, c // per_seq, kv_rows(c), :] = qkv[:, dims:]
            return carry

        lax.fori_loop(0, chunks, body, 0)

    def attend(layer):
        def one(b, tile):
            rows = pl.ds(pl.multiple_of(b * span + tile * SEG, SEG), SEG)
            window = pl.ds(pl.multiple_of(tile * SEG, SEG), WIN)
            keys = kvs[layer, b, window, 0:dims]
            values = kvs[layer, b, window, dims:]
            mask = bias[rows, :]
            mask = jnp.concatenate([mask] * groups, axis=0)
            scores = dot_nt(spread(qs[layer, rows, :]), both(keys))
            sides = []
            for side in range(2):
                s = scores[:, side * WIN : side * WIN + WIN] + mask
                top = jnp.max(s, axis=-1, keepdims=True)
                e = jnp.exp2((s - top) * exp_scale)
                sides.append((e / jnp.sum(e, axis=-1, keepdims=True)).astype(BF))
            p = jnp.concatenate(sides, axis=1)
            probs[layer, b * tiles + tile] = p
            wide = dot_nn(p, both(values))
            mixes[layer, rows, :] = gather_heads(wide).astype(BF)

        def body(i, carry):
            tile = tiles - 1 - i
            for b in range(batch):
                one(b, tile)
            return carry

        copy = forward_copy(layer)
        copy.start()
        lax.fori_loop(0, tiles - 1, body, 0)
        copy.wait()
        lax.fori_loop(tiles - 1, tiles, body, 0)

    def feed(layer):
        def body(c, carry):
            rows = chunk_rows(c)
            x = xs[2 * layer, rows, :] + dot_nn(mixes[layer, rows, :], wo[layer])
            xs[2 * layer + 1, rows, :] = x
            h = rms_apply(x, gains_ref[2 * layer + 1 : 2 * layer + 2, :])
            hs[2 * layer + 1, rows, :] = h
            for j in range(ff // 256):
                cols = slice(j * 256, j * 256 + 256)
                up = dot_nn(h, wu[layer, :, cols])
                square = up * up
                c0 = math.sqrt(2.0 / math.pi)
                t = jnp.tanh(c0 * up * (1.0 + 0.044715 * square))
                half_t = 0.5 * (1.0 + t)
                acts[layer, rows, cols] = (up * half_t).astype(BF)
                slope = half_t + (0.5 * c0) * up * (1.0 - t * t) * (1.0 + (3.0 * 0.044715) * square)
                gds[layer, rows, cols] = slope.astype(BF)
            xs[2 * layer + 2, rows, :] = x + dot_nn(acts[layer, rows, :], wd[layer])
            return carry

        lax.fori_loop(0, chunks, body, 0)

    for layer in range(layers):
        project(layer)
        attend(layer)
        feed(layer)

    lossacc[...] = jnp.zeros_like(lossacc)
    dgain[...] = jnp.zeros_like(dgain)
    top_gain = gains_ref[2 * layers : 2 * layers + 1, :]

    def losses(c, carry):
        rows = chunk_rows(c)
        x = xs[2 * layers, rows, :]
        h = rms_apply(x, top_gain)
        hs[2 * layers, rows, :] = h
        outs = dot_nt(rt[...], h)
        reward, cont = tokf[c, 0:1, :], tokf[c, 1:2, :]
        target, ret, valid = tokf[c, 2:3, :], tokf[c, 3:4, :], tokf[c, 4:5, :]
        action, code = toki[c, 1:2, :], toki[c, 2:3, :]
        logits = outs[0:VOCAB]
        top = jnp.max(logits, axis=0, keepdims=True)
        e = jnp.exp(logits - top)
        esum = jnp.sum(e, axis=0, keepdims=True)
        chosen = iota((VOCAB, ROWS), 0) == code
        picked = jnp.sum(jnp.where(chosen, logits, 0.0), axis=0, keepdims=True)
        loss = jnp.log(esum) + top - picked
        gouts[0:VOCAB, rows] = (e * (valid / esum) - jnp.where(chosen, valid, 0.0)).astype(BF)
        small = outs[VOCAB:OUTS]
        place = iota((OUTS - VOCAB, ROWS), 0)
        reward_err = small[0:1] - reward
        end_logit = small[1:2]
        value_err = small[2:3] - ret
        minus = jnp.exp(-jnp.abs(end_logit))
        soft = jnp.maximum(end_logit, 0.0) + jnp.log(1.0 + minus)
        sigmoid = jnp.where(end_logit >= 0.0, 1.0, minus) / (1.0 + minus)
        loss = loss + 0.5 * reward_err * reward_err + soft - cont * end_logit
        loss = loss + 0.5 * value_err * value_err
        actor = (place >= 3) & (place < outs_all - VOCAB)
        act_top = jnp.max(jnp.where(actor, small, NEG), axis=0, keepdims=True)
        act_e = jnp.where(actor, jnp.exp(jnp.where(actor, small - act_top, 0.0)), 0.0)
        act_sum = jnp.sum(act_e, axis=0, keepdims=True)
        log_pi = jnp.where(actor, small - act_top - jnp.log(act_sum), 0.0)
        pi = act_e / act_sum
        neg_entropy = jnp.sum(pi * log_pi, axis=0, keepdims=True)
        taken = place == action + 3
        picked_pi = jnp.sum(jnp.where(taken, log_pi, 0.0), axis=0, keepdims=True)
        gap = ret - target
        loss = loss - gap * picked_pi + ENTROPY_COEF * neg_entropy
        grad = gap * (pi - jnp.where(taken, 1.0, 0.0))
        grad = grad + ENTROPY_COEF * pi * (log_pi - neg_entropy)
        grad = jnp.where(actor, grad, 0.0)
        grad = jnp.where(place == 0, reward_err, grad)
        grad = jnp.where(place == 1, sigmoid - cont, grad)
        grad = jnp.where(place == 2, value_err, grad)
        gouts[VOCAB:OUTS, rows] = (grad * valid).astype(BF)
        lossacc[0:1, :] += loss * valid
        lossacc[1:2, :] += valid
        dh = dot_tn(gouts[:, rows], rt[...])
        grad_x, part = rms_pull(dh, x, top_gain)
        gx[rows, :] = grad_x
        dgain[2 * layers] += part
        return carry

    lax.fori_loop(0, chunks, losses, 0)
    grads_ref[0:OUTS, :] = dot_nn(gouts[...], hs[2 * layers]).astype(BF)
    loss_total = jnp.sum(lossacc[0:1, :])
    count_total = jnp.sum(lossacc[1:2, :])
    place = iota(scal_ref.shape, 0)
    scal_ref[...] = jnp.where(place == 0, loss_total, jnp.where(place == 1, count_total, 0.0))

    def feed_back(layer):
        def body(c, carry):
            rows = chunk_rows(c)
            grad = gx[rows, :]
            low = grad.astype(BF)
            gl[rows, :] = low
            for j in range(ff // 256):
                cols = slice(j * 256, j * 256 + 256)
                da = dot_nt(low, wd[layer, cols, :])
                gds[layer, rows, cols] = (da * gds[layer, rows, cols].astype(F32)).astype(BF)
            dh = dot_nt(gds[layer, rows, :], wu[layer])
            gain = gains_ref[2 * layer + 1 : 2 * layer + 2, :]
            grad_x, part = rms_pull(dh, xs[2 * layer + 1, rows, :], gain)
            dgain[2 * layer + 1] += part
            grad = grad + grad_x
            gx[rows, :] = grad
            dmix[rows, :] = dot_nt(grad.astype(BF), wo[layer]).astype(BF)
            return carry

        lax.fori_loop(0, chunks, body, 0)

    def attend_back(layer):
        def one(b, tile):
            rows = pl.ds(pl.multiple_of(b * span + tile * SEG, SEG), SEG)
            window = pl.ds(pl.multiple_of(tile * SEG, SEG), WIN)
            keys = both(kvs[layer, b, window, 0:dims])
            values = both(kvs[layer, b, window, dims:])
            queries = spread(qs[layer, rows, :])
            dout = spread(dmix[rows, :])
            p = probs[layer, b * tiles + tile]
            dp = dot_nt(dout, values)
            sides = []
            for side in range(2):
                cols = slice(side * WIN, side * WIN + WIN)
                pf = p[:, cols].astype(F32)
                d = dp[:, cols]
                sides.append((pf * (d - jnp.sum(d * pf, axis=-1, keepdims=True))).astype(BF))
            ds = jnp.concatenate(sides, axis=1)
            dq = gather_heads(dot_nn(ds, keys)) * scale
            dqkv[rows, 0:dims] = dq.astype(BF)
            dk = dot_tn(ds, queries) * scale
            dk = jnp.where(even_f, dk[0 : 2 * SEG], dk[WIN : WIN + 2 * SEG])
            dv = dot_tn(p, dout)
            dv = jnp.where(even_f, dv[0 : 2 * SEG], dv[WIN : WIN + 2 * SEG])
            old = pl.ds(pl.multiple_of(tile * SEG, SEG), SEG)
            new = pl.ds(pl.multiple_of(tile * SEG + SEG, SEG), SEG)
            dkv[b, old, 0:dims] += dk[0:SEG]
            dkv[b, old, dims:] += dv[0:SEG]
            dkv[b, new, 0:dims] = dk[SEG:]
            dkv[b, new, dims:] = dv[SEG:]

        def body(tile, carry):
            for b in range(batch):
                one(b, tile)
            return carry

        for b in range(batch):
            dkv[b, 0:SEG, :] = jnp.zeros((SEG, 2 * dims), F32)
        lax.fori_loop(0, 1, body, 0)
        for b in range(batch):
            bsend[layer, b] = dkv[b, 0:SEG, :].astype(BF)
        copy = backward_copy(layer)
        copy.start()
        lax.fori_loop(1, tiles, body, 0)
        copy.wait()
        for b in range(batch):
            dkv[b, span : span + SEG, :] += brecv[layer, b].astype(F32)

    def project_back(layer):
        def body(c, carry):
            rows = chunk_rows(c)
            dqkv[rows, dims:] = dkv[c // per_seq, kv_rows(c), :].astype(BF)
            dh = dot_nt(dqkv[rows, :], wq[layer])
            gain = gains_ref[2 * layer : 2 * layer + 1, :]
            grad_x, part = rms_pull(dh, xs[2 * layer, rows, :], gain)
            dgain[2 * layer] += part
            gx[rows, :] += grad_x
            return carry

        lax.fori_loop(0, chunks, body, 0)

    at = OUTS
    for layer in reversed(range(layers)):
        feed_back(layer)
        for j in range(ff // 256):
            cols = slice(j * 256, j * 256 + 256)
            grads_ref[at : at + 256, :] = dot_tn(acts[layer, :, cols], gl[...]).astype(BF)
            at += 256
        for j in range(ff // 256):
            cols = slice(j * 256, j * 256 + 256)
            grads_ref[at : at + 256, :] = dot_tn(hs[2 * layer + 1], gds[layer, :, cols]).astype(BF)
            at += 256
        gl[...] = gx[...].astype(BF)
        grads_ref[at : at + 256, :] = dot_tn(mixes[layer], gl[...]).astype(BF)
        at += 256
        attend_back(layer)
        project_back(layer)
        for j in range(3):
            cols = slice(j * 256, j * 256 + 256)
            grads_ref[at : at + 256, :] = dot_tn(hs[2 * layer], dqkv[:, cols]).astype(BF)
            at += 256
    gl[...] = gx[...].astype(BF)

    def mark(c, carry):
        gouts[:, chunk_rows(c)] = onehot(c)
        return carry

    lax.fori_loop(0, chunks, mark, 0)
    grads_ref[at : at + OUTS, :] = dot_nn(gouts[...], gl[...]).astype(BF)
    at += OUTS
    place = iota((16, dims), 0)
    gain_rows = jnp.zeros((16, dims), F32)
    for index in range(2 * layers + 1):
        gain_rows = jnp.where(place == index, jnp.sum(dgain[index], axis=0, keepdims=True), gain_rows)
    grads_ref[at : at + 16, :] = gain_rows.astype(BF)


def gradients(codes, actions, next_codes, lengths, rewards, continues, values, weights, seq_size):
    table, attn_in, attn_out, ffn_in, ffn_out, gains, readout = weights
    batch, span = codes.shape
    layers, dims, ff = ffn_in.shape
    total = batch * span
    tiles = span // SEG
    chunks = total // ROWS
    grad_rows = 2 * OUTS + layers * 12 * 256 + 16
    freq = jnp.exp(
        jnp.arange(dims // 2).astype(F32) * (-2.0 * math.log(10000.0) / dims)
    )[None, :]
    vmem = pl.BlockSpec(memory_space=pltpu.VMEM)
    smem = pl.BlockSpec(memory_space=pltpu.SMEM)
    kv_span = -(-(span - SEG + WIN) // 16) * 16
    return pl.pallas_call(
        functools.partial(step_kernel, layers, seq_size),
        out_shape=(
            jax.ShapeDtypeStruct((grad_rows, dims), BF),
            jax.ShapeDtypeStruct((8, 128), F32),
        ),
        in_specs=[vmem] * 3 + [smem] + [vmem] * 5 + [pl.BlockSpec(memory_space=pl.ANY)] * 4 + [vmem] * 2,
        out_specs=(vmem, vmem),
        scratch_shapes=[
            pltpu.VMEM((layers, dims, 3 * dims), BF),
            pltpu.VMEM((layers, dims, dims), BF),
            pltpu.VMEM((layers, dims, ff), BF),
            pltpu.VMEM((layers, ff, dims), BF),
            pltpu.VMEM((OUTS, dims), BF),
            pltpu.VMEM((OUTS, dims), BF),
            pltpu.VMEM((2 * layers + 1, total, dims), F32),
            pltpu.VMEM((2 * layers + 1, total, dims), BF),
            pltpu.VMEM((layers, total, dims), BF),
            pltpu.VMEM((layers, batch, kv_span, 2 * dims), BF),
            pltpu.VMEM((layers, batch * tiles, HEADS // 2 * SEG, 2 * WIN), BF),
            pltpu.VMEM((layers, total, ff), BF),
            pltpu.VMEM((layers, total, ff), BF),
            pltpu.VMEM((layers, total, dims), BF),
            pltpu.VMEM((total, WIN), F32),
            pltpu.VMEM((chunks, 8, ROWS), F32),
            pltpu.VMEM((chunks, 8, ROWS), jnp.int32),
            pltpu.VMEM((OUTS, total), BF),
            pltpu.VMEM((total, dims), F32),
            pltpu.VMEM((total, dims), BF),
            pltpu.VMEM((total, dims), BF),
            pltpu.VMEM((total, 3 * dims), BF),
            pltpu.VMEM((batch, SEG + span, 2 * dims), F32),
            pltpu.VMEM((2 * layers + 1, 8, dims), F32),
            pltpu.VMEM((8, ROWS), F32),
            pltpu.VMEM((4, 8, span), F32),
            pltpu.VMEM((tiles, 8, dims // 2), F32),
            pltpu.VMEM((layers, batch, SEG, 2 * dims), BF),
            pltpu.VMEM((layers, batch, SEG, 2 * dims), BF),
            pltpu.SemaphoreType.DMA((2 * layers,)),
            pltpu.SemaphoreType.DMA((2 * layers,)),
            pltpu.SemaphoreType.DMA((12 * layers,)),
        ],
        compiler_params=pltpu.CompilerParams(
            collective_id=0, has_side_effects=True, vmem_limit_bytes=63 * 1024 * 1024
        ),
        name="train_step",
    )(
        codes,
        actions,
        next_codes,
        lengths,
        rewards,
        continues,
        values,
        freq,
        table,
        attn_in,
        attn_out,
        ffn_in,
        ffn_out,
        gains,
        readout,
    )


def adam_update(weight, first_mom, second_mom, clipped, rate):
    new_first = BETA_ONE * first_mom + (1.0 - BETA_ONE) * clipped
    new_second = BETA_TWO * second_mom + (1.0 - BETA_TWO) * clipped * clipped
    ratio = (
        new_first
        / (1.0 - BETA_ONE**STEP)
        / (jnp.sqrt(new_second / (1.0 - BETA_TWO**STEP)) + ADAM_EPS)
    )
    return (weight - rate * (ratio + DECAY * weight), new_first, new_second)


def unpack(grads, weights):
    table, attn_in, attn_out, ffn_in, ffn_out, gains, readout = weights
    layers, dims, ff = ffn_in.shape
    read = grads[0:OUTS].T[:, : readout.shape[1]]
    at = OUTS
    per_layer = [None] * layers
    for layer in reversed(range(layers)):
        down = grads[at : at + ff]
        at += ff
        up = grads[at : at + ff].reshape(ff // 256, dims, 256).transpose(1, 0, 2).reshape(dims, ff)
        at += ff
        out = grads[at : at + dims]
        at += dims
        qkv = grads[at : at + 3 * dims].reshape(3, dims, 256).transpose(1, 0, 2).reshape(dims, 3 * dims)
        at += 3 * dims
        per_layer[layer] = (qkv, out, up, down)
    tab = grads[at : at + table.shape[0]]
    at += OUTS
    gain = grads[at : at + gains.shape[0]]
    stacked = [jnp.stack([entry[k] for entry in per_layer]) for k in range(4)]
    return (tab, *stacked, gain, read)


def local(codes, actions, next_codes, lengths, rewards, continues, target_values, *state):
    params, firsts, seconds = state[0::3], state[1::3], state[2::3]
    grads, scal = gradients(
        codes,
        actions,
        next_codes,
        lengths,
        rewards,
        continues,
        target_values,
        params,
        lax.axis_size("seq"),
    )
    grads = lax.psum(grads, ("seq", "dp")).astype(F32)
    scal = lax.psum(scal, ("seq", "dp"))
    loss_sum, step_count = scal[0, 0], scal[1, 0]
    averaged = [grad / step_count for grad in unpack(grads, params)]
    grad_norm = jnp.sqrt(sum((jnp.sum(grad * grad) for grad in averaged)))
    factor = jnp.minimum(1.0, CLIP_NORM / grad_norm)
    results = []
    for slot in range(7):
        results.extend(
            adam_update(
                params[slot], firsts[slot], seconds[slot], averaged[slot] * factor, RATES[slot]
            )
        )
    return tuple(results) + (loss_sum, step_count, grad_norm)


def solution(mesh):
    rows, whole = P("dp", "seq"), P()
    return jax.shard_map(
        local,
        mesh=mesh,
        in_specs=(rows, rows, rows, P("dp", None), rows, rows, rows) + (whole,) * 21,
        out_specs=(whole,) * 24,
        check_vma=False,
    )
```

```python
import functools
import math

import jax
import jax.numpy as jnp
import numpy as np
from jax import lax
from jax.experimental import pallas as pl
from jax.experimental.pallas import tpu as pltpu
from jax.sharding import PartitionSpec as P

HEADS = 8
VOCAB = 512
SEG = 48
STEP = 5

EPS_NORM = 1e-06
BETA_ONE = 0.9
BETA_TWO = 0.999
RATES = (0.25, 0.02, 0.08, 0.02, 0.02, 0.25, 0.02)
DECAY = 0.01
ADAM_EPS = 1e-08
CLIP_NORM = 0.05
GAMMA = 0.985
LAMBDA_RET = 0.95
ENTROPY_COEF = 0.05

BF = jnp.bfloat16
F32 = jnp.float32
ROWS = 256
QRY = 2 * SEG
KEY = 3 * SEG
OUTS = 544
NEG = -1e30
MESH = pl.DeviceIdType.MESH


def dot_nn(left, right):
    return jnp.dot(left, right, preferred_element_type=F32)


def dot_tn(left, right):
    return lax.dot_general(left, right, (((0,), (0,)), ((), ())), preferred_element_type=F32)


def dot_nt(left, right):
    return lax.dot_general(left, right, (((1,), (1,)), ((), ())), preferred_element_type=F32)


def iota(shape, dim):
    return lax.broadcasted_iota(jnp.int32, shape, dim)


def rms_apply(x, gain):
    inv = lax.rsqrt(jnp.mean(x * x, axis=-1, keepdims=True) + EPS_NORM)
    return (x * inv * gain).astype(BF)


def rms_pull(grad, x, gain):
    inv = lax.rsqrt(jnp.mean(x * x, axis=-1, keepdims=True) + EPS_NORM)
    unit = x * inv
    weighted = grad * gain
    grad_x = inv * (weighted - unit * jnp.mean(weighted * unit, axis=-1, keepdims=True))
    rows, dims = x.shape
    return grad_x, jnp.sum((grad * unit).reshape(rows // 8, 8, dims), axis=0)


def step_kernel(
    layers,
    seq_size,
    codes_ref,
    actions_ref,
    next_ref,
    lengths_ref,
    rewards_ref,
    continues_ref,
    values_ref,
    trig_ref,
    table_ref,
    attn_in_ref,
    attn_out_ref,
    ffn_in_ref,
    ffn_out_ref,
    gains_ref,
    readout_ref,
    grads_ref,
    scal_ref,
    wq,
    wo,
    wu,
    wd,
    rt,
    tb,
    xs,
    hs,
    qs,
    kvs,
    probs,
    acts,
    gds,
    mixes,
    lows,
    tokf,
    toki,
    gouts,
    gx,
    gl,
    dmix,
    dqkv,
    dkv,
    dgain,
    lossacc,
    lam,
    bsend,
    brecv,
    send_sem,
    recv_sem,
    load_sem,
):
    batch, span = codes_ref.shape
    dims = gains_ref.shape[1]
    ff = ffn_in_ref.shape[2]
    tiles = span // SEG
    pairs = span // QRY
    total = batch * span
    chunks = total // ROWS
    per_seq = span // ROWS
    vocab_all = table_ref.shape[0]
    outs_all = readout_ref.shape[0]
    head_dim = dims // HEADS
    scale = head_dim ** (-0.5)
    exp_scale = scale * math.log2(math.e)
    groups = HEADS // 2
    base = lax.axis_index("seq") * span
    me = lax.axis_index("seq")
    right = lax.rem(me + 1, seq_size)
    left = lax.rem(me + seq_size - 1, seq_size)

    barrier = pltpu.get_barrier_semaphore()
    for neighbour in (left, right):
        pl.semaphore_signal(barrier, inc=1, device_id={"seq": neighbour}, device_id_type=MESH)
    pl.semaphore_wait(barrier, 2)

    blocks = []
    for layer in range(layers):
        for j in range(3):
            blocks.append((attn_in_ref, wq, layer, slice(0, 256), slice(j * 256, j * 256 + 256)))
        blocks.append((attn_out_ref, wo, layer, slice(0, 256), slice(0, 256)))
        for j in range(ff // 256):
            blocks.append((ffn_in_ref, wu, layer, slice(0, 256), slice(j * 256, j * 256 + 256)))
        for j in range(ff // 256):
            blocks.append((ffn_out_ref, wd, layer, slice(j * 256, j * 256 + 256), slice(0, 256)))

    def block_copy(k):
        source, _, layer, rows, cols = blocks[k]
        at = 256 * (k % chunks)
        return pltpu.make_async_copy(
            source.at[layer, rows, cols], xs.at[1 + k // chunks, at : at + 256, :], load_sem.at[k]
        )

    for k in range(len(blocks)):
        block_copy(k).start()
    tb[...] = jnp.zeros_like(tb)
    tb[0:vocab_all, :] = table_ref[...].astype(BF)
    rt[...] = jnp.zeros_like(rt)
    rt[0:outs_all, :] = readout_ref[...].astype(BF)

    ends = []
    for b in range(batch):
        run = jnp.int32(0)
        row = []
        for e in range(lengths_ref.shape[1]):
            run = run + lengths_ref[b, e]
            row.append(run)
        ends.append(row)
    episodes = len(ends[0])

    lane = iota((8, span), 1)
    lam[...] = jnp.zeros_like(lam)
    lam[0, 0:batch, :] = rewards_ref[...]
    lam[1, 0:batch, :] = continues_ref[...]
    lam[2, 0:batch, :] = values_ref[...]
    last = lax.rem(lane, SEG) == SEG - 1
    decay = GAMMA * lam[1]
    value_next = pltpu.roll(lam[2], span - 1, 1)
    add = jnp.where(last, lam[2], lam[0] + decay * ((1.0 - LAMBDA_RET) * value_next))
    mul = jnp.where(last, 0.0, decay * LAMBDA_RET)
    step = 1
    while step < SEG:
        add = add + mul * pltpu.roll(add, span - step, 1)
        mul = mul * pltpu.roll(mul, span - step, 1)
        step *= 2
    lam[3] = add
    valid_rows = []
    for b in range(batch):
        after = iota((1, span), 1) + (base + 1)
        final = after == ends[b][0]
        for e in range(1, episodes):
            final = final | (after == ends[b][e])
        valid_rows.append(jnp.where(final, 0.0, 1.0))
    for c in range(chunks):
        b = c // per_seq
        lanes = slice((c % per_seq) * ROWS, (c % per_seq) * ROWS + ROWS)
        for row in range(4):
            tokf[c, row : row + 1, :] = lam[row, b : b + 1, lanes]
        tokf[c, 4:5, :] = valid_rows[b][:, lanes]
        toki[c, 0:1, :] = codes_ref[b : b + 1, lanes]
        toki[c, 1:2, :] = actions_ref[b : b + 1, lanes]
        toki[c, 2:3, :] = next_ref[b : b + 1, lanes]

    half = dims // 2
    in_sin, in_cos = trig_ref[0:SEG, 2, :], trig_ref[0:SEG, 3, :]
    end_sin, end_cos = [], []
    for b in range(batch):
        for e in range(episodes):
            far, near = lax.div(ends[b][e], SEG), lax.rem(ends[b][e], SEG)
            far_sin, far_cos = trig_ref[far, 0:1, :], trig_ref[far, 1:2, :]
            near_sin, near_cos = trig_ref[near, 2:3, :], trig_ref[near, 3:4, :]
            end_sin.append(far_sin * near_cos + far_cos * near_sin)
            end_cos.append(far_cos * near_cos - far_sin * near_sin)

    def marks(tile, carry):
        at = me * tiles + tile
        tile_sin, tile_cos = trig_ref[at, 0:1, :], trig_ref[at, 1:2, :]
        here_sin = in_sin * tile_cos + in_cos * tile_sin
        here_cos = in_cos * tile_cos - in_sin * tile_sin
        place = iota((SEG, half), 0) + (base + tile * SEG)
        for b in range(batch):
            start_sin = jnp.zeros((SEG, half), F32)
            start_cos = jnp.ones((SEG, half), F32)
            for e in range(episodes):
                passed = place >= ends[b][e]
                row = b * episodes + e
                start_sin = jnp.where(passed, end_sin[row], start_sin)
                start_cos = jnp.where(passed, end_cos[row], start_cos)
            rows = pl.ds(pl.multiple_of(b * span + tile * SEG, SEG), SEG)
            xs[0, rows, 0:half] = here_sin * start_cos - here_cos * start_sin
            xs[0, rows, half:dims] = here_cos * start_cos + here_sin * start_sin
        return carry

    lax.fori_loop(0, tiles, marks, 0)

    def lowest(pair, carry):
        within = lax.rem(iota((8, groups * QRY), 1), QRY)
        first = base + pair * QRY - SEG
        place = within + (base + pair * QRY)
        for b in range(batch):
            low = jnp.where(within >= SEG, SEG, 0)
            for e in range(episodes):
                low = jnp.where(place >= ends[b][e], jnp.maximum(low, ends[b][e] - first), low)
            lows[b * pairs + pair] = jnp.maximum(low, -first)
        return carry

    lax.fori_loop(0, pairs, lowest, 0)

    def chunk_rows(c):
        return pl.ds(pl.multiple_of(c * ROWS, ROWS), ROWS)

    def kv_rows(c):
        return pl.ds(pl.multiple_of(lax.rem(c, per_seq) * ROWS + SEG, 16), ROWS)

    for k, (_, dest, layer, rows, cols) in enumerate(blocks):
        block_copy(k).wait()
        at = 256 * (k % chunks)
        dest[layer, rows, cols] = xs[1 + k // chunks, at : at + 256, :].astype(BF)

    def onehot(c):
        code = toki[c, 0:1, :]
        act = toki[c, 1:2, :] + VOCAB
        ids = iota((OUTS, ROWS), 0)
        return jnp.where((ids == code) | (ids == act), 1.0, 0.0).astype(BF)

    def embed(c, carry):
        rows = chunk_rows(c)
        xs[0, rows, :] += dot_tn(onehot(c), tb[...])
        return carry

    lax.fori_loop(0, chunks, embed, 0)

    lane_head = iota((1, dims), 1) // head_dim
    group_mask = [jnp.where(lane_head // 2 == g, 1.0, 0.0).astype(BF) for g in range(groups)]
    even_mask = jnp.where(lax.rem(lane_head, 2) == 0, 1.0, 0.0).astype(BF)
    odd_mask = jnp.where(lax.rem(lane_head, 2) == 1, 1.0, 0.0).astype(BF)
    even_f = lax.rem(lane_head, 2) == 0

    def spread(rows):
        return jnp.concatenate([rows * group_mask[g] for g in range(groups)], axis=0)

    def both(keys):
        return jnp.concatenate([keys * even_mask, keys * odd_mask], axis=0)

    def gather_heads(wide):
        out = wide[0:QRY]
        for g in range(1, groups):
            out = jnp.where(lane_head // 2 == g, wide[g * QRY : g * QRY + QRY], out)
        return out

    def forward_copy(layer):
        return pltpu.make_async_remote_copy(
            src_ref=kvs.at[layer, :, pl.ds(span, SEG), :],
            dst_ref=kvs.at[layer, :, pl.ds(0, SEG), :],
            send_sem=send_sem.at[layer],
            recv_sem=recv_sem.at[layer],
            device_id={"seq": right},
            device_id_type=MESH,
        )

    def backward_copy(layer):
        return pltpu.make_async_remote_copy(
            src_ref=bsend.at[layer],
            dst_ref=brecv.at[layer],
            send_sem=send_sem.at[layers + layer],
            recv_sem=recv_sem.at[layers + layer],
            device_id={"seq": left},
            device_id_type=MESH,
        )

    def project(layer):
        def body(c, carry):
            rows = chunk_rows(c)
            h = rms_apply(xs[2 * layer, rows, :], gains_ref[2 * layer : 2 * layer + 1, :])
            hs[2 * layer, rows, :] = h
            qkv = dot_nn(h, wq[layer]).astype(BF)
            qs[layer, rows, :] = qkv[:, 0:dims]
            kvs[layer, c // per_seq, kv_rows(c), :] = qkv[:, dims:]
            return carry

        lax.fori_loop(0, chunks, body, 0)

    def pair_rows(b, pair):
        return pl.ds(pl.multiple_of(b * span + pair * QRY, 16), QRY)

    def pair_window(pair):
        return pl.ds(pl.multiple_of(pair * QRY, 16), KEY)

    causal = iota((KEY, groups * QRY), 0) <= lax.rem(iota((KEY, groups * QRY), 1), QRY) + SEG
    key_place = iota((KEY, groups * QRY), 0)

    def attend(layer):
        def one(b, pair):
            rows, window = pair_rows(b, pair), pair_window(pair)
            keys = kvs[layer, b, window, 0:dims]
            values = kvs[layer, b, window, dims:]
            seen = causal & (key_place >= lows[b * pairs + pair, 0:1, :])
            scores = dot_nt(both(keys), spread(qs[layer, rows, :]))
            sides = []
            for side in range(2):
                s = jnp.where(seen, scores[side * KEY : side * KEY + KEY], NEG)
                top = jnp.max(s, axis=0, keepdims=True)
                e = jnp.exp2((s - top) * exp_scale)
                sides.append((e * (1.0 / jnp.sum(e, axis=0, keepdims=True))).astype(BF))
            p = jnp.concatenate(sides, axis=0)
            probs[layer, b * pairs + pair] = p
            wide = dot_tn(p, both(values))
            mixes[layer, rows, :] = gather_heads(wide).astype(BF)

        def body(i, carry):
            for b in range(batch):
                one(b, pairs - 1 - i)
            return carry

        copy = forward_copy(layer)
        copy.start()
        lax.fori_loop(0, pairs - 1, body, 0)
        copy.wait()
        lax.fori_loop(pairs - 1, pairs, body, 0)

    def feed(layer):
        def body(c, carry):
            rows = chunk_rows(c)
            x = xs[2 * layer, rows, :] + dot_nn(mixes[layer, rows, :], wo[layer])
            xs[2 * layer + 1, rows, :] = x
            h = rms_apply(x, gains_ref[2 * layer + 1 : 2 * layer + 2, :])
            hs[2 * layer + 1, rows, :] = h
            for j in range(ff // 256):
                cols = slice(j * 256, j * 256 + 256)
                up = dot_nn(h, wu[layer, :, cols])
                square = up * up
                c0 = math.sqrt(2.0 / math.pi)
                t = jnp.tanh(c0 * up * (1.0 + 0.044715 * square))
                half_t = 0.5 * (1.0 + t)
                acts[layer, rows, cols] = (up * half_t).astype(BF)
                slope = half_t + (0.5 * c0) * up * (1.0 - t * t) * (1.0 + (3.0 * 0.044715) * square)
                gds[layer, rows, cols] = slope.astype(BF)
            xs[2 * layer + 2, rows, :] = x + dot_nn(acts[layer, rows, :], wd[layer])
            return carry

        lax.fori_loop(0, chunks, body, 0)

    for layer in range(layers):
        project(layer)
        attend(layer)
        feed(layer)

    lossacc[...] = jnp.zeros_like(lossacc)
    dgain[...] = jnp.zeros_like(dgain)
    top_gain = gains_ref[2 * layers : 2 * layers + 1, :]

    def put(at, block):
        for side in range(2):
            cols = slice(side * 128, side * 128 + 128)
            grads_ref[side, at : at + block.shape[0], :] = block[:, cols].astype(BF)

    def losses(c, carry):
        rows = chunk_rows(c)
        x = xs[2 * layers, rows, :]
        h = rms_apply(x, top_gain)
        hs[2 * layers, rows, :] = h
        outs = dot_nt(rt[...], h)
        reward, cont = tokf[c, 0:1, :], tokf[c, 1:2, :]
        target, ret, valid = tokf[c, 2:3, :], tokf[c, 3:4, :], tokf[c, 4:5, :]
        action, code = toki[c, 1:2, :], toki[c, 2:3, :]
        logits = outs[0:VOCAB]
        top = jnp.max(logits, axis=0, keepdims=True)
        e = jnp.exp(logits - top)
        esum = jnp.sum(e, axis=0, keepdims=True)
        chosen = iota((VOCAB, ROWS), 0) == code
        picked = jnp.sum(jnp.where(chosen, logits, 0.0), axis=0, keepdims=True)
        loss = jnp.log(esum) + top - picked
        gouts[0:VOCAB, rows] = (e * (valid / esum) - jnp.where(chosen, valid, 0.0)).astype(BF)
        small = outs[VOCAB:OUTS]
        place = iota((OUTS - VOCAB, ROWS), 0)
        reward_err = small[0:1] - reward
        end_logit = small[1:2]
        value_err = small[2:3] - ret
        minus = jnp.exp(-jnp.abs(end_logit))
        soft = jnp.maximum(end_logit, 0.0) + jnp.log(1.0 + minus)
        sigmoid = jnp.where(end_logit >= 0.0, 1.0, minus) / (1.0 + minus)
        loss = loss + 0.5 * reward_err * reward_err + soft - cont * end_logit
        loss = loss + 0.5 * value_err * value_err
        actor = (place >= 3) & (place < outs_all - VOCAB)
        act_top = jnp.max(jnp.where(actor, small, NEG), axis=0, keepdims=True)
        act_e = jnp.where(actor, jnp.exp(jnp.where(actor, small - act_top, 0.0)), 0.0)
        act_sum = jnp.sum(act_e, axis=0, keepdims=True)
        log_pi = jnp.where(actor, small - act_top - jnp.log(act_sum), 0.0)
        pi = act_e / act_sum
        neg_entropy = jnp.sum(pi * log_pi, axis=0, keepdims=True)
        taken = place == action + 3
        picked_pi = jnp.sum(jnp.where(taken, log_pi, 0.0), axis=0, keepdims=True)
        gap = ret - target
        loss = loss - gap * picked_pi + ENTROPY_COEF * neg_entropy
        grad = gap * (pi - jnp.where(taken, 1.0, 0.0))
        grad = grad + ENTROPY_COEF * pi * (log_pi - neg_entropy)
        grad = jnp.where(actor, grad, 0.0)
        grad = jnp.where(place == 0, reward_err, grad)
        grad = jnp.where(place == 1, sigmoid - cont, grad)
        grad = jnp.where(place == 2, value_err, grad)
        gouts[VOCAB:OUTS, rows] = (grad * valid).astype(BF)
        lossacc[0:1, :] += loss * valid
        lossacc[1:2, :] += valid
        dh = dot_tn(gouts[:, rows], rt[...])
        grad_x, part = rms_pull(dh, x, top_gain)
        gx[rows, :] = grad_x
        dgain[2 * layers] += part
        return carry

    lax.fori_loop(0, chunks, losses, 0)
    tail_at = VOCAB + layers * 12 * 256 + OUTS
    put(0, dot_nn(gouts[0:VOCAB, :], hs[2 * layers]))
    put(tail_at, dot_nn(gouts[VOCAB:OUTS, :], hs[2 * layers]))
    loss_total = jnp.sum(lossacc[0:1, :])
    count_total = jnp.sum(lossacc[1:2, :])
    place = iota(scal_ref.shape, 0)
    scal_ref[...] = jnp.where(place == 0, loss_total, jnp.where(place == 1, count_total, 0.0))

    def feed_back(layer):
        def body(c, carry):
            rows = chunk_rows(c)
            grad = gx[rows, :]
            low = grad.astype(BF)
            gl[rows, :] = low
            for j in range(ff // 256):
                cols = slice(j * 256, j * 256 + 256)
                da = dot_nt(low, wd[layer, cols, :])
                gds[layer, rows, cols] = (da * gds[layer, rows, cols].astype(F32)).astype(BF)
            dh = dot_nt(gds[layer, rows, :], wu[layer])
            gain = gains_ref[2 * layer + 1 : 2 * layer + 2, :]
            grad_x, part = rms_pull(dh, xs[2 * layer + 1, rows, :], gain)
            dgain[2 * layer + 1] += part
            grad = grad + grad_x
            gx[rows, :] = grad
            dmix[rows, :] = dot_nt(grad.astype(BF), wo[layer]).astype(BF)
            return carry

        lax.fori_loop(0, chunks, body, 0)

    def attend_back(layer):
        def one(b, pair):
            rows, window = pair_rows(b, pair), pair_window(pair)
            keys = both(kvs[layer, b, window, 0:dims])
            values = both(kvs[layer, b, window, dims:])
            queries = spread(qs[layer, rows, :])
            dout = spread(dmix[rows, :])
            p = probs[layer, b * pairs + pair]
            dp = dot_nt(values, dout)
            sides = []
            for side in range(2):
                part = slice(side * KEY, side * KEY + KEY)
                pf = p[part].astype(F32)
                d = dp[part]
                sides.append((pf * (d - jnp.sum(d * pf, axis=0, keepdims=True))).astype(BF))
            ds = jnp.concatenate(sides, axis=0)
            dq = gather_heads(dot_tn(ds, keys)) * scale
            dqkv[rows, 0:dims] = dq.astype(BF)
            dk = dot_nn(ds, queries) * scale
            dk = jnp.where(even_f, dk[0:KEY], dk[KEY:])
            dv = dot_nn(p, dout)
            dv = jnp.where(even_f, dv[0:KEY], dv[KEY:])
            old = pl.ds(pl.multiple_of(pair * QRY, 16), SEG)
            new = pl.ds(pl.multiple_of(pair * QRY + SEG, 16), QRY)
            dkv[b, old, 0:dims] += dk[0:SEG]
            dkv[b, old, dims:] += dv[0:SEG]
            dkv[b, new, 0:dims] = dk[SEG:]
            dkv[b, new, dims:] = dv[SEG:]

        def body(pair, carry):
            for b in range(batch):
                one(b, pair)
            return carry

        for b in range(batch):
            dkv[b, 0:SEG, :] = jnp.zeros((SEG, 2 * dims), F32)
        lax.fori_loop(0, 1, body, 0)
        for b in range(batch):
            bsend[layer, b] = dkv[b, 0:SEG, :].astype(BF)
        copy = backward_copy(layer)
        copy.start()
        lax.fori_loop(1, pairs, body, 0)
        copy.wait()
        for b in range(batch):
            dkv[b, span : span + SEG, :] += brecv[layer, b].astype(F32)

    def project_back(layer):
        def body(c, carry):
            rows = chunk_rows(c)
            dqkv[rows, dims:] = dkv[c // per_seq, kv_rows(c), :].astype(BF)
            dh = dot_nt(dqkv[rows, :], wq[layer])
            gain = gains_ref[2 * layer : 2 * layer + 1, :]
            grad_x, part = rms_pull(dh, xs[2 * layer, rows, :], gain)
            dgain[2 * layer] += part
            gx[rows, :] += grad_x
            return carry

        lax.fori_loop(0, chunks, body, 0)

    at = VOCAB
    for layer in reversed(range(layers)):
        feed_back(layer)
        for j in range(ff // 256):
            cols = slice(j * 256, j * 256 + 256)
            put(at, dot_tn(acts[layer, :, cols], gl[...]))
            at += 256
        for j in range(ff // 256):
            cols = slice(j * 256, j * 256 + 256)
            put(at, dot_tn(hs[2 * layer + 1], gds[layer, :, cols]))
            at += 256
        gl[...] = gx[...].astype(BF)
        put(at, dot_tn(mixes[layer], gl[...]))
        at += 256
        attend_back(layer)
        project_back(layer)
        for j in range(3):
            cols = slice(j * 256, j * 256 + 256)
            put(at, dot_tn(hs[2 * layer], dqkv[:, cols]))
            at += 256
    gl[...] = gx[...].astype(BF)

    def mark(c, carry):
        gouts[:, chunk_rows(c)] = onehot(c)
        return carry

    lax.fori_loop(0, chunks, mark, 0)
    put(at, dot_nn(gouts[...], gl[...]))
    at = tail_at + OUTS - VOCAB
    place = iota((16, dims), 0)
    gain_rows = jnp.zeros((16, dims), F32)
    for index in range(2 * layers + 1):
        gain_rows = jnp.where(place == index, jnp.sum(dgain[index], axis=0, keepdims=True), gain_rows)
    put(at, gain_rows)
    at += 16
    put(at, jnp.zeros((grads_ref.shape[1] - at, dims), F32))


def gradients(codes, actions, next_codes, lengths, rewards, continues, values, weights, seq_size):
    table, attn_in, attn_out, ffn_in, ffn_out, gains, readout = weights
    batch, span = codes.shape
    layers, dims, ff = ffn_in.shape
    total = batch * span
    tiles = span // SEG
    chunks = total // ROWS
    grad_rows = grad_row_count(layers)
    steps = np.arange(lax.axis_size("seq") * tiles + 1, dtype=np.float64)[:, None]
    freq = np.exp(np.arange(dims // 2) * (-2.0 * math.log(10000.0) / dims))
    trig = np.zeros((steps.shape[0], 8, dims // 2), np.float32)
    trig[:, 0], trig[:, 1] = np.sin(steps * SEG * freq), np.cos(steps * SEG * freq)
    trig[:, 2], trig[:, 3] = np.sin(steps * freq), np.cos(steps * freq)
    trig = jnp.asarray(trig)
    vmem = pl.BlockSpec(memory_space=pltpu.VMEM)
    smem = pl.BlockSpec(memory_space=pltpu.SMEM)
    return pl.pallas_call(
        functools.partial(step_kernel, layers, seq_size),
        out_shape=(
            jax.ShapeDtypeStruct((2, grad_rows, dims // 2), BF),
            jax.ShapeDtypeStruct((8, 128), F32),
        ),
        in_specs=[vmem] * 3 + [smem] + [vmem] * 5 + [pl.BlockSpec(memory_space=pltpu.HBM)] * 4 + [vmem] * 2,
        out_specs=(vmem, vmem),
        scratch_shapes=[
            pltpu.VMEM((layers, dims, 3 * dims), BF),
            pltpu.VMEM((layers, dims, dims), BF),
            pltpu.VMEM((layers, dims, ff), BF),
            pltpu.VMEM((layers, ff, dims), BF),
            pltpu.VMEM((OUTS, dims), BF),
            pltpu.VMEM((OUTS, dims), BF),
            pltpu.VMEM((2 * layers + 1, total, dims), F32),
            pltpu.VMEM((2 * layers + 1, total, dims), BF),
            pltpu.VMEM((layers, total, dims), BF),
            pltpu.VMEM((layers, batch, SEG + span, 2 * dims), BF),
            pltpu.VMEM((layers, total // QRY, 2 * KEY, HEADS // 2 * QRY), BF),
            pltpu.VMEM((layers, total, ff), BF),
            pltpu.VMEM((layers, total, ff), BF),
            pltpu.VMEM((layers, total, dims), BF),
            pltpu.VMEM((total // QRY, 8, HEADS // 2 * QRY), jnp.int32),
            pltpu.VMEM((chunks, 8, ROWS), F32),
            pltpu.VMEM((chunks, 8, ROWS), jnp.int32),
            pltpu.VMEM((OUTS, total), BF),
            pltpu.VMEM((total, dims), F32),
            pltpu.VMEM((total, dims), BF),
            pltpu.VMEM((total, dims), BF),
            pltpu.VMEM((total, 3 * dims), BF),
            pltpu.VMEM((batch, SEG + span, 2 * dims), F32),
            pltpu.VMEM((2 * layers + 1, 8, dims), F32),
            pltpu.VMEM((8, ROWS), F32),
            pltpu.VMEM((4, 8, span), F32),
            pltpu.VMEM((layers, batch, SEG, 2 * dims), BF),
            pltpu.VMEM((layers, batch, SEG, 2 * dims), BF),
            pltpu.SemaphoreType.DMA((2 * layers,)),
            pltpu.SemaphoreType.DMA((2 * layers,)),
            pltpu.SemaphoreType.DMA((12 * layers,)),
        ],
        compiler_params=pltpu.CompilerParams(
            collective_id=0, has_side_effects=True, vmem_limit_bytes=63 * 1024 * 1024
        ),
        name="train_step",
    )(
        codes,
        actions,
        next_codes,
        lengths,
        rewards,
        continues,
        values,
        trig,
        table,
        attn_in,
        attn_out,
        ffn_in,
        ffn_out,
        gains,
        readout,
    )


def grad_row_count(layers):
    rows = VOCAB + layers * 12 * 256 + OUTS + (OUTS - VOCAB) + 16
    return -(-rows // 256) * 256


def buckets_of(layers):
    cuts = [0, VOCAB + 8 * 256]
    for layer in range(layers):
        cuts.append(cuts[-1] + 4 * 256)
        if layer < layers - 1:
            cuts.append(cuts[-1] + 8 * 256)
    cuts[-1] = grad_row_count(layers)
    return list(zip(cuts[:-1], cuts[1:]))


class Exchange:
    def __init__(self, seq_size, dp_size, source, total, core_in, seq_in, deep_in, sems):
        self.seq_size, self.deep = seq_size, dp_size // 2
        self.owners = min(4, self.deep)
        self.source, self.total = source, total
        self.core_in, self.seq_in, self.deep_in = core_in, seq_in, deep_in
        self.send_sem, self.recv_sem = sems
        self.at_seq = lax.axis_index("seq")
        at_dp = lax.axis_index("dp")
        self.core = lax.rem(at_dp, 2)
        self.at_deep = lax.div(at_dp, 2)

    def sibling(self):
        return {"dp": self.at_deep * 2 + 1 - self.core}

    def seq_peer(self, k):
        return {"seq": lax.rem(self.at_seq + k, self.seq_size)}

    def deep_peer(self, k):
        return {"dp": lax.rem(self.at_deep + k, self.deep) * 2 + self.core}

    def peers(self):
        found = [self.sibling()]
        found += [self.seq_peer(k) for k in range(1, self.seq_size)]
        return found + [self.deep_peer(k) for k in range(1, self.deep)]

    def greet(self):
        barrier = pltpu.get_barrier_semaphore()
        found = self.peers()
        for peer in found:
            pl.semaphore_signal(barrier, inc=1, device_id=peer, device_id_type=MESH)
        pl.semaphore_wait(barrier, len(found))

    def copy(self, src, dst, bucket, slot, peer):
        return pltpu.make_async_remote_copy(
            src_ref=src,
            dst_ref=dst,
            send_sem=self.send_sem.at[bucket, slot],
            recv_sem=self.recv_sem.at[bucket, slot],
            device_id=peer,
            device_id_type=MESH,
        )

    def only(self, condition, act):
        if self.owners == self.deep:
            act()
        else:
            pl.when(condition)(act)

    def slots(self):
        return 2 * (1 + self.seq_size - 1 + self.deep - 1)

    def parts(self, bucket):
        r0, r1 = bucket
        quarter = (r1 - r0) // self.seq_size
        return r0, r1 - r0, quarter, quarter // self.owners

    def seq_rows(self, bucket, index):
        r0, _, quarter, _ = self.parts(bucket)
        return pl.ds(pl.multiple_of(r0 + index * quarter, 16), quarter)

    def share_rows(self, bucket, index):
        r0, _, quarter, share = self.parts(bucket)
        return pl.ds(pl.multiple_of(r0 // self.seq_size + index * share, 16), share)

    def own_rows(self, bucket):
        r0, _, quarter, share = self.parts(bucket)
        at = r0 + self.at_seq * quarter + lax.rem(self.at_deep, self.owners) * share
        return pl.ds(pl.multiple_of(at, 16), share)

    def core_copy(self, n, bucket):
        r0, rows, _, _ = self.parts(bucket)
        part = pl.ds(r0, rows)
        return self.copy(self.source.at[1 - self.core, part], self.core_in.at[part], n, 0, self.sibling())

    def seq_copies(self, n, bucket):
        r0, _, quarter, _ = self.parts(bucket)
        found = []
        for k in range(1, self.seq_size):
            rows = self.seq_rows(bucket, lax.rem(self.at_seq + k, self.seq_size))
            dest = self.seq_in.at[k - 1, pl.ds(r0 // self.seq_size, quarter)]
            found.append(self.copy(self.core_in.at[rows], dest, n, k, self.seq_peer(k)))
        return found

    def deep_copy(self, n, bucket, k):
        r0, _, _, share = self.parts(bucket)
        target = lax.rem(self.at_deep + k, self.deep)
        rows = self.share_rows(bucket, lax.rem(target, self.owners))
        dest = self.deep_in.at[k - 1, pl.ds(r0 // (self.seq_size * self.owners), share)]
        return self.copy(self.seq_out.at[rows], dest, n, self.seq_size - 1 + k, self.deep_peer(k))

    def back_copy(self, n, rows, slot, peer):
        there = self.total.at[self.core, rows]
        return self.copy(there, there, n, self.slots() // 2 + slot, peer)

    def core_start(self, n, bucket):
        self.core_copy(n, bucket).start()

    def core_finish(self, n, bucket):
        self.core_copy(n, bucket).wait()
        r0, rows, _, _ = self.parts(bucket)

        def add(i, carry):
            part = pl.ds(pl.multiple_of(r0 + i * 256, 256), 256)
            both = self.source[self.core, part, :].astype(F32) + self.core_in[part, :].astype(F32)
            self.core_in[part, :] = both.astype(BF)
            return carry

        lax.fori_loop(0, rows // 256, add, 0)

    def seq_start(self, n, bucket):
        for copy in self.seq_copies(n, bucket):
            copy.start()

    def seq_finish(self, n, bucket):
        for copy in self.seq_copies(n, bucket):
            copy.wait()
        r0, _, quarter, _ = self.parts(bucket)

        def add(i, carry):
            here = pl.ds(pl.multiple_of(r0 + self.at_seq * quarter + i * 64, 16), 64)
            part = pl.ds(pl.multiple_of(r0 // self.seq_size + i * 64, 16), 64)
            both = self.core_in[here, :].astype(F32)
            for k in range(self.seq_size - 1):
                both = both + self.seq_in[k, part, :].astype(F32)
            self.seq_out[part, :] = both.astype(BF)
            return carry

        lax.fori_loop(0, quarter // 64, add, 0)

    def deep_start(self, n, bucket):
        for k in range(1, self.deep):
            target = lax.rem(self.at_deep + k, self.deep)
            self.only(target < self.owners, self.deep_copy(n, bucket, k).start)

    def deep_finish(self, n, bucket):
        r0, _, _, share = self.parts(bucket)
        for k in range(1, self.deep):
            target = lax.rem(self.at_deep + k, self.deep)
            self.only(target < self.owners, self.deep_copy(n, bucket, k).wait_send)

        def act():
            for k in range(1, self.deep):
                self.deep_copy(n, bucket, k).wait_recv()
            mine = self.share_rows(bucket, lax.rem(self.at_deep, self.owners))
            both = self.seq_out[mine, :].astype(F32)
            part = pl.ds(r0 // (self.seq_size * self.owners), share)
            for k in range(self.deep - 1):
                both = both + self.deep_in[k, part, :].astype(F32)
            self.total[self.core, self.own_rows(bucket), :] = both.astype(BF)
            squares = (both * both).reshape(share // 8, 8, both.shape[1])
            self.squares[...] += jnp.sum(squares, axis=0)

        self.only(self.at_deep < self.owners, act)

    def back_deep(self, n, bucket, k):
        return self.back_copy(n, self.own_rows(bucket), self.seq_size - 1 + k, self.deep_peer(k))

    def back_deep_start(self, n, bucket):
        def act():
            for k in range(1, self.deep):
                self.back_deep(n, bucket, k).start()

        self.only(self.at_deep < self.owners, act)

    def back_deep_finish(self, n, bucket):
        def act():
            for k in range(1, self.deep):
                self.back_deep(n, bucket, k).wait_send()

        self.only(self.at_deep < self.owners, act)
        for k in range(1, self.deep):
            origin = lax.rem(self.at_deep + self.deep - k, self.deep)
            self.only(origin < self.owners, self.back_deep(n, bucket, k).wait_recv)

    def back_seq(self, n, bucket):
        rows = self.seq_rows(bucket, self.at_seq)
        return [self.back_copy(n, rows, k, self.seq_peer(k)) for k in range(1, self.seq_size)]

    def back_seq_start(self, n, bucket):
        for copy in self.back_seq(n, bucket):
            copy.start()

    def back_seq_finish(self, n, bucket):
        for copy in self.back_seq(n, bucket):
            copy.wait()

    def back_core(self, n, bucket):
        r0, rows, _, _ = self.parts(bucket)
        return self.back_copy(n, pl.ds(r0, rows), 0, self.sibling())

    def back_core_start(self, n, bucket):
        self.back_core(n, bucket).start()

    def back_core_finish(self, n, bucket):
        self.back_core(n, bucket).wait()

    def tile_copies(self, n, tile, phase):
        if phase == 0:
            slots, peers = [0], [self.sibling()]
        elif phase == 1:
            slots = list(range(1, self.seq_size))
            peers = [self.seq_peer(k) for k in slots]
        else:
            slots = [self.seq_size - 1 + k for k in range(1, self.deep)]
            peers = [self.deep_peer(k) for k in range(1, self.deep)]
        return [
            self.copy(self.tile_out.at[tile, phase], self.tile_in.at[tile, slot], n, slot, peer)
            for slot, peer in zip(slots, peers)
        ], slots

    def tile_start(self, n, tile, phase):
        for copy in self.tile_copies(n, tile, phase)[0]:
            copy.start()

    def tile_finish(self, n, tile, phase):
        copies, slots = self.tile_copies(n, tile, phase)
        for copy in copies:
            copy.wait()
        both = self.tile_out[tile, phase]
        for slot in slots:
            both = both + self.tile_in[tile, slot]
        self.tile_out[tile, phase + 1] = both


def sum_kernel(sizes, buckets, source, scal_ref, total, out_ref, core_in, seq_in, seq_out, deep_in,
               squares, tile_out, tile_in, send_sem, recv_sem):
    ex = Exchange(*sizes, source, total, core_in, seq_in, deep_in, (send_sem, recv_sem))
    ex.seq_out, ex.squares, ex.tile_out, ex.tile_in = seq_out, squares, tile_out, tile_in
    ex.greet()
    squares[...] = jnp.zeros_like(squares)
    listed = list(enumerate(buckets))
    first, second = len(buckets), len(buckets) + 1
    tile_out[0, 0] = scal_ref[...]
    for n, bucket in listed:
        ex.core_start(n, bucket)
    ex.tile_start(first, 0, 0)
    for n, bucket in listed:
        ex.core_finish(n, bucket)
        ex.seq_start(n, bucket)
    ex.tile_finish(first, 0, 0)
    ex.tile_start(first, 0, 1)
    for n, bucket in listed:
        ex.seq_finish(n, bucket)
        ex.deep_start(n, bucket)
    ex.tile_finish(first, 0, 1)
    ex.tile_start(first, 0, 2)
    for n, bucket in listed:
        ex.deep_finish(n, bucket)
        ex.back_deep_start(n, bucket)
    ex.tile_finish(first, 0, 2)
    tile_out[1, 0] = squares[...]
    ex.tile_start(second, 1, 0)
    for n, bucket in listed:
        ex.back_deep_finish(n, bucket)
        ex.back_seq_start(n, bucket)
    ex.tile_finish(second, 1, 0)
    ex.tile_start(second, 1, 1)
    for n, bucket in listed:
        ex.back_seq_finish(n, bucket)
        ex.back_core_start(n, bucket)
    ex.tile_finish(second, 1, 1)
    ex.tile_start(second, 1, 2)
    ex.tile_finish(second, 1, 2)
    for n, bucket in listed:
        ex.back_core_finish(n, bucket)
    count = tile_out[0, 3, 1:2, 0:1]
    average = jnp.sum(tile_out[1, 3]) / (count * count)
    norm = jnp.sqrt(average)
    place = iota(out_ref.shape, 0)
    out = jnp.where(place == 2, norm, tile_out[0, 3])
    out_ref[...] = jnp.where(place == 3, jnp.minimum(1.0, CLIP_NORM / norm) / count, out)


def sum_gradients(grads, scal, layers, seq_size, dp_size):
    buckets = buckets_of(layers)
    rows = grads.shape[1]
    deep = dp_size // 2
    owners = min(4, deep)
    slots = 2 * (seq_size + deep - 1)
    vmem = pl.BlockSpec(memory_space=pltpu.VMEM)
    return pl.pallas_call(
        functools.partial(sum_kernel, (seq_size, dp_size), buckets),
        out_shape=(
            jax.ShapeDtypeStruct(grads.shape, BF),
            jax.ShapeDtypeStruct((8, 128), F32),
        ),
        in_specs=[vmem, vmem],
        out_specs=(vmem, vmem),
        scratch_shapes=[
            pltpu.VMEM((rows, 128), BF),
            pltpu.VMEM((seq_size - 1, rows // seq_size, 128), BF),
            pltpu.VMEM((rows // seq_size, 128), BF),
            pltpu.VMEM((deep - 1, rows // (seq_size * owners), 128), BF),
            pltpu.VMEM((8, 128), F32),
            pltpu.VMEM((2, 4, 8, 128), F32),
            pltpu.VMEM((2, slots // 2, 8, 128), F32),
            pltpu.SemaphoreType.DMA((len(buckets) + 2, slots)),
            pltpu.SemaphoreType.DMA((len(buckets) + 2, slots)),
        ],
        compiler_params=pltpu.CompilerParams(
            collective_id=1, has_side_effects=True, vmem_limit_bytes=62 * 1024 * 1024
        ),
        name="sum_gradients",
    )(grads, scal)


def adam_update(weight, first_mom, second_mom, clipped, rate):
    new_first = BETA_ONE * first_mom + (1.0 - BETA_ONE) * clipped
    new_second = BETA_TWO * second_mom + (1.0 - BETA_TWO) * clipped * clipped
    ratio = (
        new_first
        / (1.0 - BETA_ONE**STEP)
        / (jnp.sqrt(new_second / (1.0 - BETA_TWO**STEP)) + ADAM_EPS)
    )
    return (weight - rate * (ratio + DECAY * weight), new_first, new_second)


def update_kernel(layers, scal_ref, grads_ref, *refs):
    ins, outs, here = refs[0:21], refs[21:42], refs[42:63]
    load_sem, store_sem = refs[63], refs[64]
    scale = scal_ref[3, 0]
    pieces = [(slot, layer) for slot in (4, 3, 1, 2) for layer in range(layers)]
    pieces += [(0, None), (6, None), (5, None)]

    def view(ref, layer):
        return ref if layer is None else ref.at[layer]

    def moves(n, kind):
        slot, layer = pieces[n]
        for part in range(3):
            index = 3 * slot + part
            inside = view(here[index], layer)
            if kind == 0:
                yield pltpu.make_async_copy(view(ins[index], layer), inside, load_sem.at[n, part])
            else:
                yield pltpu.make_async_copy(inside, view(outs[index], layer), store_sem.at[n, part])

    for n in range(len(pieces)):
        for move in moves(n, 0):
            move.start()

    def renew(slot, layer, rows, cols, grad):
        refs = [view(here[3 * slot + part], layer) for part in range(3)]
        new = adam_update(*[ref[rows, cols] for ref in refs], grad.astype(F32) * scale, RATES[slot])
        for ref, value in zip(refs, new):
            ref[rows, cols] = value

    offset = VOCAB
    starts = {}
    for layer in reversed(range(layers)):
        starts[4, layer] = offset
        starts[3, layer] = offset + 4 * 256
        starts[2, layer] = offset + 8 * 256
        starts[1, layer] = offset + 9 * 256
        offset += 12 * 256
    table_at, tail_at = offset, offset + OUTS
    gains_at = tail_at + OUTS - VOCAB

    for n, (slot, layer) in enumerate(pieces):
        for move in moves(n, 0):
            move.wait()
        if layer is not None:
            rows_all, cols_all = here[3 * slot].shape[1:]
            at = starts[slot, layer]
            for j in range(rows_all // 256):
                for i in range(cols_all // 256):
                    for side in range(2):
                        cols = slice(i * 256 + side * 128, i * 256 + side * 128 + 128)

                        def body(k, carry):
                            rows = pl.ds(pl.multiple_of(j * 256 + k * 64, 64), 64)
                            block = at + (j + i) * 256 + k * 64
                            grad = grads_ref[side, pl.ds(pl.multiple_of(block, 64), 64), :]
                            renew(slot, layer, rows, cols, grad)
                            return carry

                        lax.fori_loop(0, 4, body, 0)
        elif slot == 0:
            rows_all = here[0].shape[0]
            for side in range(2):
                cols = slice(side * 128, side * 128 + 128)

                def body(k, carry):
                    rows = pl.ds(pl.multiple_of(k * 64, 64), 64)
                    block = pl.ds(pl.multiple_of(table_at + k * 64, 64), 64)
                    renew(0, None, rows, cols, grads_ref[side, block, :])
                    return carry

                full = rows_all // 64
                lax.fori_loop(0, full, body, 0)
                if rows_all % 64:
                    last = slice(full * 64, rows_all)
                    block = grads_ref[side, table_at + full * 64 : table_at + full * 64 + 64, :]
                    renew(0, None, last, cols, block.astype(F32)[0 : rows_all % 64])
        elif slot == 6:
            outs_all = here[18].shape[0]
            for side in range(2):
                cols = slice(side * 128, side * 128 + 128)

                def body(k, carry):
                    rows = pl.ds(pl.multiple_of(k * 64, 64), 64)
                    renew(6, None, rows, cols, grads_ref[side, rows, :])
                    return carry

                lax.fori_loop(0, VOCAB // 64, body, 0)
                rest = grads_ref[side, tail_at : tail_at + OUTS - VOCAB, :].astype(F32)
                renew(6, None, slice(VOCAB, outs_all), cols, rest[0 : outs_all - VOCAB])
        else:
            count = here[15].shape[0]
            for side in range(2):
                cols = slice(side * 128, side * 128 + 128)
                grad = grads_ref[side, gains_at : gains_at + 16, :].astype(F32)[0:count]
                renew(5, None, slice(0, count), cols, grad)
        for move in moves(n, 1):
            move.start()
    for n in range(len(pieces)):
        for move in moves(n, 1):
            move.wait()


def update(grads, scal, state):
    layers = state[3].shape[0]
    anywhere = pl.BlockSpec(memory_space=pltpu.HBM)
    pieces = 4 * layers + 3
    return pl.pallas_call(
        functools.partial(update_kernel, layers),
        out_shape=tuple(jax.ShapeDtypeStruct(x.shape, F32) for x in state),
        in_specs=[
            pl.BlockSpec(memory_space=pltpu.SMEM),
            pl.BlockSpec(memory_space=pltpu.VMEM),
        ]
        + [anywhere] * 21,
        out_specs=(anywhere,) * 21,
        scratch_shapes=[pltpu.VMEM(x.shape, F32) for x in state]
        + [pltpu.SemaphoreType.DMA((pieces, 3)), pltpu.SemaphoreType.DMA((pieces, 3))],
        compiler_params=pltpu.CompilerParams(vmem_limit_bytes=62 * 1024 * 1024),
        name="update",
    )(scal, grads, *state)


def local(codes, actions, next_codes, lengths, rewards, continues, target_values, *state):
    state = state[0:18] + tuple(value.T for value in state[18:21])
    params = state[0::3]
    seq_size, dp_size = lax.axis_size("seq"), lax.axis_size("dp")
    layers = params[1].shape[0]
    grads, scal = gradients(
        codes, actions, next_codes, lengths, rewards, continues, target_values, params, seq_size
    )
    grads, scal = sum_gradients(grads, scal, layers, seq_size, dp_size)
    results = list(update(grads, scal, state))
    results[18:21] = [value.T for value in results[18:21]]
    return tuple(results) + (scal[0, 0], scal[1, 0], scal[2, 0])


def solution(mesh):
    rows, whole = P("dp", "seq"), P()
    return jax.shard_map(
        local,
        mesh=mesh,
        in_specs=(rows, rows, rows, P("dp", None), rows, rows, rows) + (whole,) * 21,
        out_specs=(whole,) * 24,
        check_vma=False,
    )
```

```python
import functools
import math

import jax
import jax.numpy as jnp
import numpy as np
from jax import lax
from jax.experimental import pallas as pl
from jax.experimental.pallas import tpu as pltpu
from jax.sharding import PartitionSpec as P

HEADS = 8
VOCAB = 512
SEG = 48
STEP = 5

EPS_NORM = 1e-06
BETA_ONE = 0.9
BETA_TWO = 0.999
RATES = (0.25, 0.02, 0.08, 0.02, 0.02, 0.25, 0.02)
DECAY = 0.01
ADAM_EPS = 1e-08
CLIP_NORM = 0.05
GAMMA = 0.985
LAMBDA_RET = 0.95
ENTROPY_COEF = 0.05

BF = jnp.bfloat16
F32 = jnp.float32
ROWS = 256
QRY = 2 * SEG
KEY = 3 * SEG
OUTS = 544
NEG = -1e30
MESH = pl.DeviceIdType.MESH
PER_ROW = 256 / 92e3
TRANSFERS = {
    "core": ("core", PER_ROW / 5.4, 1.1),
    "one": ("seq", PER_ROW / 2, 2.8),
    "two": ("seq", PER_ROW / 4, 2.8),
    "all": ("seq", PER_ROW, 3.3),
    "deep": ("deep", PER_ROW / 2, 3.5),
    "tile": ("tile", 0.0, 3.6),
}
LONG = ("core", "one", "two", "deep", "back_deep", "back_two", "back_one", "back_core")
SHORT = ("core", "all", "deep", "back_deep", "back_all", "back_core")
STAGE_TIME = 0.35


def dot_nn(left, right):
    return jnp.dot(left, right, preferred_element_type=F32)


def dot_tn(left, right):
    return lax.dot_general(left, right, (((0,), (0,)), ((), ())), preferred_element_type=F32)


def dot_nt(left, right):
    return lax.dot_general(left, right, (((1,), (1,)), ((), ())), preferred_element_type=F32)


def iota(shape, dim):
    return lax.broadcasted_iota(jnp.int32, shape, dim)


def rms_apply(x, gain):
    inv = lax.rsqrt(jnp.mean(x * x, axis=-1, keepdims=True) + EPS_NORM)
    return (x * inv * gain).astype(BF)


def rms_pull(grad, x, gain):
    inv = lax.rsqrt(jnp.mean(x * x, axis=-1, keepdims=True) + EPS_NORM)
    unit = x * inv
    weighted = grad * gain
    grad_x = inv * (weighted - unit * jnp.mean(weighted * unit, axis=-1, keepdims=True))
    rows, dims = x.shape
    return grad_x, jnp.sum((grad * unit).reshape(rows // 8, 8, dims), axis=0)


def grad_row_count(layers):
    rows = VOCAB + layers * 12 * 256 + OUTS + (OUTS - VOCAB) + 16
    return -(-rows // 256) * 256


def buckets_of(layers):
    cuts = [0, VOCAB + 4 * 256]
    for layer in range(layers):
        cuts.append(cuts[-1] + 5 * 256)
        cuts.append(cuts[-1] + (3 if layer == layers - 1 else 7) * 256)
    cuts.append(grad_row_count(layers))
    return list(zip(cuts[:-1], cuts[1:]))


class Exchange:
    def __init__(self, seq_size, dp_size, buckets, grads, out, core_in, one_in, two_in, two_out, deep_in,
                 squares, tile_out, tile_in, send_sem, recv_sem, out_sem):
        self.deep = dp_size // 2
        self.owners = min(4, self.deep)
        self.seq_size = seq_size
        self.buckets = buckets
        self.grads, self.out = grads, out
        self.core_in, self.one_in, self.two_in, self.two_out = core_in, one_in, two_in, two_out
        self.deep_in, self.squares = deep_in, squares
        self.tile_out, self.tile_in = tile_out, tile_in
        self.send_sem, self.recv_sem, self.out_sem = send_sem, recv_sem, out_sem
        self.slots = exchange_slots(dp_size)
        me = lax.axis_index("seq")
        at_dp = lax.axis_index("dp")
        self.me, self.core, self.at_deep = me, lax.rem(at_dp, 2), lax.div(at_dp, 2)
        across = me + 1 - 2 * lax.rem(me, 2)
        along = me + 2 - 4 * lax.div(me, 2)
        self.first = across + self.core * (along - across)
        self.second = along + self.core * (across - along)
        self.opposite = 3 - me
        self.sibling = {"dp": self.at_deep * 2 + 1 - self.core}
        self.stage, self.due, self.free, self.now, self.summed = {}, {}, {}, 0.0, 0

    def deep_peer(self, k):
        return {"dp": lax.rem(self.at_deep + k, self.deep) * 2 + self.core}

    def peers(self):
        found = [self.sibling]
        found += [{"seq": lax.rem(self.me + k, self.seq_size)} for k in range(1, self.seq_size)]
        return found + [self.deep_peer(k) for k in range(1, self.deep)]

    def greet(self):
        for peer in self.peers():
            pl.semaphore_signal(
                pltpu.get_barrier_semaphore(), inc=1, device_id=peer, device_id_type=MESH
            )

    def greeted(self):
        pl.semaphore_wait(pltpu.get_barrier_semaphore(), len(self.peers()))

    def copy(self, src, dst, n, slot, peer):
        return pltpu.make_async_remote_copy(
            src_ref=src,
            dst_ref=dst,
            send_sem=self.send_sem.at[n, slot],
            recv_sem=self.recv_sem.at[n, slot],
            device_id=peer,
            device_id_type=MESH,
        )

    def only(self, condition, act):
        if self.owners == self.deep:
            act()
        else:
            pl.when(condition)(act)

    def parts(self, n):
        r0, r1 = self.buckets[n]
        quarter = (r1 - r0) // self.seq_size
        return r0, r1 - r0, quarter, quarter // self.owners

    def quarter_rows(self, n, index):
        r0, _, quarter, _ = self.parts(n)
        return pl.ds(pl.multiple_of(r0 + index * quarter, 16), quarter)

    def packed_rows(self, n):
        r0, _, quarter, _ = self.parts(n)
        return pl.ds(r0 // self.seq_size, quarter)

    def share_rows(self, n, index):
        r0, _, _, share = self.parts(n)
        return pl.ds(pl.multiple_of(r0 // self.seq_size + index * share, 16), share)

    def own_rows(self, n):
        r0, _, quarter, share = self.parts(n)
        at = r0 + self.me * quarter + lax.rem(self.at_deep, self.owners) * share
        return pl.ds(pl.multiple_of(at, 16), share)

    def blocks(self, n, index, work):
        r0, _, quarter, _ = self.parts(n)
        size = quarter // 2 if quarter > 256 else quarter
        for at in range(0, quarter, size):
            wide = pl.ds(pl.multiple_of(r0 + index * quarter + at, 16), size)
            work(wide, pl.ds(r0 // self.seq_size + at, size))

    def core_copies(self, n):
        r0, rows, _, _ = self.parts(n)
        part = pl.ds(r0, rows)
        return [self.copy(self.grads.at[1 - self.core, part], self.core_in.at[part], n, 0, self.sibling)]

    def one_copies(self, n):
        packed = self.packed_rows(n)
        return [
            self.copy(self.core_in.at[self.quarter_rows(n, q)], self.one_in.at[k, packed], n, 1 + k,
                      {"seq": self.first})
            for k, q in enumerate((self.first, self.opposite))
        ]

    def two_copies(self, n):
        source = self.core_in.at[self.quarter_rows(n, self.second)]
        return [self.copy(source, self.two_in.at[self.packed_rows(n)], n, 3, {"seq": self.second})]

    def deep_copy(self, n, k):
        r0, _, _, share = self.parts(n)
        target = lax.rem(lax.rem(self.at_deep + k, self.deep), self.owners)
        dest = self.deep_in.at[k - 1, pl.ds(r0 // (self.seq_size * self.owners), share)]
        return self.copy(self.two_out.at[self.share_rows(n, target)], dest, n, 3 + k, self.deep_peer(k))

    def back_copy(self, n, rows, slot, peer):
        there = self.grads.at[self.core, rows]
        return self.copy(there, there, n, self.slots // 2 + slot, peer)

    def all_copies(self, n):
        packed = self.packed_rows(n)
        into = (self.one_in.at[0, packed], self.one_in.at[1, packed], self.two_in.at[packed])
        found = []
        for k in range(1, self.seq_size):
            peer = lax.rem(self.me + k, self.seq_size)
            source = self.core_in.at[self.quarter_rows(n, peer)]
            found.append(self.copy(source, into[k - 1], n, k, {"seq": peer}))
        return found

    def back_all(self, n):
        rows = self.quarter_rows(n, self.me)
        return [
            self.back_copy(n, rows, k, {"seq": lax.rem(self.me + k, self.seq_size)})
            for k in range(1, self.seq_size)
        ]

    def back_two(self, n):
        return [self.back_copy(n, self.quarter_rows(n, self.me), 3, {"seq": self.second})]

    def back_one(self, n):
        return [
            self.back_copy(n, self.quarter_rows(n, q), 1 + k, {"seq": self.first})
            for k, q in enumerate((self.me, self.second))
        ]

    def back_core(self, n):
        r0, rows, _, _ = self.parts(n)
        return [self.back_copy(n, pl.ds(r0, rows), 0, self.sibling)]

    def out_copies(self, n):
        r0, rows, _, _ = self.parts(n)
        part = pl.ds(r0, rows)
        return [
            pltpu.make_async_copy(self.grads.at[side, part], self.out.at[side, part], self.out_sem.at[n, side])
            for side in range(2)
        ]

    def start(self, copies):
        for copy in copies:
            copy.start()

    def wait(self, copies):
        for copy in copies:
            copy.wait()

    def add_in(self, n, quarters, more=()):
        def work(wide, packed):
            both = self.grads[self.core, wide, :].astype(F32) + self.core_in[wide, :].astype(F32)
            for part in more:
                both = both + part[packed, :].astype(F32)
            self.core_in[wide, :] = both.astype(BF)

        for q in quarters:
            self.blocks(n, q, work)

    def own_sum(self, n, wide, packed):
        both = self.grads[self.core, wide, :].astype(F32) + self.core_in[wide, :].astype(F32)
        both = both + self.one_in[0, packed, :].astype(F32)
        if self.path(n) is SHORT:
            both = both + self.one_in[1, packed, :].astype(F32)
        return both + self.two_in[packed, :].astype(F32)

    def after_core(self, n):
        if self.path(n) is SHORT:
            self.add_in(n, [lax.rem(self.me + k, self.seq_size) for k in range(1, self.seq_size)])
        else:
            self.add_in(n, (self.first, self.opposite))

    def after_one(self, n):
        self.add_in(n, (self.second,), (self.one_in.at[1],))

    def after_two(self, n):
        def work(wide, packed):
            self.two_out[packed, :] = self.own_sum(n, wide, packed).astype(BF)

        self.blocks(n, self.me, work)

    def after_deep(self, n):
        r0, _, _, share = self.parts(n)

        def act():
            rows = self.own_rows(n)
            both = self.own_sum(n, rows, self.share_rows(n, lax.rem(self.at_deep, self.owners)))
            part = pl.ds(r0 // (self.seq_size * self.owners), share)
            for k in range(self.deep - 1):
                both = both + self.deep_in[k, part, :].astype(F32)
            self.grads[self.core, rows, :] = both.astype(BF)
            self.squares[...] += jnp.sum((both * both).reshape(share // 8, 8, both.shape[1]), axis=0)

        self.only(self.at_deep < self.owners, act)

    def begin_deep(self, n):
        for k in range(1, self.deep):
            target = lax.rem(self.at_deep + k, self.deep)
            self.only(target < self.owners, self.deep_copy(n, k).start)

    def end_deep(self, n):
        for k in range(1, self.deep):
            target = lax.rem(self.at_deep + k, self.deep)
            self.only(target < self.owners, self.deep_copy(n, k).wait_send)

        def act():
            for k in range(1, self.deep):
                self.deep_copy(n, k).wait_recv()

        self.only(self.at_deep < self.owners, act)

    def begin_back_deep(self, n):
        rows = self.own_rows(n)

        def act():
            for k in range(1, self.deep):
                self.back_copy(n, rows, 3 + k, self.deep_peer(k)).start()

        self.only(self.at_deep < self.owners, act)

    def end_back_deep(self, n):
        rows = self.own_rows(n)

        def act():
            for k in range(1, self.deep):
                self.back_copy(n, rows, 3 + k, self.deep_peer(k)).wait_send()

        self.only(self.at_deep < self.owners, act)
        for k in range(1, self.deep):
            origin = lax.rem(self.at_deep + self.deep - k, self.deep)
            self.only(origin < self.owners, self.back_copy(n, rows, 3 + k, self.deep_peer(k)).wait_recv)

    def path(self, n):
        return SHORT if n >= len(self.buckets) - 2 else LONG

    def begin_transfer(self, n, name):
        if name == "deep":
            self.begin_deep(n)
        elif name == "back_deep":
            self.begin_back_deep(n)
        else:
            self.start(getattr(self, name if "back" in name else name + "_copies")(n))

    def end_transfer(self, n, name):
        if name == "deep":
            self.end_deep(n)
        elif name == "back_deep":
            self.end_back_deep(n)
        else:
            self.wait(getattr(self, name if "back" in name else name + "_copies")(n))
        if name == "core":
            self.after_core(n)
        elif name == "one":
            self.after_one(n)
        elif name in ("two", "all"):
            self.after_two(n)
        elif name == "deep":
            self.after_deep(n)
        elif name == "back_core":
            self.start(self.out_copies(n))

    def launch(self, n):
        step = self.stage[n]
        if n < len(self.buckets):
            name, rows = self.path(n)[step], self.buckets[n][1] - self.buckets[n][0]
            self.begin_transfer(n, name)
        else:
            name, rows = "tile", 0
            self.tile_start(n - len(self.buckets), step)
        link, share, latency = TRANSFERS[name.replace("back_", "")]
        self.free[link] = max(self.now, self.free.get(link, 0.0)) + rows * share
        self.due[n] = self.free[link] + latency

    def begin(self, n):
        self.stage[n] = 0
        self.launch(n)

    def advance(self, n):
        step = self.stage[n]
        self.now = max(self.now, self.due.pop(n)) + STAGE_TIME
        self.stage[n] += 1
        if n < len(self.buckets):
            path = self.path(n)
            self.end_transfer(n, path[step])
            self.summed += path[step] == "deep"
            more = step + 1 < len(path)
        else:
            self.tile_finish(n - len(self.buckets), step)
            more = step < 2
        if more:
            self.launch(n)
        norm = len(self.buckets) + 1
        if self.summed == len(self.buckets) and norm not in self.stage:
            self.tile_out[1, 0] = self.squares[...]
            self.begin(norm)

    def tick(self, spent):
        self.now += spent
        for n in sorted(self.due):
            if self.due[n] + 0.3 <= self.now:
                self.advance(n)

    def drain(self):
        while self.due:
            self.advance(min(self.due, key=lambda n: (self.due[n], n)))

    def tile_copies(self, tile, phase):
        if phase == 0:
            slots, peers = [0], [self.sibling]
        elif phase == 1:
            slots = list(range(1, self.seq_size))
            peers = [{"seq": lax.rem(self.me + k, self.seq_size)} for k in slots]
        else:
            slots = [3 + k for k in range(1, self.deep)]
            peers = [self.deep_peer(k) for k in range(1, self.deep)]
        n = len(self.buckets) + tile
        return [
            self.copy(self.tile_out.at[tile, phase], self.tile_in.at[tile, slot], n, slot, peer)
            for slot, peer in zip(slots, peers)
        ], slots

    def tile_start(self, tile, phase):
        self.start(self.tile_copies(tile, phase)[0])

    def tile_finish(self, tile, phase):
        copies, slots = self.tile_copies(tile, phase)
        self.wait(copies)
        both = self.tile_out[tile, phase]
        for slot in slots:
            both = both + self.tile_in[tile, slot]
        self.tile_out[tile, phase + 1] = both


def exchange_slots(dp_size):
    return 2 * (4 + dp_size // 2 - 1)


def step_kernel(
    layers,
    sizes,
    buckets,
    codes_ref,
    actions_ref,
    next_ref,
    lengths_ref,
    rewards_ref,
    continues_ref,
    values_ref,
    trig_ref,
    table_ref,
    attn_in_ref,
    attn_out_ref,
    ffn_in_ref,
    ffn_out_ref,
    gains_ref,
    readout_ref,
    out_ref,
    scal_ref,
    wq,
    wo,
    wu,
    wd,
    rt,
    tb,
    xs,
    hs,
    qs,
    kvs,
    probs,
    acts,
    gds,
    mixes,
    lows,
    tokf,
    toki,
    gouts,
    gx,
    gl,
    dmix,
    dqkv,
    carried,
    dgain,
    lossacc,
    lam,
    bsend,
    brecv,
    send_sem,
    recv_sem,
    load_sem,
    table_f,
    readout_f,
    grads_ref,
    *exchange_refs,
):
    batch, span = codes_ref.shape
    dims = gains_ref.shape[1]
    ff = ffn_in_ref.shape[2]
    tiles = span // SEG
    pairs = span // QRY
    total = batch * span
    chunks = total // ROWS
    per_seq = span // ROWS
    vocab_all = table_ref.shape[0]
    outs_all = readout_ref.shape[0]
    head_dim = dims // HEADS
    scale = head_dim ** (-0.5)
    exp_scale = scale * math.log2(math.e)
    groups = HEADS // 2
    base = lax.axis_index("seq") * span
    me = lax.axis_index("seq")
    seq_size = sizes[0]
    right = lax.rem(me + 1, seq_size)
    left = lax.rem(me + seq_size - 1, seq_size)

    ex = Exchange(*sizes, buckets, grads_ref, out_ref, *exchange_refs)
    ex.greet()
    ex.squares[...] = jnp.zeros_like(ex.squares)

    loads = [
        pltpu.make_async_copy(table_ref, table_f, load_sem.at[0]),
        pltpu.make_async_copy(readout_ref, readout_f, load_sem.at[1]),
    ]
    blocks = []
    for layer in range(layers):
        for j in range(3):
            blocks.append((attn_in_ref, wq, layer, slice(0, 256), slice(j * 256, j * 256 + 256)))
        blocks.append((attn_out_ref, wo, layer, slice(0, 256), slice(0, 256)))
        for j in range(ff // 256):
            blocks.append((ffn_in_ref, wu, layer, slice(0, 256), slice(j * 256, j * 256 + 256)))
        for j in range(ff // 256):
            blocks.append((ffn_out_ref, wd, layer, slice(j * 256, j * 256 + 256), slice(0, 256)))

    def place_of(k):
        at = (k + (2 * layers - 2) * chunks) % (2 * layers * chunks)
        return 1 + at // chunks, slice(256 * (at % chunks), 256 * (at % chunks) + 256)

    for k, (source, _, layer, rows, cols) in enumerate(blocks):
        plane, there = place_of(k)
        loads.append(
            pltpu.make_async_copy(source.at[layer, rows, cols], xs.at[plane, there, :], load_sem.at[2 + k])
        )
    for load in loads:
        load.start()

    def convert(low, high):
        for k in range(low, high):
            _, dest, layer, rows, cols = blocks[k]
            plane, there = place_of(k)
            loads[2 + k].wait()
            dest[layer, rows, cols] = xs[plane, there, :].astype(BF)

    tb[...] = jnp.zeros_like(tb)
    rt[...] = jnp.zeros_like(rt)

    ends = []
    for b in range(batch):
        run = jnp.int32(0)
        row = []
        for e in range(lengths_ref.shape[1]):
            run = run + lengths_ref[b, e]
            row.append(run)
        ends.append(row)
    episodes = len(ends[0])

    lane = iota((8, span), 1)
    lam[...] = jnp.zeros_like(lam)
    lam[0, 0:batch, :] = rewards_ref[...]
    lam[1, 0:batch, :] = continues_ref[...]
    lam[2, 0:batch, :] = values_ref[...]
    last = lax.rem(lane, SEG) == SEG - 1
    decay = GAMMA * lam[1]
    value_next = pltpu.roll(lam[2], span - 1, 1)
    add = jnp.where(last, lam[2], lam[0] + decay * ((1.0 - LAMBDA_RET) * value_next))
    mul = jnp.where(last, 0.0, decay * LAMBDA_RET)
    step = 1
    while step < SEG:
        add = add + mul * pltpu.roll(add, span - step, 1)
        mul = mul * pltpu.roll(mul, span - step, 1)
        step *= 2
    lam[3] = add
    valid_rows = []
    for b in range(batch):
        after = iota((1, span), 1) + (base + 1)
        final = after == ends[b][0]
        for e in range(1, episodes):
            final = final | (after == ends[b][e])
        valid_rows.append(jnp.where(final, 0.0, 1.0))
    for c in range(chunks):
        b = c // per_seq
        lanes = slice((c % per_seq) * ROWS, (c % per_seq) * ROWS + ROWS)
        for row in range(4):
            tokf[c, row : row + 1, :] = lam[row, b : b + 1, lanes]
        tokf[c, 4:5, :] = valid_rows[b][:, lanes]
        toki[c, 0:1, :] = codes_ref[b : b + 1, lanes]
        toki[c, 1:2, :] = actions_ref[b : b + 1, lanes]
        toki[c, 2:3, :] = next_ref[b : b + 1, lanes]

    half = dims // 2
    in_sin, in_cos = trig_ref[0:SEG, 2, :], trig_ref[0:SEG, 3, :]
    end_sin, end_cos = [], []
    for b in range(batch):
        for e in range(episodes):
            far, near = lax.div(ends[b][e], SEG), lax.rem(ends[b][e], SEG)
            far_sin, far_cos = trig_ref[far, 0:1, :], trig_ref[far, 1:2, :]
            near_sin, near_cos = trig_ref[near, 2:3, :], trig_ref[near, 3:4, :]
            end_sin.append(far_sin * near_cos + far_cos * near_sin)
            end_cos.append(far_cos * near_cos - far_sin * near_sin)

    def marks(tile, carry):
        at = me * tiles + tile
        tile_sin, tile_cos = trig_ref[at, 0:1, :], trig_ref[at, 1:2, :]
        here_sin = in_sin * tile_cos + in_cos * tile_sin
        here_cos = in_cos * tile_cos - in_sin * tile_sin
        place = iota((SEG, half), 0) + (base + tile * SEG)
        for b in range(batch):
            start_sin = jnp.zeros((SEG, half), F32)
            start_cos = jnp.ones((SEG, half), F32)
            for e in range(episodes):
                passed = place >= ends[b][e]
                row = b * episodes + e
                start_sin = jnp.where(passed, end_sin[row], start_sin)
                start_cos = jnp.where(passed, end_cos[row], start_cos)
            rows = pl.ds(pl.multiple_of(b * span + tile * SEG, SEG), SEG)
            xs[0, rows, 0:half] = here_sin * start_cos - here_cos * start_sin
            xs[0, rows, half:dims] = here_cos * start_cos + here_sin * start_sin
        return carry

    lax.fori_loop(0, tiles, marks, 0)

    def lowest(pair, carry):
        within = lax.rem(iota((8, groups * QRY), 1), QRY)
        first = base + pair * QRY - SEG
        place = within + (base + pair * QRY)
        for b in range(batch):
            low = jnp.where(within >= SEG, SEG, 0)
            for e in range(episodes):
                low = jnp.where(place >= ends[b][e], jnp.maximum(low, ends[b][e] - first), low)
            lows[b * pairs + pair] = jnp.maximum(low, -first)
        return carry

    lax.fori_loop(0, pairs, lowest, 0)

    def chunk_rows(c):
        return pl.ds(pl.multiple_of(c * ROWS, ROWS), ROWS)

    def kv_rows(c):
        return pl.ds(pl.multiple_of(lax.rem(c, per_seq) * ROWS + SEG, 16), ROWS)

    loads[0].wait()
    tb[0:vocab_all, :] = table_f[...].astype(BF)

    def onehot(c):
        code = toki[c, 0:1, :]
        act = toki[c, 1:2, :] + VOCAB
        ids = iota((OUTS, ROWS), 0)
        return jnp.where((ids == code) | (ids == act), 1.0, 0.0).astype(BF)

    def embed(c, carry):
        rows = chunk_rows(c)
        xs[0, rows, :] += dot_tn(onehot(c), tb[...])
        return carry

    lax.fori_loop(0, chunks, embed, 0)

    lane_head = iota((1, dims), 1) // head_dim
    group_mask = [jnp.where(lane_head // 2 == g, 1.0, 0.0).astype(BF) for g in range(groups)]
    even_mask = jnp.where(lax.rem(lane_head, 2) == 0, 1.0, 0.0).astype(BF)
    odd_mask = jnp.where(lax.rem(lane_head, 2) == 1, 1.0, 0.0).astype(BF)
    even_f = lax.rem(lane_head, 2) == 0

    def by_group(rows):
        return jnp.concatenate([rows * group_mask[g] for g in range(groups)], axis=0)

    def both(keys):
        return jnp.concatenate([keys * even_mask, keys * odd_mask], axis=0)

    def gather_heads(wide):
        out = wide[0:QRY]
        for g in range(1, groups):
            out = jnp.where(lane_head // 2 == g, wide[g * QRY : g * QRY + QRY], out)
        return out

    def forward_copy(layer):
        return pltpu.make_async_remote_copy(
            src_ref=kvs.at[layer, :, pl.ds(span, SEG), :],
            dst_ref=kvs.at[layer, :, pl.ds(0, SEG), :],
            send_sem=send_sem.at[layer],
            recv_sem=recv_sem.at[layer],
            device_id={"seq": right},
            device_id_type=MESH,
        )

    def backward_copy(layer):
        return pltpu.make_async_remote_copy(
            src_ref=bsend.at[layer],
            dst_ref=brecv.at[layer],
            send_sem=send_sem.at[layers + layer],
            recv_sem=recv_sem.at[layers + layer],
            device_id={"seq": left},
            device_id_type=MESH,
        )

    def project(layer):
        def body(c, carry):
            rows = chunk_rows(c)
            h = rms_apply(xs[2 * layer, rows, :], gains_ref[2 * layer : 2 * layer + 1, :])
            hs[2 * layer, rows, :] = h
            qkv = dot_nn(h, wq[layer]).astype(BF)
            qs[layer, rows, :] = qkv[:, 0:dims]
            kvs[layer, c // per_seq, kv_rows(c), :] = qkv[:, dims:]
            return carry

        lax.fori_loop(0, chunks, body, 0)

    def pair_rows(b, pair):
        return pl.ds(pl.multiple_of(b * span + pair * QRY, 16), QRY)

    def pair_window(pair):
        return pl.ds(pl.multiple_of(pair * QRY, 16), KEY)

    causal = iota((KEY, groups * QRY), 0) <= lax.rem(iota((KEY, groups * QRY), 1), QRY) + SEG
    key_place = iota((KEY, groups * QRY), 0)

    def attend(layer):
        def one(b, pair):
            rows, window = pair_rows(b, pair), pair_window(pair)
            keys = kvs[layer, b, window, 0:dims]
            values = kvs[layer, b, window, dims:]
            seen = causal & (key_place >= lows[b * pairs + pair, 0:1, :])
            scores = dot_nt(both(keys), by_group(qs[layer, rows, :]))
            sides = []
            for side in range(2):
                s = jnp.where(seen, scores[side * KEY : side * KEY + KEY], NEG)
                top = jnp.max(s, axis=0, keepdims=True)
                e = jnp.exp2((s - top) * exp_scale)
                sides.append((e * (1.0 / jnp.sum(e, axis=0, keepdims=True))).astype(BF))
            p = jnp.concatenate(sides, axis=0)
            probs[layer, b * pairs + pair] = p
            wide = dot_tn(p, both(values))
            mixes[layer, rows, :] = gather_heads(wide).astype(BF)

        def body(i, carry):
            for b in range(batch):
                one(b, pairs - 1 - i)
            return carry

        copy = forward_copy(layer)
        copy.start()
        lax.fori_loop(0, pairs - 1, body, 0)
        copy.wait()
        lax.fori_loop(pairs - 1, pairs, body, 0)

    def feed(layer):
        def body(c, carry):
            rows = chunk_rows(c)
            x = xs[2 * layer, rows, :] + dot_nn(mixes[layer, rows, :], wo[layer])
            xs[2 * layer + 1, rows, :] = x
            h = rms_apply(x, gains_ref[2 * layer + 1 : 2 * layer + 2, :])
            hs[2 * layer + 1, rows, :] = h
            for j in range(ff // 256):
                cols = slice(j * 256, j * 256 + 256)
                up = dot_nn(h, wu[layer, :, cols])
                square = up * up
                c0 = math.sqrt(2.0 / math.pi)
                t = jnp.tanh(c0 * up * (1.0 + 0.044715 * square))
                half_t = 0.5 * (1.0 + t)
                acts[layer, rows, cols] = (up * half_t).astype(BF)
                slope = half_t + (0.5 * c0) * up * (1.0 - t * t) * (1.0 + (3.0 * 0.044715) * square)
                gds[layer, rows, cols] = slope.astype(BF)
            xs[2 * layer + 2, rows, :] = x + dot_nn(acts[layer, rows, :], wd[layer])
            return carry

        lax.fori_loop(0, chunks, body, 0)

    per_layer = 4 + 2 * (ff // 256)
    for layer in range(layers):
        if layer == 0:
            convert(0, 3)
        project(layer)
        if layer == 0:
            ex.greeted()
        attend(layer)
        if layer == 0:
            convert(3, layers * per_layer)
        feed(layer)
    loads[1].wait()
    rt[0:outs_all, :] = readout_f[...].astype(BF)

    lossacc[...] = jnp.zeros_like(lossacc)
    dgain[...] = jnp.zeros_like(dgain)
    top_gain = gains_ref[2 * layers : 2 * layers + 1, :]

    def put(at, block):
        for side in range(2):
            cols = slice(side * 128, side * 128 + 128)
            grads_ref[side, at : at + block.shape[0], :] = block[:, cols].astype(BF)

    def losses(c, carry):
        rows = chunk_rows(c)
        x = xs[2 * layers, rows, :]
        h = rms_apply(x, top_gain)
        hs[2 * layers, rows, :] = h
        outs = dot_nt(rt[...], h)
        reward, cont = tokf[c, 0:1, :], tokf[c, 1:2, :]
        target, ret, valid = tokf[c, 2:3, :], tokf[c, 3:4, :], tokf[c, 4:5, :]
        action, code = toki[c, 1:2, :], toki[c, 2:3, :]
        logits = outs[0:VOCAB]
        top = jnp.max(logits, axis=0, keepdims=True)
        e = jnp.exp(logits - top)
        esum = jnp.sum(e, axis=0, keepdims=True)
        chosen = iota((VOCAB, ROWS), 0) == code
        picked = jnp.sum(jnp.where(chosen, logits, 0.0), axis=0, keepdims=True)
        loss = jnp.log(esum) + top - picked
        gouts[0:VOCAB, rows] = (e * (valid / esum) - jnp.where(chosen, valid, 0.0)).astype(BF)
        small = outs[VOCAB:OUTS]
        place = iota((OUTS - VOCAB, ROWS), 0)
        reward_err = small[0:1] - reward
        end_logit = small[1:2]
        value_err = small[2:3] - ret
        minus = jnp.exp(-jnp.abs(end_logit))
        soft = jnp.maximum(end_logit, 0.0) + jnp.log(1.0 + minus)
        sigmoid = jnp.where(end_logit >= 0.0, 1.0, minus) / (1.0 + minus)
        loss = loss + 0.5 * reward_err * reward_err + soft - cont * end_logit
        loss = loss + 0.5 * value_err * value_err
        actor = (place >= 3) & (place < outs_all - VOCAB)
        act_top = jnp.max(jnp.where(actor, small, NEG), axis=0, keepdims=True)
        act_e = jnp.where(actor, jnp.exp(jnp.where(actor, small - act_top, 0.0)), 0.0)
        act_sum = jnp.sum(act_e, axis=0, keepdims=True)
        log_pi = jnp.where(actor, small - act_top - jnp.log(act_sum), 0.0)
        pi = act_e / act_sum
        neg_entropy = jnp.sum(pi * log_pi, axis=0, keepdims=True)
        taken = place == action + 3
        picked_pi = jnp.sum(jnp.where(taken, log_pi, 0.0), axis=0, keepdims=True)
        gap = ret - target
        loss = loss - gap * picked_pi + ENTROPY_COEF * neg_entropy
        grad = gap * (pi - jnp.where(taken, 1.0, 0.0))
        grad = grad + ENTROPY_COEF * pi * (log_pi - neg_entropy)
        grad = jnp.where(actor, grad, 0.0)
        grad = jnp.where(place == 0, reward_err, grad)
        grad = jnp.where(place == 1, sigmoid - cont, grad)
        grad = jnp.where(place == 2, value_err, grad)
        gouts[VOCAB:OUTS, rows] = (grad * valid).astype(BF)
        lossacc[0:1, :] += loss * valid
        lossacc[1:2, :] += valid
        dh = dot_tn(gouts[:, rows], rt[...])
        grad_x, part = rms_pull(dh, x, top_gain)
        gx[rows, :] = grad_x
        gl[rows, :] = grad_x.astype(BF)
        dgain[2 * layers] += part
        return carry

    lax.fori_loop(0, chunks, losses, 0)
    tail_at = VOCAB + layers * 12 * 256 + OUTS
    put(0, dot_nn(gouts[0:VOCAB, :], hs[2 * layers]))
    put(tail_at, dot_nn(gouts[VOCAB:OUTS, :], hs[2 * layers]))
    loss_total = jnp.sum(lossacc[0:1, :])
    count_total = jnp.sum(lossacc[1:2, :])
    place = iota(scal_ref.shape, 0)
    ex.tile_out[0, 0] = jnp.where(place == 0, loss_total, jnp.where(place == 1, count_total, 0.0))
    ex.begin(len(buckets))

    def spread(low, high, parts, spent, body):
        for part in range(parts):
            first = low + (high - low) * part // parts
            lax.fori_loop(first, low + (high - low) * (part + 1) // parts, body, 0)
            ex.tick(spent / parts)

    def feed_back(layer):
        def body(c, carry):
            rows = chunk_rows(c)
            low = gl[rows, :]
            for j in range(ff // 256):
                cols = slice(j * 256, j * 256 + 256)
                da = dot_nt(low, wd[layer, cols, :])
                gds[layer, rows, cols] = (da * gds[layer, rows, cols].astype(F32)).astype(BF)
            dh = dot_nt(gds[layer, rows, :], wu[layer])
            gain = gains_ref[2 * layer + 1 : 2 * layer + 2, :]
            grad_x, part = rms_pull(dh, xs[2 * layer + 1, rows, :], gain)
            dgain[2 * layer + 1] += part
            grad = gx[rows, :] + grad_x
            gx[rows, :] = grad
            low = grad.astype(BF)
            gl[rows, :] = low
            dmix[rows, :] = dot_nt(low, wo[layer]).astype(BF)
            return carry

        spread(0, chunks, 3, 5.0, body)

    def attend_back(layer):
        def one(b, pair):
            rows, window = pair_rows(b, pair), pair_window(pair)
            keys = both(kvs[layer, b, window, 0:dims])
            values = both(kvs[layer, b, window, dims:])
            queries = by_group(qs[layer, rows, :])
            dout = by_group(dmix[rows, :])
            p = probs[layer, b * pairs + pair]
            dp = dot_nt(values, dout)
            sides = []
            for side in range(2):
                part = slice(side * KEY, side * KEY + KEY)
                pf = p[part].astype(F32)
                d = dp[part]
                sides.append((pf * (d - jnp.sum(d * pf, axis=0, keepdims=True))).astype(BF))
            ds = jnp.concatenate(sides, axis=0)
            dq = gather_heads(dot_tn(ds, keys)) * scale
            dqkv[rows, 0:dims] = dq.astype(BF)
            dk = dot_nn(ds, queries) * scale
            dk = jnp.where(even_f, dk[0:KEY], dk[KEY:])
            dv = dot_nn(p, dout)
            dv = jnp.where(even_f, dv[0:KEY], dv[KEY:])
            both_kv = jnp.concatenate([dk, dv], axis=1)
            old = carried[b] + both_kv[0:SEG]
            carried[b] = both_kv[QRY:]
            here = pl.ds(pl.multiple_of(b * span + pair * QRY, 16), SEG)
            dqkv[here, dims:] = both_kv[SEG:QRY].astype(BF)
            return old.astype(BF)

        def body(pair, carry):
            for b in range(batch):
                old = one(b, pair)
                before = pl.ds(pl.multiple_of(b * span + pair * QRY - SEG, 16), SEG)
                dqkv[before, dims:] = old
            return carry

        carried[...] = jnp.zeros_like(carried)
        for b in range(batch):
            bsend[layer, b] = one(b, 0)
        copy = backward_copy(layer)
        copy.start()
        ex.tick(1.1)
        spread(1, pairs, 4, 7.6, body)
        copy.wait()
        for b in range(batch):
            final = carried[b] + brecv[layer, b].astype(F32)
            dqkv[b * span + span - SEG : b * span + span, dims:] = final.astype(BF)

    def project_back(layer):
        def body(c, carry):
            rows = chunk_rows(c)
            dh = dot_nt(dqkv[rows, :], wq[layer])
            gain = gains_ref[2 * layer : 2 * layer + 1, :]
            grad_x, part = rms_pull(dh, xs[2 * layer, rows, :], gain)
            dgain[2 * layer] += part
            grad = gx[rows, :] + grad_x
            gx[rows, :] = grad
            gl[rows, :] = grad.astype(BF)
            return carry

        spread(0, chunks, 2, 2.1, body)

    at = VOCAB
    bucket = 0
    for layer in reversed(range(layers)):
        for j in range(ff // 256):
            cols = slice(j * 256, j * 256 + 256)
            put(at, dot_tn(acts[layer, :, cols], gl[...]))
            at += 256
        ex.begin(bucket)
        ex.tick(1.4)
        feed_back(layer)
        for j in range(ff // 256):
            cols = slice(j * 256, j * 256 + 256)
            put(at, dot_tn(hs[2 * layer + 1], gds[layer, :, cols]))
            at += 256
            if j % 2:
                ex.tick(0.7)
        put(at, dot_tn(mixes[layer], gl[...]))
        at += 256
        ex.begin(bucket + 1)
        ex.tick(0.4)
        attend_back(layer)
        for j in range(3):
            cols = slice(j * 256, j * 256 + 256)
            put(at, dot_tn(hs[2 * layer], dqkv[:, cols]))
            at += 256
        bucket += 2
        if layer == 0:
            ex.begin(bucket)
        ex.tick(1.0)
        project_back(layer)

    def mark(c, carry):
        gouts[:, chunk_rows(c)] = onehot(c)
        return carry

    lax.fori_loop(0, chunks, mark, 0)
    put(at, dot_nn(gouts[...], gl[...]))
    ex.tick(1.4)
    at = tail_at + OUTS - VOCAB
    place = iota((16, dims), 0)
    gain_rows = jnp.zeros((16, dims), F32)
    for index in range(2 * layers + 1):
        gain_rows = jnp.where(place == index, jnp.sum(dgain[index], axis=0, keepdims=True), gain_rows)
    put(at, gain_rows)
    at += 16
    put(at, jnp.zeros((grads_ref.shape[1] - at, dims), F32))
    ex.begin(len(buckets) - 1)
    ex.drain()
    count = ex.tile_out[0, 3, 1:2, 0:1]
    norm = jnp.sqrt(jnp.sum(ex.tile_out[1, 3]) / (count * count))
    place = iota(scal_ref.shape, 0)
    scal = jnp.where(place == 2, norm, ex.tile_out[0, 3])
    scal_ref[...] = jnp.where(place == 3, jnp.minimum(1.0, CLIP_NORM / norm) / count, scal)
    for n in range(len(buckets)):
        ex.wait(ex.out_copies(n))


def gradients(codes, actions, next_codes, lengths, rewards, continues, values, weights, sizes):
    table, attn_in, attn_out, ffn_in, ffn_out, gains, readout = weights
    batch, span = codes.shape
    layers, dims, ff = ffn_in.shape
    total = batch * span
    tiles = span // SEG
    chunks = total // ROWS
    grad_rows = grad_row_count(layers)
    buckets = buckets_of(layers)
    seq_size, dp_size = sizes
    owners = min(4, dp_size // 2)
    slots = exchange_slots(dp_size)
    hbm = pl.BlockSpec(memory_space=pltpu.HBM)
    steps = np.arange(lax.axis_size("seq") * tiles + 1, dtype=np.float64)[:, None]
    freq = np.exp(np.arange(dims // 2) * (-2.0 * math.log(10000.0) / dims))
    trig = np.zeros((steps.shape[0], 8, dims // 2), np.float32)
    trig[:, 0], trig[:, 1] = np.sin(steps * SEG * freq), np.cos(steps * SEG * freq)
    trig[:, 2], trig[:, 3] = np.sin(steps * freq), np.cos(steps * freq)
    trig = jnp.asarray(trig)
    vmem = pl.BlockSpec(memory_space=pltpu.VMEM)
    smem = pl.BlockSpec(memory_space=pltpu.SMEM)
    return pl.pallas_call(
        functools.partial(step_kernel, layers, sizes, buckets),
        out_shape=(
            jax.ShapeDtypeStruct((2, grad_rows, dims // 2), BF),
            jax.ShapeDtypeStruct((8, 128), F32),
        ),
        in_specs=[vmem] * 3 + [smem] + [vmem] * 4 + [hbm] * 5 + [vmem, hbm],
        out_specs=(hbm, vmem),
        scratch_shapes=[
            pltpu.VMEM((layers, dims, 3 * dims), BF),
            pltpu.VMEM((layers, dims, dims), BF),
            pltpu.VMEM((layers, dims, ff), BF),
            pltpu.VMEM((layers, ff, dims), BF),
            pltpu.VMEM((OUTS, dims), BF),
            pltpu.VMEM((OUTS, dims), BF),
            pltpu.VMEM((2 * layers + 1, total, dims), F32),
            pltpu.VMEM((2 * layers + 1, total, dims), BF),
            pltpu.VMEM((layers, total, dims), BF),
            pltpu.VMEM((layers, batch, SEG + span, 2 * dims), BF),
            pltpu.VMEM((layers, total // QRY, 2 * KEY, HEADS // 2 * QRY), BF),
            pltpu.VMEM((layers, total, ff), BF),
            pltpu.VMEM((layers, total, ff), BF),
            pltpu.VMEM((layers, total, dims), BF),
            pltpu.VMEM((total // QRY, 8, HEADS // 2 * QRY), jnp.int32),
            pltpu.VMEM((chunks, 8, ROWS), F32),
            pltpu.VMEM((chunks, 8, ROWS), jnp.int32),
            pltpu.VMEM((OUTS, total), BF),
            pltpu.VMEM((total, dims), F32),
            pltpu.VMEM((total, dims), BF),
            pltpu.VMEM((total, dims), BF),
            pltpu.VMEM((total, 3 * dims), BF),
            pltpu.VMEM((batch, SEG, 2 * dims), F32),
            pltpu.VMEM((2 * layers + 1, 8, dims), F32),
            pltpu.VMEM((8, ROWS), F32),
            pltpu.VMEM((4, 8, span), F32),
            pltpu.VMEM((layers, batch, SEG, 2 * dims), BF),
            pltpu.VMEM((layers, batch, SEG, 2 * dims), BF),
            pltpu.SemaphoreType.DMA((2 * layers,)),
            pltpu.SemaphoreType.DMA((2 * layers,)),
            pltpu.SemaphoreType.DMA((2 + 12 * layers,)),
            pltpu.VMEM(table.shape, F32),
            pltpu.VMEM(readout.shape, F32),
            pltpu.VMEM((2, grad_rows, dims // 2), BF),
            pltpu.VMEM((grad_rows, dims // 2), BF),
            pltpu.VMEM((2, grad_rows // seq_size, dims // 2), BF),
            pltpu.VMEM((grad_rows // seq_size, dims // 2), BF),
            pltpu.VMEM((grad_rows // seq_size, dims // 2), BF),
            pltpu.VMEM((dp_size // 2 - 1, grad_rows // (seq_size * owners), dims // 2), BF),
            pltpu.VMEM((8, dims // 2), F32),
            pltpu.VMEM((2, 4, 8, 128), F32),
            pltpu.VMEM((2, slots // 2, 8, 128), F32),
            pltpu.SemaphoreType.DMA((len(buckets) + 2, slots)),
            pltpu.SemaphoreType.DMA((len(buckets) + 2, slots)),
            pltpu.SemaphoreType.DMA((len(buckets), 2)),
        ],
        compiler_params=pltpu.CompilerParams(
            collective_id=0, has_side_effects=True, vmem_limit_bytes=63 * 1024 * 1024
        ),
        name="train_step",
    )(
        codes,
        actions,
        next_codes,
        lengths,
        rewards,
        continues,
        values,
        trig,
        table,
        attn_in,
        attn_out,
        ffn_in,
        ffn_out,
        gains,
        readout,
    )


def adam_update(weight, first_mom, second_mom, clipped, rate):
    new_first = BETA_ONE * first_mom + (1.0 - BETA_ONE) * clipped
    new_second = BETA_TWO * second_mom + (1.0 - BETA_TWO) * clipped * clipped
    ratio = (
        new_first
        / (1.0 - BETA_ONE**STEP)
        / (jnp.sqrt(new_second / (1.0 - BETA_TWO**STEP)) + ADAM_EPS)
    )
    return (weight - rate * (ratio + DECAY * weight), new_first, new_second)


def update_kernel(layers, scal_ref, sums_ref, *refs):
    ins, outs, here = refs[0:21], refs[21:42], refs[42:63]
    load_sem, store_sem, sum_sem, grads_ref = refs[63:]
    scale = scal_ref[3, 0]
    pieces = [(slot, layer) for slot in (4, 3, 1, 2) for layer in range(layers)]
    pieces += [(0, None), (6, None), (5, None)]

    def view(ref, layer):
        return ref if layer is None else ref.at[layer]

    def moves(n, kind):
        slot, layer = pieces[n]
        for part in range(3):
            index = 3 * slot + part
            inside = view(here[index], layer)
            if kind == 0:
                yield pltpu.make_async_copy(view(ins[index], layer), inside, load_sem.at[n, part])
            else:
                yield pltpu.make_async_copy(inside, view(outs[index], layer), store_sem.at[n, part])

    fetch = [
        pltpu.make_async_copy(sums_ref.at[side], grads_ref.at[side], sum_sem.at[side]) for side in range(2)
    ]
    for n in range(len(pieces)):
        if n == 1:
            for move in fetch:
                move.start()
        for move in moves(n, 0):
            move.start()

    def renew(slot, layer, rows, cols, grad):
        refs = [view(here[3 * slot + part], layer) for part in range(3)]
        new = adam_update(*[ref[rows, cols] for ref in refs], grad.astype(F32) * scale, RATES[slot])
        for ref, value in zip(refs, new):
            ref[rows, cols] = value

    offset = VOCAB
    starts = {}
    for layer in reversed(range(layers)):
        starts[4, layer] = offset
        starts[3, layer] = offset + 4 * 256
        starts[2, layer] = offset + 8 * 256
        starts[1, layer] = offset + 9 * 256
        offset += 12 * 256
    table_at, tail_at = offset, offset + OUTS
    gains_at = tail_at + OUTS - VOCAB

    for n, (slot, layer) in enumerate(pieces):
        for move in moves(n, 0):
            move.wait()
        if n == 0:
            for move in fetch:
                move.wait()
        if layer is not None:
            rows_all, cols_all = here[3 * slot].shape[1:]
            at = starts[slot, layer]
            for j in range(rows_all // 256):
                for i in range(cols_all // 256):
                    for side in range(2):
                        cols = slice(i * 256 + side * 128, i * 256 + side * 128 + 128)

                        def body(k, carry):
                            rows = pl.ds(pl.multiple_of(j * 256 + k * 64, 64), 64)
                            block = at + (j + i) * 256 + k * 64
                            grad = grads_ref[side, pl.ds(pl.multiple_of(block, 64), 64), :]
                            renew(slot, layer, rows, cols, grad)
                            return carry

                        lax.fori_loop(0, 4, body, 0)
        elif slot == 0:
            rows_all = here[0].shape[0]
            for side in range(2):
                cols = slice(side * 128, side * 128 + 128)

                def body(k, carry):
                    rows = pl.ds(pl.multiple_of(k * 64, 64), 64)
                    block = pl.ds(pl.multiple_of(table_at + k * 64, 64), 64)
                    renew(0, None, rows, cols, grads_ref[side, block, :])
                    return carry

                full = rows_all // 64
                lax.fori_loop(0, full, body, 0)
                if rows_all % 64:
                    last = slice(full * 64, rows_all)
                    block = grads_ref[side, table_at + full * 64 : table_at + full * 64 + 64, :]
                    renew(0, None, last, cols, block.astype(F32)[0 : rows_all % 64])
        elif slot == 6:
            outs_all = here[18].shape[0]
            for side in range(2):
                cols = slice(side * 128, side * 128 + 128)

                def body(k, carry):
                    rows = pl.ds(pl.multiple_of(k * 64, 64), 64)
                    renew(6, None, rows, cols, grads_ref[side, rows, :])
                    return carry

                lax.fori_loop(0, VOCAB // 64, body, 0)
                rest = grads_ref[side, tail_at : tail_at + OUTS - VOCAB, :].astype(F32)
                renew(6, None, slice(VOCAB, outs_all), cols, rest[0 : outs_all - VOCAB])
        else:
            count = here[15].shape[0]
            for side in range(2):
                cols = slice(side * 128, side * 128 + 128)
                grad = grads_ref[side, gains_at : gains_at + 16, :].astype(F32)[0:count]
                renew(5, None, slice(0, count), cols, grad)
        for move in moves(n, 1):
            move.start()
    for n in range(len(pieces)):
        for move in moves(n, 1):
            move.wait()


def update(grads, scal, state):
    layers = state[3].shape[0]
    anywhere = pl.BlockSpec(memory_space=pltpu.HBM)
    pieces = 4 * layers + 3
    return pl.pallas_call(
        functools.partial(update_kernel, layers),
        out_shape=tuple(jax.ShapeDtypeStruct(x.shape, F32) for x in state),
        in_specs=[
            pl.BlockSpec(memory_space=pltpu.SMEM),
            anywhere,
        ]
        + [anywhere] * 21,
        out_specs=(anywhere,) * 21,
        scratch_shapes=[pltpu.VMEM(x.shape, F32) for x in state]
        + [
            pltpu.SemaphoreType.DMA((pieces, 3)),
            pltpu.SemaphoreType.DMA((pieces, 3)),
            pltpu.SemaphoreType.DMA((2,)),
            pltpu.VMEM(grads.shape, BF),
        ],
        compiler_params=pltpu.CompilerParams(vmem_limit_bytes=62 * 1024 * 1024),
        name="update",
    )(scal, grads, *state)


def local(codes, actions, next_codes, lengths, rewards, continues, target_values, *state):
    state = state[0:18] + tuple(value.T for value in state[18:21])
    params = state[0::3]
    seq_size, dp_size = lax.axis_size("seq"), lax.axis_size("dp")
    sizes = (seq_size, dp_size)
    grads, scal = gradients(
        codes, actions, next_codes, lengths, rewards, continues, target_values, params, sizes
    )
    results = list(update(grads, scal, state))
    results[18:21] = [value.T for value in results[18:21]]
    return tuple(results) + (scal[0, 0], scal[1, 0], scal[2, 0])


def solution(mesh):
    rows, whole = P("dp", "seq"), P()
    return jax.shard_map(
        local,
        mesh=mesh,
        in_specs=(rows, rows, rows, P("dp", None), rows, rows, rows) + (whole,) * 21,
        out_specs=(whole,) * 24,
        check_vma=False,
    )
```

```python
import functools
import math

import jax
import jax.numpy as jnp
import numpy as np
from jax import lax
from jax.experimental import pallas as pl
from jax.experimental.pallas import tpu as pltpu
from jax.sharding import PartitionSpec as P

HEADS = 8
VOCAB = 512
SEG = 48
STEP = 5

EPS_NORM = 1e-06
BETA_ONE = 0.9
BETA_TWO = 0.999
RATES = (0.25, 0.02, 0.08, 0.02, 0.02, 0.25, 0.02)
DECAY = 0.01
ADAM_EPS = 1e-08
CLIP_NORM = 0.05
GAMMA = 0.985
LAMBDA_RET = 0.95
ENTROPY_COEF = 0.05

BF = jnp.bfloat16
F32 = jnp.float32
ROWS = 256
QRY = 2 * SEG
KEY = 3 * SEG
OUTS = 544
NEG = -1e30
MESH = pl.DeviceIdType.MESH
PER_ROW = 256 / 92e3
TRANSFERS = {
    "core": ("core", PER_ROW / 5.4, 1.1),
    "seq": ("seq", PER_ROW, 3.3),
    "deep": ("deep", PER_ROW / 2, 3.5),
    "tile": ("tile", 0.0, 3.6),
}
PATH = ("core", "seq", "deep", "back_deep", "back_seq", "back_core")
STAGE_TIME = 0.35


def dot_nn(left, right):
    return jnp.dot(left, right, preferred_element_type=F32)


def dot_tn(left, right):
    return lax.dot_general(left, right, (((0,), (0,)), ((), ())), preferred_element_type=F32)


def dot_nt(left, right):
    return lax.dot_general(left, right, (((1,), (1,)), ((), ())), preferred_element_type=F32)


def iota(shape, dim):
    return lax.broadcasted_iota(jnp.int32, shape, dim)


def rms_apply(x, gain):
    inv = lax.rsqrt(jnp.mean(x * x, axis=-1, keepdims=True) + EPS_NORM)
    return (x * inv * gain).astype(BF)


def rms_pull(grad, x, gain):
    inv = lax.rsqrt(jnp.mean(x * x, axis=-1, keepdims=True) + EPS_NORM)
    unit = x * inv
    weighted = grad * gain
    grad_x = inv * (weighted - unit * jnp.mean(weighted * unit, axis=-1, keepdims=True))
    rows, dims = x.shape
    return grad_x, jnp.sum((grad * unit).reshape(rows // 8, 8, dims), axis=0)


def grad_row_count(layers):
    rows = VOCAB + layers * 12 * 256 + OUTS + (OUTS - VOCAB) + 16
    return -(-rows // 256) * 256


def buckets_of(layers):
    cuts = [0, VOCAB + 4 * 256]
    for layer in range(layers):
        cuts.append(cuts[-1] + 5 * 256)
        cuts.append(cuts[-1] + (3 if layer == layers - 1 else 7) * 256)
    cuts.append(grad_row_count(layers))
    return list(zip(cuts[:-1], cuts[1:]))


def owners_of(bucket, seq_size, deep):
    quarter = (bucket[1] - bucket[0]) // seq_size
    return max(k for k in range(1, deep + 1) if quarter % (16 * k) == 0)


class Exchange:
    def __init__(self, seq_size, dp_size, buckets, grads, out, core_in, seq_in, seq_out, deep_in,
                 squares, tile_out, tile_in, send_sem, recv_sem, out_sem):
        self.deep = dp_size // 2
        self.seq_size = seq_size
        self.buckets = buckets
        self.grads, self.out = grads, out
        self.core_in, self.seq_in, self.seq_out, self.deep_in = core_in, seq_in, seq_out, deep_in
        self.squares = squares
        self.tile_out, self.tile_in = tile_out, tile_in
        self.send_sem, self.recv_sem, self.out_sem = send_sem, recv_sem, out_sem
        self.slots = exchange_slots(dp_size)
        me = lax.axis_index("seq")
        at_dp = lax.axis_index("dp")
        self.me, self.core, self.at_deep = me, lax.rem(at_dp, 2), lax.div(at_dp, 2)
        self.sibling = {"dp": self.at_deep * 2 + 1 - self.core}
        self.stage, self.due, self.free, self.now, self.summed = {}, {}, {}, 0.0, 0

    def deep_peer(self, k):
        return {"dp": lax.rem(self.at_deep + k, self.deep) * 2 + self.core}

    def peers(self):
        found = [self.sibling]
        found += [{"seq": lax.rem(self.me + k, self.seq_size)} for k in range(1, self.seq_size)]
        return found + [self.deep_peer(k) for k in range(1, self.deep)]

    def greet(self):
        for peer in self.peers():
            pl.semaphore_signal(
                pltpu.get_barrier_semaphore(), inc=1, device_id=peer, device_id_type=MESH
            )

    def greeted(self):
        pl.semaphore_wait(pltpu.get_barrier_semaphore(), len(self.peers()))

    def copy(self, src, dst, n, slot, peer):
        return pltpu.make_async_remote_copy(
            src_ref=src,
            dst_ref=dst,
            send_sem=self.send_sem.at[n, slot],
            recv_sem=self.recv_sem.at[n, slot],
            device_id=peer,
            device_id_type=MESH,
        )

    def only(self, n, index, act):
        owners = owners_of(self.buckets[n], self.seq_size, self.deep)
        if owners == self.deep:
            act()
        else:
            pl.when(index < owners)(act)

    def parts(self, n):
        r0, r1 = self.buckets[n]
        quarter = (r1 - r0) // self.seq_size
        return r0, r1 - r0, quarter, quarter // owners_of(self.buckets[n], self.seq_size, self.deep)

    def place(self, n, index):
        return lax.rem(index, owners_of(self.buckets[n], self.seq_size, self.deep))

    def deep_rows(self, n):
        at = sum(self.parts(k)[3] for k in range(n))
        return pl.ds(at, self.parts(n)[3])

    def quarter_rows(self, n, index):
        r0, _, quarter, _ = self.parts(n)
        return pl.ds(pl.multiple_of(r0 + index * quarter, 16), quarter)

    def packed_rows(self, n):
        r0, _, quarter, _ = self.parts(n)
        return pl.ds(r0 // self.seq_size, quarter)

    def share_rows(self, n, index):
        r0, _, _, share = self.parts(n)
        return pl.ds(pl.multiple_of(r0 // self.seq_size + index * share, 16), share)

    def own_rows(self, n):
        r0, _, quarter, share = self.parts(n)
        at = r0 + self.me * quarter + self.place(n, self.at_deep) * share
        return pl.ds(pl.multiple_of(at, 16), share)

    def blocks(self, n, index, work):
        r0, _, quarter, _ = self.parts(n)
        size = quarter // 2 if quarter > 256 else quarter
        for at in range(0, quarter, size):
            wide = pl.ds(pl.multiple_of(r0 + index * quarter + at, 16), size)
            work(wide, pl.ds(r0 // self.seq_size + at, size))

    def core_copies(self, n):
        r0, rows, _, _ = self.parts(n)
        part = pl.ds(r0, rows)
        return [self.copy(self.grads.at[1 - self.core, part], self.core_in.at[part], n, 0, self.sibling)]

    def seq_copies(self, n):
        packed = self.packed_rows(n)
        found = []
        for k in range(1, self.seq_size):
            peer = lax.rem(self.me + k, self.seq_size)
            source = self.core_in.at[self.quarter_rows(n, peer)]
            found.append(self.copy(source, self.seq_in.at[k - 1, packed], n, k, {"seq": peer}))
        return found

    def deep_copy(self, n, k):
        target = self.place(n, lax.rem(self.at_deep + k, self.deep))
        dest = self.deep_in.at[k - 1, self.deep_rows(n)]
        return self.copy(self.seq_out.at[self.share_rows(n, target)], dest, n, 3 + k, self.deep_peer(k))

    def back_copy(self, n, rows, slot, peer):
        there = self.grads.at[self.core, rows]
        return self.copy(there, there, n, self.slots // 2 + slot, peer)

    def back_seq(self, n):
        rows = self.quarter_rows(n, self.me)
        return [
            self.back_copy(n, rows, k, {"seq": lax.rem(self.me + k, self.seq_size)})
            for k in range(1, self.seq_size)
        ]

    def back_core(self, n):
        r0, rows, _, _ = self.parts(n)
        return [self.back_copy(n, pl.ds(r0, rows), 0, self.sibling)]

    def out_copies(self, n):
        r0, rows, _, _ = self.parts(n)
        part = pl.ds(r0, rows)
        return [
            pltpu.make_async_copy(self.grads.at[side, part], self.out.at[side, part], self.out_sem.at[n, side])
            for side in range(2)
        ]

    def start(self, copies):
        for copy in copies:
            copy.start()

    def wait(self, copies):
        for copy in copies:
            copy.wait()

    def own_sum(self, wide, packed):
        both = self.grads[self.core, wide, :].astype(F32) + self.core_in[wide, :].astype(F32)
        for k in range(self.seq_size - 1):
            both = both + self.seq_in[k, packed, :].astype(F32)
        return both

    def after_core(self, n):
        def work(wide, packed):
            both = self.grads[self.core, wide, :].astype(F32) + self.core_in[wide, :].astype(F32)
            self.core_in[wide, :] = both.astype(BF)

        for k in range(1, self.seq_size):
            self.blocks(n, lax.rem(self.me + k, self.seq_size), work)

    def after_seq(self, n):
        def work(wide, packed):
            self.seq_out[packed, :] = self.own_sum(wide, packed).astype(BF)

        self.blocks(n, self.me, work)

    def after_deep(self, n):
        share = self.parts(n)[3]

        def act():
            rows = self.own_rows(n)
            both = self.own_sum(rows, self.share_rows(n, self.place(n, self.at_deep)))
            part = self.deep_rows(n)
            for k in range(self.deep - 1):
                both = both + self.deep_in[k, part, :].astype(F32)
            self.grads[self.core, rows, :] = both.astype(BF)
            self.squares[...] += jnp.sum((both * both).reshape(share // 8, 8, both.shape[1]), axis=0)

        self.only(n, self.at_deep, act)

    def begin_deep(self, n):
        for k in range(1, self.deep):
            target = lax.rem(self.at_deep + k, self.deep)
            self.only(n, target, self.deep_copy(n, k).start)

    def end_deep(self, n):
        for k in range(1, self.deep):
            target = lax.rem(self.at_deep + k, self.deep)
            self.only(n, target, self.deep_copy(n, k).wait_send)

        def act():
            for k in range(1, self.deep):
                self.deep_copy(n, k).wait_recv()

        self.only(n, self.at_deep, act)

    def begin_back_deep(self, n):
        rows = self.own_rows(n)

        def act():
            for k in range(1, self.deep):
                self.back_copy(n, rows, 3 + k, self.deep_peer(k)).start()

        self.only(n, self.at_deep, act)

    def end_back_deep(self, n):
        rows = self.own_rows(n)

        def act():
            for k in range(1, self.deep):
                self.back_copy(n, rows, 3 + k, self.deep_peer(k)).wait_send()

        self.only(n, self.at_deep, act)
        for k in range(1, self.deep):
            origin = lax.rem(self.at_deep + self.deep - k, self.deep)
            self.only(n, origin, self.back_copy(n, rows, 3 + k, self.deep_peer(k)).wait_recv)

    def begin_transfer(self, n, name):
        if name == "deep":
            self.begin_deep(n)
        elif name == "back_deep":
            self.begin_back_deep(n)
        else:
            self.start(getattr(self, name if "back" in name else name + "_copies")(n))

    def end_transfer(self, n, name):
        if name == "deep":
            self.end_deep(n)
        elif name == "back_deep":
            self.end_back_deep(n)
        else:
            self.wait(getattr(self, name if "back" in name else name + "_copies")(n))
        if name == "core":
            self.after_core(n)
        elif name == "seq":
            self.after_seq(n)
        elif name == "deep":
            self.after_deep(n)
        elif name == "back_core":
            self.start(self.out_copies(n))

    def launch(self, n):
        step = self.stage[n]
        if n < len(self.buckets):
            name, rows = PATH[step], self.buckets[n][1] - self.buckets[n][0]
            self.begin_transfer(n, name)
        else:
            name, rows = "tile", 0
            self.tile_start(n - len(self.buckets), step)
        link, share, latency = TRANSFERS[name.replace("back_", "")]
        self.free[link] = max(self.now, self.free.get(link, 0.0)) + rows * share
        self.due[n] = self.free[link] + latency

    def begin(self, n):
        self.stage[n] = 0
        self.launch(n)

    def advance(self, n):
        step = self.stage[n]
        self.now = max(self.now, self.due.pop(n)) + STAGE_TIME
        self.stage[n] += 1
        if n < len(self.buckets):
            self.end_transfer(n, PATH[step])
            self.summed += PATH[step] == "deep"
            more = step + 1 < len(PATH)
        else:
            self.tile_finish(n - len(self.buckets), step)
            more = step < 2
        if more:
            self.launch(n)
        norm = len(self.buckets) + 1
        if self.summed == len(self.buckets) and norm not in self.stage:
            self.tile_out[1, 0] = self.squares[...]
            self.begin(norm)

    def tick(self, spent):
        self.now += spent
        for n in sorted(self.due):
            if self.due[n] + 0.3 <= self.now:
                self.advance(n)

    def drain(self):
        while self.due:
            self.advance(min(self.due, key=lambda n: (self.due[n], n)))

    def tile_copies(self, tile, phase):
        if phase == 0:
            slots, peers = [0], [self.sibling]
        elif phase == 1:
            slots = list(range(1, self.seq_size))
            peers = [{"seq": lax.rem(self.me + k, self.seq_size)} for k in slots]
        else:
            slots = [3 + k for k in range(1, self.deep)]
            peers = [self.deep_peer(k) for k in range(1, self.deep)]
        n = len(self.buckets) + tile
        return [
            self.copy(self.tile_out.at[tile, phase], self.tile_in.at[tile, slot], n, slot, peer)
            for slot, peer in zip(slots, peers)
        ], slots

    def tile_start(self, tile, phase):
        self.start(self.tile_copies(tile, phase)[0])

    def tile_finish(self, tile, phase):
        copies, slots = self.tile_copies(tile, phase)
        self.wait(copies)
        both = self.tile_out[tile, phase]
        for slot in slots:
            both = both + self.tile_in[tile, slot]
        self.tile_out[tile, phase + 1] = both


def exchange_slots(dp_size):
    return 2 * (4 + dp_size // 2 - 1)


def step_kernel(
    layers,
    sizes,
    buckets,
    codes_ref,
    actions_ref,
    next_ref,
    lengths_ref,
    rewards_ref,
    continues_ref,
    values_ref,
    trig_ref,
    table_ref,
    attn_in_ref,
    attn_out_ref,
    ffn_in_ref,
    ffn_out_ref,
    gains_ref,
    readout_ref,
    out_ref,
    scal_ref,
    wq,
    wo,
    wu,
    wd,
    rt,
    tb,
    xs,
    hs,
    qs,
    kvs,
    probs,
    acts,
    gds,
    mixes,
    lows,
    tokf,
    toki,
    gouts,
    gx,
    gl,
    dmix,
    dqkv,
    carried,
    dgain,
    lossacc,
    lam,
    bsend,
    brecv,
    send_sem,
    recv_sem,
    load_sem,
    table_f,
    readout_f,
    grads_ref,
    *exchange_refs,
):
    batch, span = codes_ref.shape
    dims = gains_ref.shape[1]
    ff = ffn_in_ref.shape[2]
    tiles = span // SEG
    pairs = span // QRY
    total = batch * span
    chunks = total // ROWS
    per_seq = span // ROWS
    vocab_all = table_ref.shape[0]
    outs_all = readout_ref.shape[0]
    head_dim = dims // HEADS
    scale = head_dim ** (-0.5)
    exp_scale = scale * math.log2(math.e)
    groups = HEADS // 2
    base = lax.axis_index("seq") * span
    me = lax.axis_index("seq")
    seq_size = sizes[0]
    right = lax.rem(me + 1, seq_size)
    left = lax.rem(me + seq_size - 1, seq_size)

    ex = Exchange(*sizes, buckets, grads_ref, out_ref, *exchange_refs)
    ex.greet()
    ex.squares[...] = jnp.zeros_like(ex.squares)

    loads = [
        pltpu.make_async_copy(table_ref, table_f, load_sem.at[0]),
        pltpu.make_async_copy(readout_ref, readout_f, load_sem.at[1]),
    ]
    blocks = []
    for layer in range(layers):
        for j in range(3):
            blocks.append((attn_in_ref, wq, layer, slice(0, 256), slice(j * 256, j * 256 + 256)))
        blocks.append((attn_out_ref, wo, layer, slice(0, 256), slice(0, 256)))
        for j in range(ff // 256):
            blocks.append((ffn_in_ref, wu, layer, slice(0, 256), slice(j * 256, j * 256 + 256)))
        for j in range(ff // 256):
            blocks.append((ffn_out_ref, wd, layer, slice(j * 256, j * 256 + 256), slice(0, 256)))

    def place_of(k):
        at = (k + (2 * layers - 2) * chunks) % (2 * layers * chunks)
        return 1 + at // chunks, slice(256 * (at % chunks), 256 * (at % chunks) + 256)

    for k, (source, _, layer, rows, cols) in enumerate(blocks):
        plane, there = place_of(k)
        loads.append(
            pltpu.make_async_copy(source.at[layer, rows, cols], xs.at[plane, there, :], load_sem.at[2 + k])
        )
    for load in loads:
        load.start()

    def convert(low, high):
        for k in range(low, high):
            _, dest, layer, rows, cols = blocks[k]
            plane, there = place_of(k)
            loads[2 + k].wait()
            dest[layer, rows, cols] = xs[plane, there, :].astype(BF)

    tb[...] = jnp.zeros_like(tb)
    rt[...] = jnp.zeros_like(rt)

    ends = []
    for b in range(batch):
        run = jnp.int32(0)
        row = []
        for e in range(lengths_ref.shape[1]):
            run = run + lengths_ref[b, e]
            row.append(run)
        ends.append(row)
    episodes = len(ends[0])

    lane = iota((8, span), 1)
    lam[...] = jnp.zeros_like(lam)
    lam[0, 0:batch, :] = rewards_ref[...]
    lam[1, 0:batch, :] = continues_ref[...]
    lam[2, 0:batch, :] = values_ref[...]
    last = lax.rem(lane, SEG) == SEG - 1
    decay = GAMMA * lam[1]
    value_next = pltpu.roll(lam[2], span - 1, 1)
    add = jnp.where(last, lam[2], lam[0] + decay * ((1.0 - LAMBDA_RET) * value_next))
    mul = jnp.where(last, 0.0, decay * LAMBDA_RET)
    step = 1
    while step < SEG:
        add = add + mul * pltpu.roll(add, span - step, 1)
        mul = mul * pltpu.roll(mul, span - step, 1)
        step *= 2
    lam[3] = add
    valid_rows = []
    for b in range(batch):
        after = iota((1, span), 1) + (base + 1)
        final = after == ends[b][0]
        for e in range(1, episodes):
            final = final | (after == ends[b][e])
        valid_rows.append(jnp.where(final, 0.0, 1.0))
    for c in range(chunks):
        b = c // per_seq
        lanes = slice((c % per_seq) * ROWS, (c % per_seq) * ROWS + ROWS)
        for row in range(4):
            tokf[c, row : row + 1, :] = lam[row, b : b + 1, lanes]
        tokf[c, 4:5, :] = valid_rows[b][:, lanes]
        toki[c, 0:1, :] = codes_ref[b : b + 1, lanes]
        toki[c, 1:2, :] = actions_ref[b : b + 1, lanes]
        toki[c, 2:3, :] = next_ref[b : b + 1, lanes]

    half = dims // 2
    in_sin, in_cos = trig_ref[0:SEG, 2, :], trig_ref[0:SEG, 3, :]
    end_sin, end_cos = [], []
    for b in range(batch):
        for e in range(episodes):
            far, near = lax.div(ends[b][e], SEG), lax.rem(ends[b][e], SEG)
            far_sin, far_cos = trig_ref[far, 0:1, :], trig_ref[far, 1:2, :]
            near_sin, near_cos = trig_ref[near, 2:3, :], trig_ref[near, 3:4, :]
            end_sin.append(far_sin * near_cos + far_cos * near_sin)
            end_cos.append(far_cos * near_cos - far_sin * near_sin)

    def marks(tile, carry):
        at = me * tiles + tile
        tile_sin, tile_cos = trig_ref[at, 0:1, :], trig_ref[at, 1:2, :]
        here_sin = in_sin * tile_cos + in_cos * tile_sin
        here_cos = in_cos * tile_cos - in_sin * tile_sin
        place = iota((SEG, half), 0) + (base + tile * SEG)
        for b in range(batch):
            start_sin = jnp.zeros((SEG, half), F32)
            start_cos = jnp.ones((SEG, half), F32)
            for e in range(episodes):
                passed = place >= ends[b][e]
                row = b * episodes + e
                start_sin = jnp.where(passed, end_sin[row], start_sin)
                start_cos = jnp.where(passed, end_cos[row], start_cos)
            rows = pl.ds(pl.multiple_of(b * span + tile * SEG, SEG), SEG)
            xs[0, rows, 0:half] = here_sin * start_cos - here_cos * start_sin
            xs[0, rows, half:dims] = here_cos * start_cos + here_sin * start_sin
        return carry

    lax.fori_loop(0, tiles, marks, 0)

    def lowest(pair, carry):
        within = lax.rem(iota((8, groups * QRY), 1), QRY)
        first = base + pair * QRY - SEG
        place = within + (base + pair * QRY)
        for b in range(batch):
            low = jnp.where(within >= SEG, SEG, 0)
            for e in range(episodes):
                low = jnp.where(place >= ends[b][e], jnp.maximum(low, ends[b][e] - first), low)
            lows[b * pairs + pair] = jnp.maximum(low, -first)
        return carry

    lax.fori_loop(0, pairs, lowest, 0)

    def chunk_rows(c):
        return pl.ds(pl.multiple_of(c * ROWS, ROWS), ROWS)

    def kv_rows(c):
        return pl.ds(pl.multiple_of(lax.rem(c, per_seq) * ROWS + SEG, 16), ROWS)

    loads[0].wait()
    tb[0:vocab_all, :] = table_f[...].astype(BF)

    def onehot(c):
        code = toki[c, 0:1, :]
        act = toki[c, 1:2, :] + VOCAB
        ids = iota((OUTS, ROWS), 0)
        return jnp.where((ids == code) | (ids == act), 1.0, 0.0).astype(BF)

    def both_chunks(i):
        return (2 * i, 2 * i + 1)

    def embed(i, carry):
        for c in both_chunks(i):
            xs[0, chunk_rows(c), :] += dot_tn(onehot(c), tb[...])
        return carry

    lax.fori_loop(0, chunks // 2, embed, 0)

    lane_head = iota((1, dims), 1) // head_dim
    group_mask = [jnp.where(lane_head // 2 == g, 1.0, 0.0).astype(BF) for g in range(groups)]
    even_mask = jnp.where(lax.rem(lane_head, 2) == 0, 1.0, 0.0).astype(BF)
    odd_mask = jnp.where(lax.rem(lane_head, 2) == 1, 1.0, 0.0).astype(BF)
    even_f = lax.rem(lane_head, 2) == 0

    def by_group(rows):
        return jnp.concatenate([rows * group_mask[g] for g in range(groups)], axis=0)

    def both(keys):
        return jnp.concatenate([keys * even_mask, keys * odd_mask], axis=0)

    def gather_heads(wide):
        out = wide[0:QRY]
        for g in range(1, groups):
            out = jnp.where(lane_head // 2 == g, wide[g * QRY : g * QRY + QRY], out)
        return out

    def forward_copy(layer):
        return pltpu.make_async_remote_copy(
            src_ref=kvs.at[layer, :, pl.ds(span, SEG), :],
            dst_ref=kvs.at[layer, :, pl.ds(0, SEG), :],
            send_sem=send_sem.at[layer],
            recv_sem=recv_sem.at[layer],
            device_id={"seq": right},
            device_id_type=MESH,
        )

    def backward_copy(layer):
        return pltpu.make_async_remote_copy(
            src_ref=bsend.at[layer],
            dst_ref=brecv.at[layer],
            send_sem=send_sem.at[layers + layer],
            recv_sem=recv_sem.at[layers + layer],
            device_id={"seq": left},
            device_id_type=MESH,
        )

    def project(layer):
        gain = gains_ref[2 * layer : 2 * layer + 1, :]

        def body(i, carry):
            pieces = [(c, chunk_rows(c)) for c in both_chunks(i)]
            normed = [rms_apply(xs[2 * layer, rows, :], gain) for _, rows in pieces]
            wide = [dot_nn(h, wq[layer]).astype(BF) for h in normed]
            for (c, rows), h, qkv in zip(pieces, normed, wide):
                hs[2 * layer, rows, :] = h
                qs[layer, rows, :] = qkv[:, 0:dims]
                kvs[layer, c // per_seq, kv_rows(c), :] = qkv[:, dims:]
            return carry

        lax.fori_loop(0, chunks // 2, body, 0)

    def pair_rows(b, pair):
        return pl.ds(pl.multiple_of(b * span + pair * QRY, 16), QRY)

    def pair_window(pair):
        return pl.ds(pl.multiple_of(pair * QRY, 16), KEY)

    causal = iota((KEY, groups * QRY), 0) <= lax.rem(iota((KEY, groups * QRY), 1), QRY) + SEG
    key_place = iota((KEY, groups * QRY), 0)

    def attend(layer):
        def body(i, carry):
            items = [(b, pairs - 1 - 2 * i - j) for j in range(2) for b in range(batch)]
            scores = []
            for b, pair in items:
                keys = kvs[layer, b, pair_window(pair), 0:dims]
                scores.append(dot_nt(both(keys), by_group(qs[layer, pair_rows(b, pair), :])))
            weights = []
            for (b, pair), score in zip(items, scores):
                seen = causal & (key_place >= lows[b * pairs + pair, 0:1, :])
                sides = []
                for side in range(2):
                    s = jnp.where(seen, score[side * KEY : side * KEY + KEY], NEG)
                    top = jnp.max(s, axis=0, keepdims=True)
                    e = jnp.exp2((s - top) * exp_scale)
                    sides.append((e * (1.0 / jnp.sum(e, axis=0, keepdims=True))).astype(BF))
                p = jnp.concatenate(sides, axis=0)
                probs[layer, b * pairs + pair] = p
                weights.append(p)
            for (b, pair), p in zip(items, weights):
                values = kvs[layer, b, pair_window(pair), dims:]
                wide = dot_tn(p, both(values))
                mixes[layer, pair_rows(b, pair), :] = gather_heads(wide).astype(BF)
            return carry

        copy = forward_copy(layer)
        copy.start()
        lax.fori_loop(0, pairs // 2 - 1, body, 0)
        copy.wait()
        lax.fori_loop(pairs // 2 - 1, pairs // 2, body, 0)

    def feed(layer):
        gain = gains_ref[2 * layer + 1 : 2 * layer + 2, :]
        c0, c1 = math.sqrt(2.0 / math.pi), 0.044715

        def body(i, carry):
            pieces = [chunk_rows(c) for c in both_chunks(i)]
            mids = [xs[2 * layer, rows, :] + dot_nn(mixes[layer, rows, :], wo[layer]) for rows in pieces]
            normed = [rms_apply(x, gain) for x in mids]
            for rows, x, h in zip(pieces, mids, normed):
                xs[2 * layer + 1, rows, :] = x
                hs[2 * layer + 1, rows, :] = h
            hidden = [[], []]
            for j in range(ff // 256):
                cols = slice(j * 256, j * 256 + 256)
                for rows, h, parts in zip(pieces, normed, hidden):
                    up = dot_nn(h, wu[layer, :, cols])
                    square = up * up
                    half_t = 0.5 + 0.5 * jnp.tanh(up * (c0 + (c0 * c1) * square))
                    act = up * half_t
                    slope = half_t + (1.0 - half_t) * act * (2.0 * c0 + (6.0 * c0 * c1) * square)
                    parts.append(act.astype(BF))
                    gds[layer, rows, cols] = slope.astype(BF)
            for rows, x, parts in zip(pieces, mids, hidden):
                act = jnp.concatenate(parts, axis=1)
                acts[layer, rows, :] = act
                xs[2 * layer + 2, rows, :] = x + dot_nn(act, wd[layer])
            return carry

        lax.fori_loop(0, chunks // 2, body, 0)

    per_layer = 4 + 2 * (ff // 256)
    for layer in range(layers):
        if layer == 0:
            convert(0, 3)
        project(layer)
        if layer == 0:
            ex.greeted()
        attend(layer)
        if layer == 0:
            convert(3, layers * per_layer)
        feed(layer)
    loads[1].wait()
    rt[0:outs_all, :] = readout_f[...].astype(BF)

    lossacc[...] = jnp.zeros_like(lossacc)
    dgain[...] = jnp.zeros_like(dgain)
    top_gain = gains_ref[2 * layers : 2 * layers + 1, :]

    def put(at, block):
        for side in range(2):
            cols = slice(side * 128, side * 128 + 128)
            grads_ref[side, at : at + block.shape[0], :] = block[:, cols].astype(BF)

    def loss_grad(c, outs):
        reward, cont = tokf[c, 0:1, :], tokf[c, 1:2, :]
        target, ret, valid = tokf[c, 2:3, :], tokf[c, 3:4, :], tokf[c, 4:5, :]
        action, code = toki[c, 1:2, :], toki[c, 2:3, :]
        logits = outs[0:VOCAB]
        top = jnp.max(logits, axis=0, keepdims=True)
        e = jnp.exp(logits - top)
        esum = jnp.sum(e, axis=0, keepdims=True)
        chosen = iota((VOCAB, ROWS), 0) == code
        picked = jnp.sum(jnp.where(chosen, logits, 0.0), axis=0, keepdims=True)
        loss = jnp.log(esum) + top - picked
        grad_logits = (e * (valid / esum) - jnp.where(chosen, valid, 0.0)).astype(BF)
        small = outs[VOCAB:OUTS]
        place = iota((OUTS - VOCAB, ROWS), 0)
        reward_err = small[0:1] - reward
        end_logit = small[1:2]
        value_err = small[2:3] - ret
        minus = jnp.exp(-jnp.abs(end_logit))
        soft = jnp.maximum(end_logit, 0.0) + jnp.log(1.0 + minus)
        sigmoid = jnp.where(end_logit >= 0.0, 1.0, minus) / (1.0 + minus)
        loss = loss + 0.5 * reward_err * reward_err + soft - cont * end_logit
        loss = loss + 0.5 * value_err * value_err
        actor = (place >= 3) & (place < outs_all - VOCAB)
        act_top = jnp.max(jnp.where(actor, small, NEG), axis=0, keepdims=True)
        act_e = jnp.where(actor, jnp.exp(jnp.where(actor, small - act_top, 0.0)), 0.0)
        act_sum = jnp.sum(act_e, axis=0, keepdims=True)
        log_pi = jnp.where(actor, small - act_top - jnp.log(act_sum), 0.0)
        pi = act_e / act_sum
        neg_entropy = jnp.sum(pi * log_pi, axis=0, keepdims=True)
        taken = place == action + 3
        picked_pi = jnp.sum(jnp.where(taken, log_pi, 0.0), axis=0, keepdims=True)
        gap = ret - target
        loss = loss - gap * picked_pi + ENTROPY_COEF * neg_entropy
        grad = gap * (pi - jnp.where(taken, 1.0, 0.0))
        grad = grad + ENTROPY_COEF * pi * (log_pi - neg_entropy)
        grad = jnp.where(actor, grad, 0.0)
        grad = jnp.where(place == 0, reward_err, grad)
        grad = jnp.where(place == 1, sigmoid - cont, grad)
        grad = jnp.where(place == 2, value_err, grad)
        lossacc[0:1, :] += loss * valid
        lossacc[1:2, :] += valid
        return jnp.concatenate([grad_logits, (grad * valid).astype(BF)], axis=0)

    def losses(i, carry):
        pieces = [(c, chunk_rows(c)) for c in both_chunks(i)]
        hidden = [xs[2 * layers, rows, :] for _, rows in pieces]
        normed = [rms_apply(x, top_gain) for x in hidden]
        outs = [dot_nt(rt[...], h) for h in normed]
        found = [loss_grad(c, out) for (c, _), out in zip(pieces, outs)]
        pulled = [dot_tn(grad, rt[...]) for grad in found]
        for (c, rows), x, h, grad, dh in zip(pieces, hidden, normed, found, pulled):
            hs[2 * layers, rows, :] = h
            gouts[:, rows] = grad
            grad_x, part = rms_pull(dh, x, top_gain)
            gx[rows, :] = grad_x
            gl[rows, :] = grad_x.astype(BF)
            dgain[2 * layers] += part
        return carry

    lax.fori_loop(0, chunks // 2, losses, 0)
    tail_at = VOCAB + layers * 12 * 256 + OUTS
    put(0, dot_nn(gouts[0:VOCAB, :], hs[2 * layers]))
    put(tail_at, dot_nn(gouts[VOCAB:OUTS, :], hs[2 * layers]))
    loss_total = jnp.sum(lossacc[0:1, :])
    count_total = jnp.sum(lossacc[1:2, :])
    place = iota(scal_ref.shape, 0)
    ex.tile_out[0, 0] = jnp.where(place == 0, loss_total, jnp.where(place == 1, count_total, 0.0))
    ex.begin(len(buckets))

    def spread(low, high, parts, spent, body):
        for part in range(parts):
            first = low + (high - low) * part // parts
            lax.fori_loop(first, low + (high - low) * (part + 1) // parts, body, 0)
            ex.tick(spent / parts)

    def feed_back(layer):
        gain = gains_ref[2 * layer + 1 : 2 * layer + 2, :]

        def body(i, carry):
            pieces = [chunk_rows(c) for c in both_chunks(i)]
            hidden = [[], []]
            for j in range(ff // 256):
                cols = slice(j * 256, j * 256 + 256)
                for rows, parts in zip(pieces, hidden):
                    da = dot_nt(gl[rows, :], wd[layer, cols, :])
                    parts.append((da * gds[layer, rows, cols].astype(F32)).astype(BF))
            hidden = [jnp.concatenate(parts, axis=1) for parts in hidden]
            pulled = [dot_nt(du, wu[layer]) for du in hidden]
            for rows, du, dh in zip(pieces, hidden, pulled):
                gds[layer, rows, :] = du
                grad_x, part = rms_pull(dh, xs[2 * layer + 1, rows, :], gain)
                dgain[2 * layer + 1] += part
                grad = gx[rows, :] + grad_x
                gx[rows, :] = grad
                low = grad.astype(BF)
                gl[rows, :] = low
                dmix[rows, :] = dot_nt(low, wo[layer]).astype(BF)
            return carry

        spread(0, chunks // 2, 3, 3.3, body)

    def attend_back(layer):
        def steps(i):
            items = [(b, 2 * i + j) for j in range(2) for b in range(batch)]
            keys, values, queries, douts = [], [], [], []
            for b, pair in items:
                window, rows = pair_window(pair), pair_rows(b, pair)
                keys.append(both(kvs[layer, b, window, 0:dims]))
                values.append(both(kvs[layer, b, window, dims:]))
                queries.append(by_group(qs[layer, rows, :]))
                douts.append(by_group(dmix[rows, :]))
            weights = [probs[layer, b * pairs + pair] for b, pair in items]
            pulled = [dot_nt(value, dout) for value, dout in zip(values, douts)]
            slopes = []
            for p, dp in zip(weights, pulled):
                sides = []
                for side in range(2):
                    part = slice(side * KEY, side * KEY + KEY)
                    pf = p[part].astype(F32)
                    d = dp[part]
                    sides.append((pf * (d - jnp.sum(d * pf, axis=0, keepdims=True))).astype(BF))
                slopes.append(jnp.concatenate(sides, axis=0))
            for (b, pair), ds, key in zip(items, slopes, keys):
                dqkv[pair_rows(b, pair), 0:dims] = (gather_heads(dot_tn(ds, key)) * scale).astype(BF)
            wide = []
            for ds, query, p, dout in zip(slopes, queries, weights, douts):
                dk = dot_nn(ds, query) * scale
                dv = dot_nn(p, dout)
                dk = jnp.where(even_f, dk[0:KEY], dk[KEY:])
                wide.append(jnp.concatenate([dk, jnp.where(even_f, dv[0:KEY], dv[KEY:])], axis=1))
            return items, wide

        def keep(items, wide):
            before = [carried[b] + wide[b][0:SEG] for b in range(batch)]
            for at, (b, pair) in enumerate(items):
                rows = pl.multiple_of(b * span + pair * QRY, 16)
                dqkv[pl.ds(rows, SEG), dims:] = wide[at][SEG:QRY].astype(BF)
                if at + batch < len(items):
                    ending = wide[at][QRY:] + wide[at + batch][0:SEG]
                    dqkv[pl.ds(pl.multiple_of(rows + SEG, 16), SEG), dims:] = ending.astype(BF)
                else:
                    carried[b] = wide[at][QRY:]
            return before

        def body(i, carry):
            before = keep(*steps(i))
            for b in range(batch):
                rows = pl.ds(pl.multiple_of(b * span + i * 2 * QRY - SEG, 16), SEG)
                dqkv[rows, dims:] = before[b].astype(BF)
            return carry

        carried[...] = jnp.zeros_like(carried)
        before = keep(*steps(0))
        for b in range(batch):
            bsend[layer, b] = before[b].astype(BF)
        copy = backward_copy(layer)
        copy.start()
        ex.tick(1.7)
        spread(1, pairs // 2, 3, 5.1, body)
        copy.wait()
        for b in range(batch):
            final = carried[b] + brecv[layer, b].astype(F32)
            dqkv[b * span + span - SEG : b * span + span, dims:] = final.astype(BF)

    def project_back(layer):
        gain = gains_ref[2 * layer : 2 * layer + 1, :]

        def body(i, carry):
            pieces = [chunk_rows(c) for c in both_chunks(i)]
            pulled = [dot_nt(dqkv[rows, :], wq[layer]) for rows in pieces]
            for rows, dh in zip(pieces, pulled):
                grad_x, part = rms_pull(dh, xs[2 * layer, rows, :], gain)
                dgain[2 * layer] += part
                grad = gx[rows, :] + grad_x
                gx[rows, :] = grad
                gl[rows, :] = grad.astype(BF)
            return carry

        spread(0, chunks // 2, 2, 1.5, body)

    at = VOCAB
    bucket = 0
    for layer in reversed(range(layers)):
        for j in range(ff // 256):
            cols = slice(j * 256, j * 256 + 256)
            put(at, dot_tn(acts[layer, :, cols], gl[...]))
            at += 256
        ex.begin(bucket)
        ex.tick(1.2)
        feed_back(layer)
        for j in range(ff // 256):
            cols = slice(j * 256, j * 256 + 256)
            put(at, dot_tn(hs[2 * layer + 1], gds[layer, :, cols]))
            at += 256
            if j % 2:
                ex.tick(0.4)
        put(at, dot_tn(mixes[layer], gl[...]))
        at += 256
        ex.begin(bucket + 1)
        ex.tick(0.2)
        attend_back(layer)
        for j in range(3):
            cols = slice(j * 256, j * 256 + 256)
            put(at, dot_tn(hs[2 * layer], dqkv[:, cols]))
            at += 256
        bucket += 2
        if layer == 0:
            ex.begin(bucket)
        ex.tick(0.7)
        project_back(layer)

    def mark(c, carry):
        gouts[:, chunk_rows(c)] = onehot(c)
        return carry

    lax.fori_loop(0, chunks, mark, 0)
    put(at, dot_nn(gouts[...], gl[...]))
    ex.tick(1.6)
    at = tail_at + OUTS - VOCAB
    place = iota((16, dims), 0)
    gain_rows = jnp.zeros((16, dims), F32)
    for index in range(2 * layers + 1):
        gain_rows = jnp.where(place == index, jnp.sum(dgain[index], axis=0, keepdims=True), gain_rows)
    put(at, gain_rows)
    at += 16
    put(at, jnp.zeros((grads_ref.shape[1] - at, dims), F32))
    ex.begin(len(buckets) - 1)
    ex.drain()
    count = ex.tile_out[0, 3, 1:2, 0:1]
    norm = jnp.sqrt(jnp.sum(ex.tile_out[1, 3]) / (count * count))
    place = iota(scal_ref.shape, 0)
    scal = jnp.where(place == 2, norm, ex.tile_out[0, 3])
    scal_ref[...] = jnp.where(place == 3, jnp.minimum(1.0, CLIP_NORM / norm) / count, scal)
    for n in range(len(buckets)):
        ex.wait(ex.out_copies(n))


def gradients(codes, actions, next_codes, lengths, rewards, continues, values, weights, sizes):
    table, attn_in, attn_out, ffn_in, ffn_out, gains, readout = weights
    batch, span = codes.shape
    layers, dims, ff = ffn_in.shape
    total = batch * span
    tiles = span // SEG
    chunks = total // ROWS
    grad_rows = grad_row_count(layers)
    buckets = buckets_of(layers)
    seq_size, dp_size = sizes
    shares = [(b[1] - b[0]) // seq_size // owners_of(b, seq_size, dp_size // 2) for b in buckets]
    slots = exchange_slots(dp_size)
    hbm = pl.BlockSpec(memory_space=pltpu.HBM)
    steps = np.arange(lax.axis_size("seq") * tiles + 1, dtype=np.float64)[:, None]
    freq = np.exp(np.arange(dims // 2) * (-2.0 * math.log(10000.0) / dims))
    trig = np.zeros((steps.shape[0], 8, dims // 2), np.float32)
    trig[:, 0], trig[:, 1] = np.sin(steps * SEG * freq), np.cos(steps * SEG * freq)
    trig[:, 2], trig[:, 3] = np.sin(steps * freq), np.cos(steps * freq)
    trig = jnp.asarray(trig)
    vmem = pl.BlockSpec(memory_space=pltpu.VMEM)
    smem = pl.BlockSpec(memory_space=pltpu.SMEM)
    return pl.pallas_call(
        functools.partial(step_kernel, layers, sizes, buckets),
        out_shape=(
            jax.ShapeDtypeStruct((2, grad_rows, dims // 2), BF),
            jax.ShapeDtypeStruct((8, 128), F32),
        ),
        in_specs=[vmem] * 3 + [smem] + [vmem] * 4 + [hbm] * 5 + [vmem, hbm],
        out_specs=(hbm, vmem),
        scratch_shapes=[
            pltpu.VMEM((layers, dims, 3 * dims), BF),
            pltpu.VMEM((layers, dims, dims), BF),
            pltpu.VMEM((layers, dims, ff), BF),
            pltpu.VMEM((layers, ff, dims), BF),
            pltpu.VMEM((OUTS, dims), BF),
            pltpu.VMEM((OUTS, dims), BF),
            pltpu.VMEM((2 * layers + 1, total, dims), F32),
            pltpu.VMEM((2 * layers + 1, total, dims), BF),
            pltpu.VMEM((layers, total, dims), BF),
            pltpu.VMEM((layers, batch, SEG + span, 2 * dims), BF),
            pltpu.VMEM((layers, total // QRY, 2 * KEY, HEADS // 2 * QRY), BF),
            pltpu.VMEM((layers, total, ff), BF),
            pltpu.VMEM((layers, total, ff), BF),
            pltpu.VMEM((layers, total, dims), BF),
            pltpu.VMEM((total // QRY, 8, HEADS // 2 * QRY), jnp.int32),
            pltpu.VMEM((chunks, 8, ROWS), F32),
            pltpu.VMEM((chunks, 8, ROWS), jnp.int32),
            pltpu.VMEM((OUTS, total), BF),
            pltpu.VMEM((total, dims), F32),
            pltpu.VMEM((total, dims), BF),
            pltpu.VMEM((total, dims), BF),
            pltpu.VMEM((total, 3 * dims), BF),
            pltpu.VMEM((batch, SEG, 2 * dims), F32),
            pltpu.VMEM((2 * layers + 1, 8, dims), F32),
            pltpu.VMEM((8, ROWS), F32),
            pltpu.VMEM((4, 8, span), F32),
            pltpu.VMEM((layers, batch, SEG, 2 * dims), BF),
            pltpu.VMEM((layers, batch, SEG, 2 * dims), BF),
            pltpu.SemaphoreType.DMA((2 * layers,)),
            pltpu.SemaphoreType.DMA((2 * layers,)),
            pltpu.SemaphoreType.DMA((2 + 12 * layers,)),
            pltpu.VMEM(table.shape, F32),
            pltpu.VMEM(readout.shape, F32),
            pltpu.VMEM((2, grad_rows, dims // 2), BF),
            pltpu.VMEM((grad_rows, dims // 2), BF),
            pltpu.VMEM((seq_size - 1, grad_rows // seq_size, dims // 2), BF),
            pltpu.VMEM((grad_rows // seq_size, dims // 2), BF),
            pltpu.VMEM((dp_size // 2 - 1, sum(shares), dims // 2), BF),
            pltpu.VMEM((8, dims // 2), F32),
            pltpu.VMEM((2, 4, 8, 128), F32),
            pltpu.VMEM((2, slots // 2, 8, 128), F32),
            pltpu.SemaphoreType.DMA((len(buckets) + 2, slots)),
            pltpu.SemaphoreType.DMA((len(buckets) + 2, slots)),
            pltpu.SemaphoreType.DMA((len(buckets), 2)),
        ],
        compiler_params=pltpu.CompilerParams(
            collective_id=0, has_side_effects=True, vmem_limit_bytes=63 * 1024 * 1024
        ),
        name="train_step",
    )(
        codes,
        actions,
        next_codes,
        lengths,
        rewards,
        continues,
        values,
        trig,
        table,
        attn_in,
        attn_out,
        ffn_in,
        ffn_out,
        gains,
        readout,
    )


def adam_update(weight, first_mom, second_mom, clipped, rate):
    new_first = BETA_ONE * first_mom + (1.0 - BETA_ONE) * clipped
    new_second = BETA_TWO * second_mom + (1.0 - BETA_TWO) * clipped * clipped
    root = jnp.sqrt(new_second * (1.0 / (1.0 - BETA_TWO**STEP))) + ADAM_EPS
    ratio = new_first * (rate / (1.0 - BETA_ONE**STEP)) / root
    return (weight * (1.0 - rate * DECAY) - ratio, new_first, new_second)


AHEAD = 5


def update_kernel(layers, scal_ref, sums_ref, *refs):
    ins, outs, scalars, here = refs[0:21], refs[21:42], refs[42:45], refs[45:66]
    load_sem, store_sem, sum_sem, grads_ref = refs[66:]
    scale = scal_ref[3, 0]
    for k, ref in enumerate(scalars):
        ref[0, 0] = scal_ref[k, 0]
    pieces = [(slot, layer) for slot in (4, 3, 1, 2) for layer in range(layers)]
    pieces += [(0, None), (5, None), (6, None)]

    offset = VOCAB
    starts = {}
    for layer in reversed(range(layers)):
        starts[4, layer] = offset
        starts[3, layer] = offset + 4 * 256
        starts[2, layer] = offset + 8 * 256
        starts[1, layer] = offset + 9 * 256
        offset += 12 * 256
    table_at, tail_at = offset, offset + OUTS
    gains_at = tail_at + OUTS - VOCAB

    def view(ref, layer):
        return ref if layer is None else ref.at[layer]

    def moves(n, kind):
        slot, layer = pieces[n]
        for part in range(3):
            index = 3 * slot + part
            inside = view(here[index], layer)
            if kind == 0:
                yield pltpu.make_async_copy(view(ins[index], layer), inside, load_sem.at[n, part])
            else:
                yield pltpu.make_async_copy(inside, view(outs[index], layer), store_sem.at[n, part])

    def fetch(n):
        slot, layer = pieces[n]
        rows = {0: (table_at, OUTS), 6: (0, VOCAB), 5: (tail_at, sums_ref.shape[1] - tail_at)}
        if layer is not None:
            rows[slot] = (starts[slot, layer], here[3 * slot].shape[1] * here[3 * slot].shape[2] // 256)
        at, count = rows[slot]
        part = pl.ds(at, count)
        return pltpu.make_async_copy(sums_ref.at[:, part], grads_ref.at[:, part], sum_sem.at[n])

    def begin(n):
        for move in moves(n, 0):
            move.start()
        fetch(n).start()

    for n in range(AHEAD):
        begin(n)

    def renew(slot, layer, rows, cols, grad):
        refs = [view(here[3 * slot + part], layer) for part in range(3)]
        new = adam_update(*[ref[rows, cols] for ref in refs], grad.astype(F32) * scale, RATES[slot])
        for ref, value in zip(refs, new):
            ref[rows, cols] = value

    for n, (slot, layer) in enumerate(pieces):
        if n + AHEAD < len(pieces):
            begin(n + AHEAD)
        for move in moves(n, 0):
            move.wait()
        fetch(n).wait()
        if layer is not None:
            rows_all, cols_all = here[3 * slot].shape[1:]
            at = starts[slot, layer]
            for j in range(rows_all // 256):
                for i in range(cols_all // 256):
                    for side in range(2):
                        cols = slice(i * 256 + side * 128, i * 256 + side * 128 + 128)

                        def body(k, carry):
                            rows = pl.ds(pl.multiple_of(j * 256 + k * 64, 64), 64)
                            block = at + (j + i) * 256 + k * 64
                            grad = grads_ref[side, pl.ds(pl.multiple_of(block, 64), 64), :]
                            renew(slot, layer, rows, cols, grad)
                            return carry

                        lax.fori_loop(0, 4, body, 0)
        elif slot == 0:
            rows_all = here[0].shape[0]
            for side in range(2):
                cols = slice(side * 128, side * 128 + 128)

                def body(k, carry):
                    rows = pl.ds(pl.multiple_of(k * 64, 64), 64)
                    block = pl.ds(pl.multiple_of(table_at + k * 64, 64), 64)
                    renew(0, None, rows, cols, grads_ref[side, block, :])
                    return carry

                full = rows_all // 64
                lax.fori_loop(0, full, body, 0)
                if rows_all % 64:
                    last = slice(full * 64, rows_all)
                    block = grads_ref[side, table_at + full * 64 : tail_at, :]
                    renew(0, None, last, cols, block.astype(F32)[0 : rows_all % 64])
        elif slot == 6:
            outs_all = here[18].shape[0]
            for side in range(2):
                cols = slice(side * 128, side * 128 + 128)

                def body(k, carry):
                    rows = pl.ds(pl.multiple_of(k * 64, 64), 64)
                    renew(6, None, rows, cols, grads_ref[side, rows, :])
                    return carry

                lax.fori_loop(0, VOCAB // 64, body, 0)
                rest = grads_ref[side, tail_at : tail_at + OUTS - VOCAB, :].astype(F32)
                renew(6, None, slice(VOCAB, outs_all), cols, rest[0 : outs_all - VOCAB])
        else:
            count = here[15].shape[0]
            for side in range(2):
                cols = slice(side * 128, side * 128 + 128)
                grad = grads_ref[side, gains_at : gains_at + 16, :].astype(F32)[0:count]
                renew(5, None, slice(0, count), cols, grad)
        for move in moves(n, 1):
            move.start()
    for n in range(len(pieces)):
        for move in moves(n, 1):
            move.wait()


def update(grads, scal, state):
    layers = state[3].shape[0]
    anywhere = pl.BlockSpec(memory_space=pltpu.HBM)
    pieces = 4 * layers + 3
    return pl.pallas_call(
        functools.partial(update_kernel, layers),
        out_shape=tuple(jax.ShapeDtypeStruct(x.shape, F32) for x in state)
        + (jax.ShapeDtypeStruct((1, 1), F32),) * 3,
        in_specs=[
            pl.BlockSpec(memory_space=pltpu.SMEM),
            anywhere,
        ]
        + [anywhere] * 21,
        out_specs=(anywhere,) * 21 + (pl.BlockSpec(memory_space=pltpu.SMEM),) * 3,
        scratch_shapes=[pltpu.VMEM(x.shape, F32) for x in state]
        + [
            pltpu.SemaphoreType.DMA((pieces, 3)),
            pltpu.SemaphoreType.DMA((pieces, 3)),
            pltpu.SemaphoreType.DMA((pieces,)),
            pltpu.VMEM(grads.shape, BF),
        ],
        compiler_params=pltpu.CompilerParams(vmem_limit_bytes=62 * 1024 * 1024),
        name="update",
    )(scal, grads, *state)


def local(codes, actions, next_codes, lengths, rewards, continues, target_values, *state):
    state = state[0:18] + tuple(value.T for value in state[18:21])
    params = state[0::3]
    seq_size, dp_size = lax.axis_size("seq"), lax.axis_size("dp")
    sizes = (seq_size, dp_size)
    grads, scal = gradients(
        codes, actions, next_codes, lengths, rewards, continues, target_values, params, sizes
    )
    results = list(update(grads, scal, state))
    results[18:21] = [value.T for value in results[18:21]]
    results[21:24] = [value.reshape(()) for value in results[21:24]]
    return tuple(results)


def solution(mesh):
    rows, whole = P("dp", "seq"), P()
    return jax.shard_map(
        local,
        mesh=mesh,
        in_specs=(rows, rows, rows, P("dp", None), rows, rows, rows) + (whole,) * 21,
        out_specs=(whole,) * 24,
        check_vma=False,
    )
```

```python
import functools
import math

import jax
import jax.numpy as jnp
import numpy as np
from jax import lax
from jax.experimental import pallas as pl
from jax.experimental.pallas import tpu as pltpu
from jax.sharding import PartitionSpec as P

HEADS = 8
VOCAB = 512
SEG = 48
STEP = 5

EPS_NORM = 1e-06
BETA_ONE = 0.9
BETA_TWO = 0.999
RATES = (0.25, 0.02, 0.08, 0.02, 0.02, 0.25, 0.02)
DECAY = 0.01
ADAM_EPS = 1e-08
CLIP_NORM = 0.05
GAMMA = 0.985
LAMBDA_RET = 0.95
ENTROPY_COEF = 0.05

BF = jnp.bfloat16
F32 = jnp.float32
ROWS = 256
QRY = 2 * SEG
KEY = 3 * SEG
OUTS = 544
NEG = -1e30
MESH = pl.DeviceIdType.MESH
PER_ROW = 256 / 92e3
TRANSFERS = {
    "core": ("core", PER_ROW / 5.4, 1.1),
    "seq": ("seq", PER_ROW, 3.3),
    "deep": ("deep", PER_ROW / 2, 3.5),
    "tile": ("tile", 0.0, 3.6),
}
PATH = ("core", "seq", "deep", "back_deep", "back_seq", "back_core")
STAGE_TIME = 0.35


def dot_nn(left, right):
    return jnp.dot(left, right, preferred_element_type=F32)


def dot_tn(left, right):
    return lax.dot_general(left, right, (((0,), (0,)), ((), ())), preferred_element_type=F32)


def dot_nt(left, right):
    return lax.dot_general(left, right, (((1,), (1,)), ((), ())), preferred_element_type=F32)


def iota(shape, dim):
    return lax.broadcasted_iota(jnp.int32, shape, dim)


def rms_apply(x, gain):
    inv = lax.rsqrt(jnp.mean(x * x, axis=-1, keepdims=True) + EPS_NORM)
    return (x * inv * gain).astype(BF)


def rms_pull(grad, x, gain):
    inv = lax.rsqrt(jnp.mean(x * x, axis=-1, keepdims=True) + EPS_NORM)
    unit = x * inv
    weighted = grad * gain
    grad_x = inv * (weighted - unit * jnp.mean(weighted * unit, axis=-1, keepdims=True))
    rows, dims = x.shape
    return grad_x, jnp.sum((grad * unit).reshape(rows // 8, 8, dims), axis=0)


def grad_row_count(layers):
    rows = VOCAB + layers * 12 * 256 + OUTS + (OUTS - VOCAB) + 16
    return -(-rows // 256) * 256


def buckets_of(layers):
    cuts = [0, VOCAB + 4 * 256]
    for layer in range(layers):
        cuts.append(cuts[-1] + 5 * 256)
        cuts.append(cuts[-1] + (3 if layer == layers - 1 else 7) * 256)
    cuts.append(grad_row_count(layers))
    return list(zip(cuts[:-1], cuts[1:]))


def owners_of(bucket, seq_size, deep):
    quarter = (bucket[1] - bucket[0]) // seq_size
    return max(k for k in range(1, deep + 1) if quarter % (16 * k) == 0)


class Exchange:
    def __init__(self, seq_size, dp_size, buckets, grads, out, core_in, seq_in, seq_out, deep_in,
                 squares, tile_out, tile_in, send_sem, recv_sem, out_sem):
        self.deep = dp_size // 2
        self.seq_size = seq_size
        self.buckets = buckets
        self.grads, self.out = grads, out
        self.core_in, self.seq_in, self.seq_out, self.deep_in = core_in, seq_in, seq_out, deep_in
        self.squares = squares
        self.tile_out, self.tile_in = tile_out, tile_in
        self.send_sem, self.recv_sem, self.out_sem = send_sem, recv_sem, out_sem
        self.slots = exchange_slots(dp_size)
        me = lax.axis_index("seq")
        at_dp = lax.axis_index("dp")
        self.me, self.core, self.at_deep = me, lax.rem(at_dp, 2), lax.div(at_dp, 2)
        self.sibling = {"dp": self.at_deep * 2 + 1 - self.core}
        self.stage, self.due, self.free, self.now, self.summed = {}, {}, {}, 0.0, 0

    def deep_peer(self, k):
        return {"dp": lax.rem(self.at_deep + k, self.deep) * 2 + self.core}

    def peers(self):
        found = [self.sibling]
        found += [{"seq": lax.rem(self.me + k, self.seq_size)} for k in range(1, self.seq_size)]
        return found + [self.deep_peer(k) for k in range(1, self.deep)]

    def greet(self):
        for peer in self.peers():
            pl.semaphore_signal(
                pltpu.get_barrier_semaphore(), inc=1, device_id=peer, device_id_type=MESH
            )

    def greeted(self):
        pl.semaphore_wait(pltpu.get_barrier_semaphore(), len(self.peers()))

    def copy(self, src, dst, n, slot, peer):
        return pltpu.make_async_remote_copy(
            src_ref=src,
            dst_ref=dst,
            send_sem=self.send_sem.at[n, slot],
            recv_sem=self.recv_sem.at[n, slot],
            device_id=peer,
            device_id_type=MESH,
        )

    def only(self, n, index, act):
        owners = owners_of(self.buckets[n], self.seq_size, self.deep)
        if owners == self.deep:
            act()
        else:
            pl.when(index < owners)(act)

    def parts(self, n):
        r0, r1 = self.buckets[n]
        quarter = (r1 - r0) // self.seq_size
        return r0, r1 - r0, quarter, quarter // owners_of(self.buckets[n], self.seq_size, self.deep)

    def place(self, n, index):
        return lax.rem(index, owners_of(self.buckets[n], self.seq_size, self.deep))

    def deep_rows(self, n):
        at = sum(self.parts(k)[3] for k in range(n))
        return pl.ds(at, self.parts(n)[3])

    def quarter_rows(self, n, index):
        r0, _, quarter, _ = self.parts(n)
        return pl.ds(pl.multiple_of(r0 + index * quarter, 16), quarter)

    def packed_rows(self, n):
        r0, _, quarter, _ = self.parts(n)
        return pl.ds(r0 // self.seq_size, quarter)

    def share_rows(self, n, index):
        r0, _, _, share = self.parts(n)
        return pl.ds(pl.multiple_of(r0 // self.seq_size + index * share, 16), share)

    def own_rows(self, n):
        r0, _, quarter, share = self.parts(n)
        at = r0 + self.me * quarter + self.place(n, self.at_deep) * share
        return pl.ds(pl.multiple_of(at, 16), share)

    def blocks(self, n, index, work):
        r0, _, quarter, _ = self.parts(n)
        size = quarter // 2 if quarter > 256 else quarter
        for at in range(0, quarter, size):
            wide = pl.ds(pl.multiple_of(r0 + index * quarter + at, 16), size)
            work(wide, pl.ds(r0 // self.seq_size + at, size))

    def core_copies(self, n):
        r0, rows, _, _ = self.parts(n)
        part = pl.ds(r0, rows)
        return [self.copy(self.grads.at[1 - self.core, part], self.core_in.at[part], n, 0, self.sibling)]

    def seq_copies(self, n):
        packed = self.packed_rows(n)
        found = []
        for k in range(1, self.seq_size):
            peer = lax.rem(self.me + k, self.seq_size)
            source = self.core_in.at[self.quarter_rows(n, peer)]
            found.append(self.copy(source, self.seq_in.at[k - 1, packed], n, k, {"seq": peer}))
        return found

    def deep_copy(self, n, k):
        target = self.place(n, lax.rem(self.at_deep + k, self.deep))
        dest = self.deep_in.at[k - 1, self.deep_rows(n)]
        return self.copy(self.seq_out.at[self.share_rows(n, target)], dest, n, 3 + k, self.deep_peer(k))

    def back_copy(self, n, rows, slot, peer):
        there = self.grads.at[self.core, rows]
        return self.copy(there, there, n, self.slots // 2 + slot, peer)

    def back_seq(self, n):
        rows = self.quarter_rows(n, self.me)
        return [
            self.back_copy(n, rows, k, {"seq": lax.rem(self.me + k, self.seq_size)})
            for k in range(1, self.seq_size)
        ]

    def back_core(self, n):
        r0, rows, _, _ = self.parts(n)
        return [self.back_copy(n, pl.ds(r0, rows), 0, self.sibling)]

    def out_copies(self, n):
        r0, rows, _, _ = self.parts(n)
        part = pl.ds(r0, rows)
        return [
            pltpu.make_async_copy(self.grads.at[side, part], self.out.at[side, part], self.out_sem.at[n, side])
            for side in range(2)
        ]

    def start(self, copies):
        for copy in copies:
            copy.start()

    def wait(self, copies):
        for copy in copies:
            copy.wait()

    def own_sum(self, wide, packed):
        both = self.grads[self.core, wide, :].astype(F32) + self.core_in[wide, :].astype(F32)
        for k in range(self.seq_size - 1):
            both = both + self.seq_in[k, packed, :].astype(F32)
        return both

    def after_core(self, n):
        def work(wide, packed):
            both = self.grads[self.core, wide, :].astype(F32) + self.core_in[wide, :].astype(F32)
            self.core_in[wide, :] = both.astype(BF)

        for k in range(1, self.seq_size):
            self.blocks(n, lax.rem(self.me + k, self.seq_size), work)

    def after_seq(self, n):
        def work(wide, packed):
            self.seq_out[packed, :] = self.own_sum(wide, packed).astype(BF)

        self.blocks(n, self.me, work)

    def after_deep(self, n):
        share = self.parts(n)[3]

        def act():
            rows = self.own_rows(n)
            both = self.own_sum(rows, self.share_rows(n, self.place(n, self.at_deep)))
            part = self.deep_rows(n)
            for k in range(self.deep - 1):
                both = both + self.deep_in[k, part, :].astype(F32)
            self.grads[self.core, rows, :] = both.astype(BF)
            self.squares[...] += jnp.sum((both * both).reshape(share // 8, 8, both.shape[1]), axis=0)

        self.only(n, self.at_deep, act)

    def begin_deep(self, n):
        for k in range(1, self.deep):
            target = lax.rem(self.at_deep + k, self.deep)
            self.only(n, target, self.deep_copy(n, k).start)

    def end_deep(self, n):
        for k in range(1, self.deep):
            target = lax.rem(self.at_deep + k, self.deep)
            self.only(n, target, self.deep_copy(n, k).wait_send)

        def act():
            for k in range(1, self.deep):
                self.deep_copy(n, k).wait_recv()

        self.only(n, self.at_deep, act)

    def begin_back_deep(self, n):
        rows = self.own_rows(n)

        def act():
            for k in range(1, self.deep):
                self.back_copy(n, rows, 3 + k, self.deep_peer(k)).start()

        self.only(n, self.at_deep, act)

    def end_back_deep(self, n):
        rows = self.own_rows(n)

        def act():
            for k in range(1, self.deep):
                self.back_copy(n, rows, 3 + k, self.deep_peer(k)).wait_send()

        self.only(n, self.at_deep, act)
        for k in range(1, self.deep):
            origin = lax.rem(self.at_deep + self.deep - k, self.deep)
            self.only(n, origin, self.back_copy(n, rows, 3 + k, self.deep_peer(k)).wait_recv)

    def begin_transfer(self, n, name):
        if name == "deep":
            self.begin_deep(n)
        elif name == "back_deep":
            self.begin_back_deep(n)
        else:
            self.start(getattr(self, name if "back" in name else name + "_copies")(n))

    def end_transfer(self, n, name):
        if name == "deep":
            self.end_deep(n)
        elif name == "back_deep":
            self.end_back_deep(n)
        else:
            self.wait(getattr(self, name if "back" in name else name + "_copies")(n))
        if name == "core":
            self.after_core(n)
        elif name == "seq":
            self.after_seq(n)
        elif name == "deep":
            self.after_deep(n)
        elif name == "back_core":
            self.start(self.out_copies(n))

    def plan_launch(self, n):
        if n < len(self.buckets):
            name, rows = PATH[self.stage[n]], self.buckets[n][1] - self.buckets[n][0]
        else:
            name, rows = "tile", 0
        link, share, latency = TRANSFERS[name.replace("back_", "")]
        self.free[link] = max(self.now, self.free.get(link, 0.0)) + rows * share
        self.due[n] = self.free[link] + latency

    def plan_begin(self, n):
        self.stage[n] = 0
        self.plan_launch(n)
        return (n, None, 0)

    def plan_advance(self, n):
        step = self.stage[n]
        self.now = max(self.now, self.due.pop(n)) + STAGE_TIME
        self.stage[n] += 1
        last = (len(PATH) if n < len(self.buckets) else 3) - 1
        if step < last:
            self.plan_launch(n)
        todo = [(n, step, step + 1 if step < last else None)]
        if n < len(self.buckets):
            self.summed += PATH[step] == "deep"
        norm = len(self.buckets) + 1
        if self.summed == len(self.buckets) and norm not in self.stage:
            todo.append(self.plan_begin(norm))
        return todo

    def plan(self, spent):
        self.now += spent
        todo = []
        for n in sorted(self.due):
            if self.due[n] + 0.3 <= self.now:
                todo += self.plan_advance(n)
        return todo

    def run(self, todo):
        for n, ended, begun in todo:
            if n < len(self.buckets):
                if ended is not None:
                    self.end_transfer(n, PATH[ended])
                if begun is not None:
                    self.begin_transfer(n, PATH[begun])
            else:
                tile = n - len(self.buckets)
                if tile == 1 and ended is None:
                    self.tile_out[1, 0] = self.squares[...]
                if ended is not None:
                    self.tile_finish(tile, ended)
                if begun is not None:
                    self.tile_start(tile, begun)

    def begin(self, n):
        self.run([self.plan_begin(n)])

    def tick(self, spent):
        self.run(self.plan(spent))

    def drain(self):
        while self.due:
            self.run(self.plan_advance(min(self.due, key=lambda n: (self.due[n], n))))

    def tile_copies(self, tile, phase):
        if phase == 0:
            slots, peers = [0], [self.sibling]
        elif phase == 1:
            slots = list(range(1, self.seq_size))
            peers = [{"seq": lax.rem(self.me + k, self.seq_size)} for k in slots]
        else:
            slots = [3 + k for k in range(1, self.deep)]
            peers = [self.deep_peer(k) for k in range(1, self.deep)]
        n = len(self.buckets) + tile
        return [
            self.copy(self.tile_out.at[tile, phase], self.tile_in.at[tile, slot], n, slot, peer)
            for slot, peer in zip(slots, peers)
        ], slots

    def tile_start(self, tile, phase):
        self.start(self.tile_copies(tile, phase)[0])

    def tile_finish(self, tile, phase):
        copies, slots = self.tile_copies(tile, phase)
        self.wait(copies)
        both = self.tile_out[tile, phase]
        for slot in slots:
            both = both + self.tile_in[tile, slot]
        self.tile_out[tile, phase + 1] = both


def exchange_slots(dp_size):
    return 2 * (4 + dp_size // 2 - 1)


def step_kernel(
    layers,
    sizes,
    buckets,
    codes_ref,
    actions_ref,
    next_ref,
    lengths_ref,
    rewards_ref,
    continues_ref,
    values_ref,
    trig_ref,
    table_ref,
    attn_in_ref,
    attn_out_ref,
    ffn_in_ref,
    ffn_out_ref,
    gains_ref,
    readout_ref,
    out_ref,
    scal_ref,
    wq,
    wo,
    wu,
    wd,
    rt,
    tb,
    xs,
    hs,
    qs,
    kvs,
    probs,
    acts,
    gds,
    mixes,
    lows,
    tokf,
    toki,
    gouts,
    gx,
    gl,
    dmix,
    dqkv,
    carried,
    dgain,
    lossacc,
    lam,
    bsend,
    brecv,
    send_sem,
    recv_sem,
    load_sem,
    table_f,
    readout_f,
    grads_ref,
    *exchange_refs,
):
    batch, span = codes_ref.shape
    dims = gains_ref.shape[1]
    ff = ffn_in_ref.shape[2]
    tiles = span // SEG
    pairs = span // QRY
    total = batch * span
    chunks = total // ROWS
    per_seq = span // ROWS
    vocab_all = table_ref.shape[0]
    outs_all = readout_ref.shape[0]
    head_dim = dims // HEADS
    scale = head_dim ** (-0.5)
    exp_scale = scale * math.log2(math.e)
    groups = HEADS // 2
    base = lax.axis_index("seq") * span
    me = lax.axis_index("seq")
    seq_size = sizes[0]
    right = lax.rem(me + 1, seq_size)
    left = lax.rem(me + seq_size - 1, seq_size)

    ex = Exchange(*sizes, buckets, grads_ref, out_ref, *exchange_refs)
    ex.greet()
    ex.squares[...] = jnp.zeros_like(ex.squares)

    loads = [
        pltpu.make_async_copy(table_ref, table_f, load_sem.at[0]),
        pltpu.make_async_copy(readout_ref, readout_f, load_sem.at[1]),
    ]
    blocks = []
    for layer in range(layers):
        for j in range(3):
            blocks.append((attn_in_ref, wq, layer, slice(0, 256), slice(j * 256, j * 256 + 256)))
        blocks.append((attn_out_ref, wo, layer, slice(0, 256), slice(0, 256)))
        for j in range(ff // 256):
            blocks.append((ffn_in_ref, wu, layer, slice(0, 256), slice(j * 256, j * 256 + 256)))
        for j in range(ff // 256):
            blocks.append((ffn_out_ref, wd, layer, slice(j * 256, j * 256 + 256), slice(0, 256)))

    def place_of(k):
        at = (k + (2 * layers - 2) * chunks) % (2 * layers * chunks)
        return 1 + at // chunks, slice(256 * (at % chunks), 256 * (at % chunks) + 256)

    for k, (source, _, layer, rows, cols) in enumerate(blocks):
        plane, there = place_of(k)
        loads.append(
            pltpu.make_async_copy(source.at[layer, rows, cols], xs.at[plane, there, :], load_sem.at[2 + k])
        )
    for load in loads:
        load.start()

    def convert(low, high):
        for k in range(low, high):
            _, dest, layer, rows, cols = blocks[k]
            plane, there = place_of(k)
            loads[2 + k].wait()
            dest[layer, rows, cols] = xs[plane, there, :].astype(BF)

    tb[...] = jnp.zeros_like(tb)
    rt[...] = jnp.zeros_like(rt)

    ends = []
    for b in range(batch):
        run = jnp.int32(0)
        row = []
        for e in range(lengths_ref.shape[1]):
            run = run + lengths_ref[b, e]
            row.append(run)
        ends.append(row)
    episodes = len(ends[0])

    lane = iota((8, span), 1)
    lam[...] = jnp.zeros_like(lam)
    lam[0, 0:batch, :] = rewards_ref[...]
    lam[1, 0:batch, :] = continues_ref[...]
    lam[2, 0:batch, :] = values_ref[...]
    last = lax.rem(lane, SEG) == SEG - 1
    decay = GAMMA * lam[1]
    value_next = pltpu.roll(lam[2], span - 1, 1)
    add = jnp.where(last, lam[2], lam[0] + decay * ((1.0 - LAMBDA_RET) * value_next))
    mul = jnp.where(last, 0.0, decay * LAMBDA_RET)
    step = 1
    while step < SEG:
        add = add + mul * pltpu.roll(add, span - step, 1)
        mul = mul * pltpu.roll(mul, span - step, 1)
        step *= 2
    lam[3] = add
    valid_rows = []
    for b in range(batch):
        after = iota((1, span), 1) + (base + 1)
        final = after == ends[b][0]
        for e in range(1, episodes):
            final = final | (after == ends[b][e])
        valid_rows.append(jnp.where(final, 0.0, 1.0))
    for c in range(chunks):
        b = c // per_seq
        lanes = slice((c % per_seq) * ROWS, (c % per_seq) * ROWS + ROWS)
        for row in range(4):
            tokf[c, row : row + 1, :] = lam[row, b : b + 1, lanes]
        tokf[c, 4:5, :] = valid_rows[b][:, lanes]
        toki[c, 0:1, :] = codes_ref[b : b + 1, lanes]
        toki[c, 1:2, :] = actions_ref[b : b + 1, lanes]
        toki[c, 2:3, :] = next_ref[b : b + 1, lanes]

    half = dims // 2
    in_sin, in_cos = trig_ref[0:SEG, 2, :], trig_ref[0:SEG, 3, :]
    end_sin, end_cos = [], []
    for b in range(batch):
        for e in range(episodes):
            far, near = lax.div(ends[b][e], SEG), lax.rem(ends[b][e], SEG)
            far_sin, far_cos = trig_ref[far, 0:1, :], trig_ref[far, 1:2, :]
            near_sin, near_cos = trig_ref[near, 2:3, :], trig_ref[near, 3:4, :]
            end_sin.append(far_sin * near_cos + far_cos * near_sin)
            end_cos.append(far_cos * near_cos - far_sin * near_sin)

    def marks(tile, carry):
        at = me * tiles + tile
        tile_sin, tile_cos = trig_ref[at, 0:1, :], trig_ref[at, 1:2, :]
        here_sin = in_sin * tile_cos + in_cos * tile_sin
        here_cos = in_cos * tile_cos - in_sin * tile_sin
        place = iota((SEG, half), 0) + (base + tile * SEG)
        for b in range(batch):
            start_sin = jnp.zeros((SEG, half), F32)
            start_cos = jnp.ones((SEG, half), F32)
            for e in range(episodes):
                passed = place >= ends[b][e]
                row = b * episodes + e
                start_sin = jnp.where(passed, end_sin[row], start_sin)
                start_cos = jnp.where(passed, end_cos[row], start_cos)
            rows = pl.ds(pl.multiple_of(b * span + tile * SEG, SEG), SEG)
            xs[0, rows, 0:half] = here_sin * start_cos - here_cos * start_sin
            xs[0, rows, half:dims] = here_cos * start_cos + here_sin * start_sin
        return carry

    lax.fori_loop(0, tiles, marks, 0)

    def lowest(pair, carry):
        within = lax.rem(iota((8, groups * QRY), 1), QRY)
        first = base + pair * QRY - SEG
        place = within + (base + pair * QRY)
        for b in range(batch):
            low = jnp.where(within >= SEG, SEG, 0)
            for e in range(episodes):
                low = jnp.where(place >= ends[b][e], jnp.maximum(low, ends[b][e] - first), low)
            lows[b * pairs + pair] = jnp.maximum(low, -first)
        return carry

    lax.fori_loop(0, pairs, lowest, 0)

    def chunk_rows(c):
        return pl.ds(pl.multiple_of(c * ROWS, ROWS), ROWS)

    def kv_rows(c):
        return pl.ds(pl.multiple_of(lax.rem(c, per_seq) * ROWS + SEG, 16), ROWS)

    loads[0].wait()
    tb[0:vocab_all, :] = table_f[...].astype(BF)

    def onehot(c):
        code = toki[c, 0:1, :]
        act = toki[c, 1:2, :] + VOCAB
        ids = iota((OUTS, ROWS), 0)
        return jnp.where((ids == code) | (ids == act), 1.0, 0.0).astype(BF)

    def both_chunks(i):
        return (2 * i, 2 * i + 1)

    def embed(i, carry):
        for c in both_chunks(i):
            xs[0, chunk_rows(c), :] += dot_tn(onehot(c), tb[...])
        return carry

    lax.fori_loop(0, chunks // 2, embed, 0)

    lane_head = iota((1, dims), 1) // head_dim
    group_mask = [jnp.where(lane_head // 2 == g, 1.0, 0.0).astype(BF) for g in range(groups)]
    even_mask = jnp.where(lax.rem(lane_head, 2) == 0, 1.0, 0.0).astype(BF)
    odd_mask = jnp.where(lax.rem(lane_head, 2) == 1, 1.0, 0.0).astype(BF)
    even_f = lax.rem(lane_head, 2) == 0

    def by_group(rows):
        return jnp.concatenate([rows * group_mask[g] for g in range(groups)], axis=0)

    def both(keys):
        return jnp.concatenate([keys * even_mask, keys * odd_mask], axis=0)

    def gather_heads(wide):
        out = wide[0:QRY]
        for g in range(1, groups):
            out = jnp.where(lane_head // 2 == g, wide[g * QRY : g * QRY + QRY], out)
        return out

    def forward_copy(layer):
        return pltpu.make_async_remote_copy(
            src_ref=kvs.at[layer, :, pl.ds(span, SEG), :],
            dst_ref=kvs.at[layer, :, pl.ds(0, SEG), :],
            send_sem=send_sem.at[layer],
            recv_sem=recv_sem.at[layer],
            device_id={"seq": right},
            device_id_type=MESH,
        )

    def backward_copy(layer):
        return pltpu.make_async_remote_copy(
            src_ref=bsend.at[layer],
            dst_ref=brecv.at[layer],
            send_sem=send_sem.at[layers + layer],
            recv_sem=recv_sem.at[layers + layer],
            device_id={"seq": left},
            device_id_type=MESH,
        )

    def project(layer):
        gain = gains_ref[2 * layer : 2 * layer + 1, :]

        def body(i, carry):
            pieces = [(c, chunk_rows(c)) for c in both_chunks(i)]
            normed = [rms_apply(xs[2 * layer, rows, :], gain) for _, rows in pieces]
            wide = [dot_nn(h, wq[layer]).astype(BF) for h in normed]
            for (c, rows), h, qkv in zip(pieces, normed, wide):
                hs[2 * layer, rows, :] = h
                qs[layer, rows, :] = qkv[:, 0:dims]
                kvs[layer, c // per_seq, kv_rows(c), :] = qkv[:, dims:]
            return carry

        lax.fori_loop(0, chunks // 2, body, 0)

    def pair_rows(b, pair):
        return pl.ds(pl.multiple_of(b * span + pair * QRY, 16), QRY)

    def pair_window(pair):
        return pl.ds(pl.multiple_of(pair * QRY, 16), KEY)

    causal = iota((KEY, groups * QRY), 0) <= lax.rem(iota((KEY, groups * QRY), 1), QRY) + SEG
    key_place = iota((KEY, groups * QRY), 0)

    def attend(layer):
        copy = forward_copy(layer)

        def body(i, carry):
            items = [(b, pairs - 1 - 2 * i - j) for j in range(2) for b in range(batch)]
            pl.when(i == pairs // 2 - 1)(copy.wait)
            scores = []
            for b, pair in items:
                keys = kvs[layer, b, pair_window(pair), 0:dims]
                scores.append(dot_nt(both(keys), by_group(qs[layer, pair_rows(b, pair), :])))
            weights = []
            for (b, pair), score in zip(items, scores):
                seen = causal & (key_place >= lows[b * pairs + pair, 0:1, :])
                sides = []
                for side in range(2):
                    s = jnp.where(seen, score[side * KEY : side * KEY + KEY], NEG)
                    top = jnp.max(s, axis=0, keepdims=True)
                    e = jnp.exp2((s - top) * exp_scale)
                    sides.append((e * (1.0 / jnp.sum(e, axis=0, keepdims=True))).astype(BF))
                p = jnp.concatenate(sides, axis=0)
                probs[layer, b * pairs + pair] = p
                weights.append(p)
            for (b, pair), p in zip(items, weights):
                values = kvs[layer, b, pair_window(pair), dims:]
                wide = dot_tn(p, both(values))
                mixes[layer, pair_rows(b, pair), :] = gather_heads(wide).astype(BF)
            return carry

        copy.start()
        lax.fori_loop(0, pairs // 2, body, 0)

    def feed(layer):
        gain = gains_ref[2 * layer + 1 : 2 * layer + 2, :]
        c0, c1 = math.sqrt(2.0 / math.pi), 0.044715

        def body(i, carry):
            pieces = [chunk_rows(c) for c in both_chunks(i)]
            mids = [xs[2 * layer, rows, :] + dot_nn(mixes[layer, rows, :], wo[layer]) for rows in pieces]
            normed = [rms_apply(x, gain) for x in mids]
            for rows, x, h in zip(pieces, mids, normed):
                xs[2 * layer + 1, rows, :] = x
                hs[2 * layer + 1, rows, :] = h
            hidden = [[], []]
            for j in range(ff // 256):
                cols = slice(j * 256, j * 256 + 256)
                for rows, h, parts in zip(pieces, normed, hidden):
                    up = dot_nn(h, wu[layer, :, cols])
                    square = up * up
                    half_t = 0.5 + 0.5 * jnp.tanh(up * (c0 + (c0 * c1) * square))
                    act = up * half_t
                    slope = half_t + (1.0 - half_t) * act * (2.0 * c0 + (6.0 * c0 * c1) * square)
                    parts.append(act.astype(BF))
                    gds[layer, rows, cols] = slope.astype(BF)
            for rows, x, parts in zip(pieces, mids, hidden):
                act = jnp.concatenate(parts, axis=1)
                acts[layer, rows, :] = act
                xs[2 * layer + 2, rows, :] = x + dot_nn(act, wd[layer])
            return carry

        lax.fori_loop(0, chunks // 2, body, 0)

    per_layer = 4 + 2 * (ff // 256)
    for layer in range(layers):
        if layer == 0:
            convert(0, 3)
        project(layer)
        if layer == 0:
            ex.greeted()
        attend(layer)
        if layer == 0:
            convert(3, layers * per_layer)
        feed(layer)
    loads[1].wait()
    rt[0:outs_all, :] = readout_f[...].astype(BF)

    lossacc[...] = jnp.zeros_like(lossacc)
    dgain[...] = jnp.zeros_like(dgain)
    top_gain = gains_ref[2 * layers : 2 * layers + 1, :]

    def put(at, block):
        for side in range(2):
            cols = slice(side * 128, side * 128 + 128)
            grads_ref[side, at : at + block.shape[0], :] = block[:, cols].astype(BF)

    def loss_grad(c, outs):
        reward, cont = tokf[c, 0:1, :], tokf[c, 1:2, :]
        target, ret, valid = tokf[c, 2:3, :], tokf[c, 3:4, :], tokf[c, 4:5, :]
        action, code = toki[c, 1:2, :], toki[c, 2:3, :]
        logits = outs[0:VOCAB]
        top = jnp.max(logits, axis=0, keepdims=True)
        e = jnp.exp(logits - top)
        esum = jnp.sum(e, axis=0, keepdims=True)
        chosen = iota((VOCAB, ROWS), 0) == code
        picked = jnp.sum(jnp.where(chosen, logits, 0.0), axis=0, keepdims=True)
        loss = jnp.log(esum) + top - picked
        grad_logits = (e * (valid / esum) - jnp.where(chosen, valid, 0.0)).astype(BF)
        small = outs[VOCAB:OUTS]
        place = iota((OUTS - VOCAB, ROWS), 0)
        reward_err = small[0:1] - reward
        end_logit = small[1:2]
        value_err = small[2:3] - ret
        minus = jnp.exp(-jnp.abs(end_logit))
        soft = jnp.maximum(end_logit, 0.0) + jnp.log(1.0 + minus)
        sigmoid = jnp.where(end_logit >= 0.0, 1.0, minus) / (1.0 + minus)
        loss = loss + 0.5 * reward_err * reward_err + soft - cont * end_logit
        loss = loss + 0.5 * value_err * value_err
        actor = (place >= 3) & (place < outs_all - VOCAB)
        act_top = jnp.max(jnp.where(actor, small, NEG), axis=0, keepdims=True)
        act_e = jnp.where(actor, jnp.exp(jnp.where(actor, small - act_top, 0.0)), 0.0)
        act_sum = jnp.sum(act_e, axis=0, keepdims=True)
        log_pi = jnp.where(actor, small - act_top - jnp.log(act_sum), 0.0)
        pi = act_e / act_sum
        neg_entropy = jnp.sum(pi * log_pi, axis=0, keepdims=True)
        taken = place == action + 3
        picked_pi = jnp.sum(jnp.where(taken, log_pi, 0.0), axis=0, keepdims=True)
        gap = ret - target
        loss = loss - gap * picked_pi + ENTROPY_COEF * neg_entropy
        grad = gap * (pi - jnp.where(taken, 1.0, 0.0))
        grad = grad + ENTROPY_COEF * pi * (log_pi - neg_entropy)
        grad = jnp.where(actor, grad, 0.0)
        grad = jnp.where(place == 0, reward_err, grad)
        grad = jnp.where(place == 1, sigmoid - cont, grad)
        grad = jnp.where(place == 2, value_err, grad)
        lossacc[0:1, :] += loss * valid
        lossacc[1:2, :] += valid
        return jnp.concatenate([grad_logits, (grad * valid).astype(BF)], axis=0)

    def losses(i, carry):
        pieces = [(c, chunk_rows(c)) for c in both_chunks(i)]
        hidden = [xs[2 * layers, rows, :] for _, rows in pieces]
        normed = [rms_apply(x, top_gain) for x in hidden]
        outs = [dot_nt(rt[...], h) for h in normed]
        found = [loss_grad(c, out) for (c, _), out in zip(pieces, outs)]
        pulled = [dot_tn(grad, rt[...]) for grad in found]
        for (c, rows), x, h, grad, dh in zip(pieces, hidden, normed, found, pulled):
            hs[2 * layers, rows, :] = h
            gouts[:, rows] = grad
            grad_x, part = rms_pull(dh, x, top_gain)
            gx[rows, :] = grad_x
            gl[rows, :] = grad_x.astype(BF)
            dgain[2 * layers] += part
        return carry

    lax.fori_loop(0, chunks // 2, losses, 0)
    tail_at = VOCAB + layers * 12 * 256 + OUTS
    put(0, dot_nn(gouts[0:VOCAB, :], hs[2 * layers]))
    put(tail_at, dot_nn(gouts[VOCAB:OUTS, :], hs[2 * layers]))
    loss_total = jnp.sum(lossacc[0:1, :])
    count_total = jnp.sum(lossacc[1:2, :])
    place = iota(scal_ref.shape, 0)
    ex.tile_out[0, 0] = jnp.where(place == 0, loss_total, jnp.where(place == 1, count_total, 0.0))
    ex.begin(len(buckets))

    def spread(count, spent, body):
        plans = [ex.plan(spent / count) for _ in range(count)]

        def run(i, carry):
            body(i)
            for k, todo in enumerate(plans):
                if todo:
                    pl.when(i == k)(functools.partial(ex.run, todo))
            return carry

        lax.fori_loop(0, count, run, 0)

    def feed_back(layer):
        gain = gains_ref[2 * layer + 1 : 2 * layer + 2, :]

        def body(i):
            pieces = [chunk_rows(c) for c in both_chunks(i)]
            hidden = [[], []]
            for j in range(ff // 256):
                cols = slice(j * 256, j * 256 + 256)
                for rows, parts in zip(pieces, hidden):
                    da = dot_nt(gl[rows, :], wd[layer, cols, :])
                    parts.append((da * gds[layer, rows, cols].astype(F32)).astype(BF))
            hidden = [jnp.concatenate(parts, axis=1) for parts in hidden]
            pulled = [dot_nt(du, wu[layer]) for du in hidden]
            for rows, du, dh in zip(pieces, hidden, pulled):
                gds[layer, rows, :] = du
                grad_x, part = rms_pull(dh, xs[2 * layer + 1, rows, :], gain)
                dgain[2 * layer + 1] += part
                grad = gx[rows, :] + grad_x
                gx[rows, :] = grad
                low = grad.astype(BF)
                gl[rows, :] = low
                dmix[rows, :] = dot_nt(low, wo[layer]).astype(BF)

        spread(chunks // 2, 3.3, body)

    def attend_back(layer):
        def steps(i):
            items = [(b, 2 * i + j) for j in range(2) for b in range(batch)]
            keys, values, queries, douts = [], [], [], []
            for b, pair in items:
                window, rows = pair_window(pair), pair_rows(b, pair)
                keys.append(both(kvs[layer, b, window, 0:dims]))
                values.append(both(kvs[layer, b, window, dims:]))
                queries.append(by_group(qs[layer, rows, :]))
                douts.append(by_group(dmix[rows, :]))
            weights = [probs[layer, b * pairs + pair] for b, pair in items]
            pulled = [dot_nt(value, dout) for value, dout in zip(values, douts)]
            slopes = []
            for p, dp in zip(weights, pulled):
                sides = []
                for side in range(2):
                    part = slice(side * KEY, side * KEY + KEY)
                    pf = p[part].astype(F32)
                    d = dp[part]
                    sides.append((pf * (d - jnp.sum(d * pf, axis=0, keepdims=True))).astype(BF))
                slopes.append(jnp.concatenate(sides, axis=0))
            for (b, pair), ds, key in zip(items, slopes, keys):
                dqkv[pair_rows(b, pair), 0:dims] = (gather_heads(dot_tn(ds, key)) * scale).astype(BF)
            wide = []
            for ds, query, p, dout in zip(slopes, queries, weights, douts):
                dk = dot_nn(ds, query) * scale
                dv = dot_nn(p, dout)
                dk = jnp.where(even_f, dk[0:KEY], dk[KEY:])
                wide.append(jnp.concatenate([dk, jnp.where(even_f, dv[0:KEY], dv[KEY:])], axis=1))
            return items, wide

        def keep(items, wide):
            before = [carried[b] + wide[b][0:SEG] for b in range(batch)]
            for at, (b, pair) in enumerate(items):
                rows = pl.multiple_of(b * span + pair * QRY, 16)
                dqkv[pl.ds(rows, SEG), dims:] = wide[at][SEG:QRY].astype(BF)
                if at + batch < len(items):
                    ending = wide[at][QRY:] + wide[at + batch][0:SEG]
                    dqkv[pl.ds(pl.multiple_of(rows + SEG, 16), SEG), dims:] = ending.astype(BF)
                else:
                    carried[b] = wide[at][QRY:]
            return before

        copy = backward_copy(layer)

        def body(i):
            before = [rows.astype(BF) for rows in keep(*steps(i))]

            @pl.when(i == 0)
            def _():
                for b in range(batch):
                    bsend[layer, b] = before[b]
                copy.start()

            @pl.when(i > 0)
            def _():
                for b in range(batch):
                    rows = pl.ds(pl.multiple_of(b * span + i * 2 * QRY - SEG, 16), SEG)
                    dqkv[rows, dims:] = before[b]

        carried[...] = jnp.zeros_like(carried)
        spread(pairs // 2, 6.8, body)
        copy.wait()
        for b in range(batch):
            final = carried[b] + brecv[layer, b].astype(F32)
            dqkv[b * span + span - SEG : b * span + span, dims:] = final.astype(BF)

    def project_back(layer):
        gain = gains_ref[2 * layer : 2 * layer + 1, :]

        def body(i):
            pieces = [chunk_rows(c) for c in both_chunks(i)]
            pulled = [dot_nt(dqkv[rows, :], wq[layer]) for rows in pieces]
            for rows, dh in zip(pieces, pulled):
                grad_x, part = rms_pull(dh, xs[2 * layer, rows, :], gain)
                dgain[2 * layer] += part
                grad = gx[rows, :] + grad_x
                gx[rows, :] = grad
                gl[rows, :] = grad.astype(BF)

        spread(chunks // 2, 1.5, body)

    at = VOCAB
    bucket = 0
    for layer in reversed(range(layers)):
        for j in range(ff // 256):
            cols = slice(j * 256, j * 256 + 256)
            put(at, dot_tn(acts[layer, :, cols], gl[...]))
            at += 256
        ex.begin(bucket)
        ex.tick(1.2)
        feed_back(layer)
        for j in range(ff // 256):
            cols = slice(j * 256, j * 256 + 256)
            put(at, dot_tn(hs[2 * layer + 1], gds[layer, :, cols]))
            at += 256
            if j % 2:
                ex.tick(0.4)
        put(at, dot_tn(mixes[layer], gl[...]))
        at += 256
        ex.begin(bucket + 1)
        ex.tick(0.2)
        attend_back(layer)
        for j in range(3):
            cols = slice(j * 256, j * 256 + 256)
            put(at, dot_tn(hs[2 * layer], dqkv[:, cols]))
            at += 256
        bucket += 2
        if layer == 0:
            ex.begin(bucket)
        ex.tick(0.7)
        project_back(layer)

    def mark(c, carry):
        gouts[:, chunk_rows(c)] = onehot(c)
        return carry

    lax.fori_loop(0, chunks, mark, 0)
    put(at, dot_nn(gouts[...], gl[...]))
    ex.tick(1.6)
    at = tail_at + OUTS - VOCAB
    place = iota((16, dims), 0)
    gain_rows = jnp.zeros((16, dims), F32)
    for index in range(2 * layers + 1):
        gain_rows = jnp.where(place == index, jnp.sum(dgain[index], axis=0, keepdims=True), gain_rows)
    put(at, gain_rows)
    at += 16
    put(at, jnp.zeros((grads_ref.shape[1] - at, dims), F32))
    ex.begin(len(buckets) - 1)
    ex.drain()
    count = ex.tile_out[0, 3, 1:2, 0:1]
    norm = jnp.sqrt(jnp.sum(ex.tile_out[1, 3]) / (count * count))
    place = iota(scal_ref.shape, 0)
    scal = jnp.where(place == 2, norm, ex.tile_out[0, 3])
    scal_ref[...] = jnp.where(place == 3, jnp.minimum(1.0, CLIP_NORM / norm) / count, scal)
    for n in range(len(buckets)):
        ex.wait(ex.out_copies(n))


def gradients(codes, actions, next_codes, lengths, rewards, continues, values, weights, sizes):
    table, attn_in, attn_out, ffn_in, ffn_out, gains, readout = weights
    batch, span = codes.shape
    layers, dims, ff = ffn_in.shape
    total = batch * span
    tiles = span // SEG
    chunks = total // ROWS
    grad_rows = grad_row_count(layers)
    buckets = buckets_of(layers)
    seq_size, dp_size = sizes
    shares = [(b[1] - b[0]) // seq_size // owners_of(b, seq_size, dp_size // 2) for b in buckets]
    slots = exchange_slots(dp_size)
    hbm = pl.BlockSpec(memory_space=pltpu.HBM)
    steps = np.arange(lax.axis_size("seq") * tiles + 1, dtype=np.float64)[:, None]
    freq = np.exp(np.arange(dims // 2) * (-2.0 * math.log(10000.0) / dims))
    trig = np.zeros((steps.shape[0], 8, dims // 2), np.float32)
    trig[:, 0], trig[:, 1] = np.sin(steps * SEG * freq), np.cos(steps * SEG * freq)
    trig[:, 2], trig[:, 3] = np.sin(steps * freq), np.cos(steps * freq)
    trig = jnp.asarray(trig)
    vmem = pl.BlockSpec(memory_space=pltpu.VMEM)
    smem = pl.BlockSpec(memory_space=pltpu.SMEM)
    return pl.pallas_call(
        functools.partial(step_kernel, layers, sizes, buckets),
        out_shape=(
            jax.ShapeDtypeStruct((2, grad_rows, dims // 2), BF),
            jax.ShapeDtypeStruct((8, 128), F32),
        ),
        in_specs=[vmem] * 3 + [smem] + [vmem] * 4 + [hbm] * 5 + [vmem, hbm],
        out_specs=(hbm, vmem),
        scratch_shapes=[
            pltpu.VMEM((layers, dims, 3 * dims), BF),
            pltpu.VMEM((layers, dims, dims), BF),
            pltpu.VMEM((layers, dims, ff), BF),
            pltpu.VMEM((layers, ff, dims), BF),
            pltpu.VMEM((OUTS, dims), BF),
            pltpu.VMEM((OUTS, dims), BF),
            pltpu.VMEM((2 * layers + 1, total, dims), F32),
            pltpu.VMEM((2 * layers + 1, total, dims), BF),
            pltpu.VMEM((layers, total, dims), BF),
            pltpu.VMEM((layers, batch, SEG + span, 2 * dims), BF),
            pltpu.VMEM((layers, total // QRY, 2 * KEY, HEADS // 2 * QRY), BF),
            pltpu.VMEM((layers, total, ff), BF),
            pltpu.VMEM((layers, total, ff), BF),
            pltpu.VMEM((layers, total, dims), BF),
            pltpu.VMEM((total // QRY, 8, HEADS // 2 * QRY), jnp.int32),
            pltpu.VMEM((chunks, 8, ROWS), F32),
            pltpu.VMEM((chunks, 8, ROWS), jnp.int32),
            pltpu.VMEM((OUTS, total), BF),
            pltpu.VMEM((total, dims), F32),
            pltpu.VMEM((total, dims), BF),
            pltpu.VMEM((total, dims), BF),
            pltpu.VMEM((total, 3 * dims), BF),
            pltpu.VMEM((batch, SEG, 2 * dims), F32),
            pltpu.VMEM((2 * layers + 1, 8, dims), F32),
            pltpu.VMEM((8, ROWS), F32),
            pltpu.VMEM((4, 8, span), F32),
            pltpu.VMEM((layers, batch, SEG, 2 * dims), BF),
            pltpu.VMEM((layers, batch, SEG, 2 * dims), BF),
            pltpu.SemaphoreType.DMA((2 * layers,)),
            pltpu.SemaphoreType.DMA((2 * layers,)),
            pltpu.SemaphoreType.DMA((2 + 12 * layers,)),
            pltpu.VMEM(table.shape, F32),
            pltpu.VMEM(readout.shape, F32),
            pltpu.VMEM((2, grad_rows, dims // 2), BF),
            pltpu.VMEM((grad_rows, dims // 2), BF),
            pltpu.VMEM((seq_size - 1, grad_rows // seq_size, dims // 2), BF),
            pltpu.VMEM((grad_rows // seq_size, dims // 2), BF),
            pltpu.VMEM((dp_size // 2 - 1, sum(shares), dims // 2), BF),
            pltpu.VMEM((8, dims // 2), F32),
            pltpu.VMEM((2, 4, 8, 128), F32),
            pltpu.VMEM((2, slots // 2, 8, 128), F32),
            pltpu.SemaphoreType.DMA((len(buckets) + 2, slots)),
            pltpu.SemaphoreType.DMA((len(buckets) + 2, slots)),
            pltpu.SemaphoreType.DMA((len(buckets), 2)),
        ],
        compiler_params=pltpu.CompilerParams(
            collective_id=0, has_side_effects=True, vmem_limit_bytes=63 * 1024 * 1024
        ),
        name="train_step",
    )(
        codes,
        actions,
        next_codes,
        lengths,
        rewards,
        continues,
        values,
        trig,
        table,
        attn_in,
        attn_out,
        ffn_in,
        ffn_out,
        gains,
        readout,
    )


def adam_update(weight, first_mom, second_mom, clipped, rate):
    new_first = BETA_ONE * first_mom + (1.0 - BETA_ONE) * clipped
    new_second = BETA_TWO * second_mom + (1.0 - BETA_TWO) * clipped * clipped
    root = jnp.sqrt(new_second * (1.0 / (1.0 - BETA_TWO**STEP))) + ADAM_EPS
    ratio = new_first * (rate / (1.0 - BETA_ONE**STEP)) / root
    return (weight * (1.0 - rate * DECAY) - ratio, new_first, new_second)


AHEAD = 5


def update_kernel(layers, scal_ref, sums_ref, *refs):
    ins, outs, scalars, here = refs[0:21], refs[21:42], refs[42:45], refs[45:66]
    load_sem, store_sem, sum_sem, grads_ref = refs[66:]
    scale = scal_ref[3, 0]
    for k, ref in enumerate(scalars):
        ref[0, 0] = scal_ref[k, 0]
    pieces = [(slot, layer) for slot in (4, 3, 1, 2) for layer in range(layers)]
    pieces += [(0, None), (5, None), (6, None)]

    offset = VOCAB
    starts = {}
    for layer in reversed(range(layers)):
        starts[4, layer] = offset
        starts[3, layer] = offset + 4 * 256
        starts[2, layer] = offset + 8 * 256
        starts[1, layer] = offset + 9 * 256
        offset += 12 * 256
    table_at, tail_at = offset, offset + OUTS
    gains_at = tail_at + OUTS - VOCAB

    def view(ref, layer):
        return ref if layer is None else ref.at[layer]

    def moves(n, kind):
        slot, layer = pieces[n]
        for part in range(3):
            index = 3 * slot + part
            inside = view(here[index], layer)
            if kind == 0:
                yield pltpu.make_async_copy(view(ins[index], layer), inside, load_sem.at[n, part])
            else:
                yield pltpu.make_async_copy(inside, view(outs[index], layer), store_sem.at[n, part])

    def fetch(n):
        slot, layer = pieces[n]
        rows = {0: (table_at, OUTS), 6: (0, VOCAB), 5: (tail_at, sums_ref.shape[1] - tail_at)}
        if layer is not None:
            rows[slot] = (starts[slot, layer], here[3 * slot].shape[1] * here[3 * slot].shape[2] // 256)
        at, count = rows[slot]
        part = pl.ds(at, count)
        return pltpu.make_async_copy(sums_ref.at[:, part], grads_ref.at[:, part], sum_sem.at[n])

    def begin(n):
        for move in moves(n, 0):
            move.start()
        fetch(n).start()

    for n in range(AHEAD):
        begin(n)

    def renew(slot, layer, rows, cols, grad):
        refs = [view(here[3 * slot + part], layer) for part in range(3)]
        new = adam_update(*[ref[rows, cols] for ref in refs], grad.astype(F32) * scale, RATES[slot])
        for ref, value in zip(refs, new):
            ref[rows, cols] = value

    for n, (slot, layer) in enumerate(pieces):
        if n + AHEAD < len(pieces):
            begin(n + AHEAD)
        for move in moves(n, 0):
            move.wait()
        fetch(n).wait()
        if layer is not None:
            rows_all, cols_all = here[3 * slot].shape[1:]
            at = starts[slot, layer]
            for j in range(rows_all // 256):
                for i in range(cols_all // 256):
                    for side in range(2):
                        cols = slice(i * 256 + side * 128, i * 256 + side * 128 + 128)

                        def body(k, carry):
                            rows = pl.ds(pl.multiple_of(j * 256 + k * 64, 64), 64)
                            block = at + (j + i) * 256 + k * 64
                            grad = grads_ref[side, pl.ds(pl.multiple_of(block, 64), 64), :]
                            renew(slot, layer, rows, cols, grad)
                            return carry

                        lax.fori_loop(0, 4, body, 0)
        elif slot == 0:
            rows_all = here[0].shape[0]
            for side in range(2):
                cols = slice(side * 128, side * 128 + 128)

                def body(k, carry):
                    rows = pl.ds(pl.multiple_of(k * 64, 64), 64)
                    block = pl.ds(pl.multiple_of(table_at + k * 64, 64), 64)
                    renew(0, None, rows, cols, grads_ref[side, block, :])
                    return carry

                full = rows_all // 64
                lax.fori_loop(0, full, body, 0)
                if rows_all % 64:
                    last = slice(full * 64, rows_all)
                    block = grads_ref[side, table_at + full * 64 : tail_at, :]
                    renew(0, None, last, cols, block.astype(F32)[0 : rows_all % 64])
        elif slot == 6:
            outs_all = here[18].shape[0]
            for side in range(2):
                cols = slice(side * 128, side * 128 + 128)

                def body(k, carry):
                    rows = pl.ds(pl.multiple_of(k * 64, 64), 64)
                    renew(6, None, rows, cols, grads_ref[side, rows, :])
                    return carry

                lax.fori_loop(0, VOCAB // 64, body, 0)
                rest = grads_ref[side, tail_at : tail_at + OUTS - VOCAB, :].astype(F32)
                renew(6, None, slice(VOCAB, outs_all), cols, rest[0 : outs_all - VOCAB])
        else:
            count = here[15].shape[0]
            for side in range(2):
                cols = slice(side * 128, side * 128 + 128)
                grad = grads_ref[side, gains_at : gains_at + 16, :].astype(F32)[0:count]
                renew(5, None, slice(0, count), cols, grad)
        for move in moves(n, 1):
            move.start()
    for n in range(len(pieces)):
        for move in moves(n, 1):
            move.wait()


def update(grads, scal, state):
    layers = state[3].shape[0]
    anywhere = pl.BlockSpec(memory_space=pltpu.HBM)
    pieces = 4 * layers + 3
    return pl.pallas_call(
        functools.partial(update_kernel, layers),
        out_shape=tuple(jax.ShapeDtypeStruct(x.shape, F32) for x in state)
        + (jax.ShapeDtypeStruct((1, 1), F32),) * 3,
        in_specs=[
            pl.BlockSpec(memory_space=pltpu.SMEM),
            anywhere,
        ]
        + [anywhere] * 21,
        out_specs=(anywhere,) * 21 + (pl.BlockSpec(memory_space=pltpu.SMEM),) * 3,
        scratch_shapes=[pltpu.VMEM(x.shape, F32) for x in state]
        + [
            pltpu.SemaphoreType.DMA((pieces, 3)),
            pltpu.SemaphoreType.DMA((pieces, 3)),
            pltpu.SemaphoreType.DMA((pieces,)),
            pltpu.VMEM(grads.shape, BF),
        ],
        compiler_params=pltpu.CompilerParams(vmem_limit_bytes=62 * 1024 * 1024),
        name="update",
    )(scal, grads, *state)


def local(codes, actions, next_codes, lengths, rewards, continues, target_values, *state):
    state = state[0:18] + tuple(value.T for value in state[18:21])
    params = state[0::3]
    seq_size, dp_size = lax.axis_size("seq"), lax.axis_size("dp")
    sizes = (seq_size, dp_size)
    grads, scal = gradients(
        codes, actions, next_codes, lengths, rewards, continues, target_values, params, sizes
    )
    results = list(update(grads, scal, state))
    results[18:21] = [value.T for value in results[18:21]]
    results[21:24] = [value.reshape(()) for value in results[21:24]]
    return tuple(results)


def solution(mesh):
    rows, whole = P("dp", "seq"), P()
    return jax.shard_map(
        local,
        mesh=mesh,
        in_specs=(rows, rows, rows, P("dp", None), rows, rows, rows) + (whole,) * 21,
        out_specs=(whole,) * 24,
        check_vma=False,
    )
```

```python
import functools
import math

import jax
import jax.numpy as jnp
import numpy as np
from jax import lax
from jax.experimental import pallas as pl
from jax.experimental.pallas import tpu as pltpu
from jax.sharding import PartitionSpec as P

HEADS = 8
VOCAB = 512
SEG = 48
STEP = 5

EPS_NORM = 1e-06
BETA_ONE = 0.9
BETA_TWO = 0.999
RATES = (0.25, 0.02, 0.08, 0.02, 0.02, 0.25, 0.02)
DECAY = 0.01
ADAM_EPS = 1e-08
CLIP_NORM = 0.05
GAMMA = 0.985
LAMBDA_RET = 0.95
ENTROPY_COEF = 0.05

BF = jnp.bfloat16
F32 = jnp.float32
ROWS = 256
QRY = SEG
KEY = QRY + SEG
PER = 4
OUTS = 544
NEG = -1e30
MESH = pl.DeviceIdType.MESH
PER_ROW = 256 / 92e3
TRANSFERS = {
    "core": ("core", PER_ROW / 5.4, 1.1),
    "seq": ("seq", PER_ROW, 3.3),
    "deep": ("deep", PER_ROW / 2, 3.5),
    "tile": ("tile", 0.0, 3.6),
}
PATH = ("core", "seq", "deep", "back_deep", "back_seq", "back_core")
STAGE_TIME = 0.35


def dot_nn(left, right):
    return jnp.dot(left, right, preferred_element_type=F32)


def dot_tn(left, right):
    return lax.dot_general(left, right, (((0,), (0,)), ((), ())), preferred_element_type=F32)


def dot_nt(left, right):
    return lax.dot_general(left, right, (((1,), (1,)), ((), ())), preferred_element_type=F32)


def iota(shape, dim):
    return lax.broadcasted_iota(jnp.int32, shape, dim)


def rms_apply(x, gain):
    inv = lax.rsqrt(jnp.mean(x * x, axis=-1, keepdims=True) + EPS_NORM)
    return (x * inv * gain).astype(BF)


def rms_pull(grad, x, gain):
    inv = lax.rsqrt(jnp.mean(x * x, axis=-1, keepdims=True) + EPS_NORM)
    unit = x * inv
    weighted = grad * gain
    grad_x = inv * (weighted - unit * jnp.mean(weighted * unit, axis=-1, keepdims=True))
    rows, dims = x.shape
    return grad_x, jnp.sum((grad * unit).reshape(rows // 8, 8, dims), axis=0)


def grad_row_count(layers):
    rows = VOCAB + layers * 12 * 256 + OUTS + (OUTS - VOCAB) + 16
    return -(-rows // 256) * 256


def buckets_of(layers):
    cuts = [0, VOCAB + 4 * 256]
    for layer in range(layers):
        cuts.append(cuts[-1] + 5 * 256)
        cuts.append(cuts[-1] + (3 if layer == layers - 1 else 7) * 256)
    cuts.append(grad_row_count(layers))
    return list(zip(cuts[:-1], cuts[1:]))


def owners_of(bucket, seq_size, deep):
    quarter = (bucket[1] - bucket[0]) // seq_size
    return max(k for k in range(1, deep + 1) if quarter % (16 * k) == 0)


class Exchange:
    def __init__(self, seq_size, dp_size, buckets, grads, out, core_in, seq_in, seq_out, deep_in,
                 squares, tile_out, tile_in, send_sem, recv_sem, out_sem):
        self.deep = dp_size // 2
        self.seq_size = seq_size
        self.buckets = buckets
        self.grads, self.out = grads, out
        self.core_in, self.seq_in, self.seq_out, self.deep_in = core_in, seq_in, seq_out, deep_in
        self.squares = squares
        self.tile_out, self.tile_in = tile_out, tile_in
        self.send_sem, self.recv_sem, self.out_sem = send_sem, recv_sem, out_sem
        self.slots = exchange_slots(dp_size)
        me = lax.axis_index("seq")
        at_dp = lax.axis_index("dp")
        self.me, self.core, self.at_deep = me, lax.rem(at_dp, 2), lax.div(at_dp, 2)
        self.sibling = {"dp": self.at_deep * 2 + 1 - self.core}
        self.stage, self.due, self.free, self.now, self.summed = {}, {}, {}, 0.0, 0

    def deep_peer(self, k):
        return {"dp": lax.rem(self.at_deep + k, self.deep) * 2 + self.core}

    def peers(self):
        found = [self.sibling]
        found += [{"seq": lax.rem(self.me + k, self.seq_size)} for k in range(1, self.seq_size)]
        return found + [self.deep_peer(k) for k in range(1, self.deep)]

    def greet(self):
        for peer in self.peers():
            pl.semaphore_signal(
                pltpu.get_barrier_semaphore(), inc=1, device_id=peer, device_id_type=MESH
            )

    def greeted(self):
        pl.semaphore_wait(pltpu.get_barrier_semaphore(), len(self.peers()))

    def copy(self, src, dst, n, slot, peer):
        return pltpu.make_async_remote_copy(
            src_ref=src,
            dst_ref=dst,
            send_sem=self.send_sem.at[n, slot],
            recv_sem=self.recv_sem.at[n, slot],
            device_id=peer,
            device_id_type=MESH,
        )

    def only(self, n, index, act):
        owners = owners_of(self.buckets[n], self.seq_size, self.deep)
        if owners == self.deep:
            act()
        else:
            pl.when(index < owners)(act)

    def parts(self, n):
        r0, r1 = self.buckets[n]
        quarter = (r1 - r0) // self.seq_size
        return r0, r1 - r0, quarter, quarter // owners_of(self.buckets[n], self.seq_size, self.deep)

    def place(self, n, index):
        return lax.rem(index, owners_of(self.buckets[n], self.seq_size, self.deep))

    def deep_rows(self, n):
        at = sum(self.parts(k)[3] for k in range(n))
        return pl.ds(at, self.parts(n)[3])

    def quarter_rows(self, n, index):
        r0, _, quarter, _ = self.parts(n)
        return pl.ds(pl.multiple_of(r0 + index * quarter, 16), quarter)

    def packed_rows(self, n):
        r0, _, quarter, _ = self.parts(n)
        return pl.ds(r0 // self.seq_size, quarter)

    def share_rows(self, n, index):
        r0, _, _, share = self.parts(n)
        return pl.ds(pl.multiple_of(r0 // self.seq_size + index * share, 16), share)

    def own_rows(self, n):
        r0, _, quarter, share = self.parts(n)
        at = r0 + self.me * quarter + self.place(n, self.at_deep) * share
        return pl.ds(pl.multiple_of(at, 16), share)

    def blocks(self, n, index, work):
        r0, _, quarter, _ = self.parts(n)
        size = quarter // 2 if quarter > 256 else quarter
        for at in range(0, quarter, size):
            wide = pl.ds(pl.multiple_of(r0 + index * quarter + at, 16), size)
            work(wide, pl.ds(r0 // self.seq_size + at, size))

    def core_copies(self, n):
        r0, rows, _, _ = self.parts(n)
        part = pl.ds(r0, rows)
        return [self.copy(self.grads.at[1 - self.core, part], self.core_in.at[part], n, 0, self.sibling)]

    def seq_copies(self, n):
        packed = self.packed_rows(n)
        found = []
        for k in range(1, self.seq_size):
            peer = lax.rem(self.me + k, self.seq_size)
            source = self.core_in.at[self.quarter_rows(n, peer)]
            found.append(self.copy(source, self.seq_in.at[k - 1, packed], n, k, {"seq": peer}))
        return found

    def deep_copy(self, n, k):
        target = self.place(n, lax.rem(self.at_deep + k, self.deep))
        dest = self.deep_in.at[k - 1, self.deep_rows(n)]
        return self.copy(self.seq_out.at[self.share_rows(n, target)], dest, n, 3 + k, self.deep_peer(k))

    def back_copy(self, n, rows, slot, peer):
        there = self.grads.at[self.core, rows]
        return self.copy(there, there, n, self.slots // 2 + slot, peer)

    def back_seq(self, n):
        rows = self.quarter_rows(n, self.me)
        return [
            self.back_copy(n, rows, k, {"seq": lax.rem(self.me + k, self.seq_size)})
            for k in range(1, self.seq_size)
        ]

    def back_core(self, n):
        r0, rows, _, _ = self.parts(n)
        return [self.back_copy(n, pl.ds(r0, rows), 0, self.sibling)]

    def out_copies(self, n):
        r0, rows, _, _ = self.parts(n)
        part = pl.ds(r0, rows)
        return [
            pltpu.make_async_copy(self.grads.at[side, part], self.out.at[side, part], self.out_sem.at[n, side])
            for side in range(2)
        ]

    def start(self, copies):
        for copy in copies:
            copy.start()

    def wait(self, copies):
        for copy in copies:
            copy.wait()

    def own_sum(self, wide, packed):
        both = self.grads[self.core, wide, :].astype(F32) + self.core_in[wide, :].astype(F32)
        for k in range(self.seq_size - 1):
            both = both + self.seq_in[k, packed, :].astype(F32)
        return both

    def after_core(self, n):
        def work(wide, packed):
            both = self.grads[self.core, wide, :].astype(F32) + self.core_in[wide, :].astype(F32)
            self.core_in[wide, :] = both.astype(BF)

        for k in range(1, self.seq_size):
            self.blocks(n, lax.rem(self.me + k, self.seq_size), work)

    def after_seq(self, n):
        def work(wide, packed):
            self.seq_out[packed, :] = self.own_sum(wide, packed).astype(BF)

        self.blocks(n, self.me, work)

    def after_deep(self, n):
        share = self.parts(n)[3]

        def act():
            rows = self.own_rows(n)
            both = self.own_sum(rows, self.share_rows(n, self.place(n, self.at_deep)))
            part = self.deep_rows(n)
            for k in range(self.deep - 1):
                both = both + self.deep_in[k, part, :].astype(F32)
            self.grads[self.core, rows, :] = both.astype(BF)
            self.squares[...] += jnp.sum((both * both).reshape(share // 8, 8, both.shape[1]), axis=0)

        self.only(n, self.at_deep, act)

    def begin_deep(self, n):
        for k in range(1, self.deep):
            target = lax.rem(self.at_deep + k, self.deep)
            self.only(n, target, self.deep_copy(n, k).start)

    def end_deep(self, n):
        for k in range(1, self.deep):
            target = lax.rem(self.at_deep + k, self.deep)
            self.only(n, target, self.deep_copy(n, k).wait_send)

        def act():
            for k in range(1, self.deep):
                self.deep_copy(n, k).wait_recv()

        self.only(n, self.at_deep, act)

    def begin_back_deep(self, n):
        rows = self.own_rows(n)

        def act():
            for k in range(1, self.deep):
                self.back_copy(n, rows, 3 + k, self.deep_peer(k)).start()

        self.only(n, self.at_deep, act)

    def end_back_deep(self, n):
        rows = self.own_rows(n)

        def act():
            for k in range(1, self.deep):
                self.back_copy(n, rows, 3 + k, self.deep_peer(k)).wait_send()

        self.only(n, self.at_deep, act)
        for k in range(1, self.deep):
            origin = lax.rem(self.at_deep + self.deep - k, self.deep)
            self.only(n, origin, self.back_copy(n, rows, 3 + k, self.deep_peer(k)).wait_recv)

    def begin_transfer(self, n, name):
        if name == "deep":
            self.begin_deep(n)
        elif name == "back_deep":
            self.begin_back_deep(n)
        else:
            self.start(getattr(self, name if "back" in name else name + "_copies")(n))

    def end_transfer(self, n, name):
        if name == "deep":
            self.end_deep(n)
        elif name == "back_deep":
            self.end_back_deep(n)
        else:
            self.wait(getattr(self, name if "back" in name else name + "_copies")(n))
        if name == "core":
            self.after_core(n)
        elif name == "seq":
            self.after_seq(n)
        elif name == "deep":
            self.after_deep(n)
        elif name == "back_core":
            self.start(self.out_copies(n))

    def plan_launch(self, n):
        if n < len(self.buckets):
            name, rows = PATH[self.stage[n]], self.buckets[n][1] - self.buckets[n][0]
        else:
            name, rows = "tile", 0
        link, share, latency = TRANSFERS[name.replace("back_", "")]
        self.free[link] = max(self.now, self.free.get(link, 0.0)) + rows * share
        self.due[n] = self.free[link] + latency

    def plan_begin(self, n):
        self.stage[n] = 0
        self.plan_launch(n)
        return (n, None, 0)

    def plan_advance(self, n):
        step = self.stage[n]
        self.now = max(self.now, self.due.pop(n)) + STAGE_TIME
        self.stage[n] += 1
        last = (len(PATH) if n < len(self.buckets) else 3) - 1
        if step < last:
            self.plan_launch(n)
        todo = [(n, step, step + 1 if step < last else None)]
        if n < len(self.buckets):
            self.summed += PATH[step] == "deep"
        norm = len(self.buckets) + 1
        if self.summed == len(self.buckets) and norm not in self.stage:
            todo.append(self.plan_begin(norm))
        return todo

    def plan(self, spent):
        self.now += spent
        todo = []
        for n in sorted(self.due):
            if self.due[n] + 0.8 <= self.now:
                todo += self.plan_advance(n)
        return todo

    def run(self, todo):
        for n, ended, begun in todo:
            if n < len(self.buckets):
                if ended is not None:
                    self.end_transfer(n, PATH[ended])
                if begun is not None:
                    self.begin_transfer(n, PATH[begun])
            else:
                tile = n - len(self.buckets)
                if tile == 1 and ended is None:
                    self.tile_out[1, 0] = self.squares[...]
                if ended is not None:
                    self.tile_finish(tile, ended)
                if begun is not None:
                    self.tile_start(tile, begun)

    def begin(self, n):
        self.run([self.plan_begin(n)])

    def tick(self, spent):
        self.run(self.plan(spent))

    def drain(self):
        while self.due:
            self.run(self.plan_advance(min(self.due, key=lambda n: (self.due[n], n))))

    def tile_copies(self, tile, phase):
        if phase == 0:
            slots, peers = [0], [self.sibling]
        elif phase == 1:
            slots = list(range(1, self.seq_size))
            peers = [{"seq": lax.rem(self.me + k, self.seq_size)} for k in slots]
        else:
            slots = [3 + k for k in range(1, self.deep)]
            peers = [self.deep_peer(k) for k in range(1, self.deep)]
        n = len(self.buckets) + tile
        return [
            self.copy(self.tile_out.at[tile, phase], self.tile_in.at[tile, slot], n, slot, peer)
            for slot, peer in zip(slots, peers)
        ], slots

    def tile_start(self, tile, phase):
        self.start(self.tile_copies(tile, phase)[0])

    def tile_finish(self, tile, phase):
        copies, slots = self.tile_copies(tile, phase)
        self.wait(copies)
        both = self.tile_out[tile, phase]
        for slot in slots:
            both = both + self.tile_in[tile, slot]
        self.tile_out[tile, phase + 1] = both


def exchange_slots(dp_size):
    return 2 * (4 + dp_size // 2 - 1)


def step_kernel(
    layers,
    sizes,
    buckets,
    codes_ref,
    actions_ref,
    next_ref,
    lengths_ref,
    rewards_ref,
    continues_ref,
    values_ref,
    trig_ref,
    table_ref,
    attn_in_ref,
    attn_out_ref,
    ffn_in_ref,
    ffn_out_ref,
    gains_ref,
    readout_ref,
    out_ref,
    scal_ref,
    wq,
    wo,
    wu,
    wd,
    rt,
    tb,
    xs,
    hs,
    qs,
    kvs,
    probs,
    acts,
    gds,
    mixes,
    lows,
    tokf,
    toki,
    gouts,
    gx,
    gl,
    dmix,
    dqkv,
    carried,
    dgain,
    lossacc,
    lam,
    bsend,
    brecv,
    send_sem,
    recv_sem,
    load_sem,
    table_f,
    readout_f,
    grads_ref,
    *exchange_refs,
):
    batch, span = codes_ref.shape
    dims = gains_ref.shape[1]
    ff = ffn_in_ref.shape[2]
    tiles = span // SEG
    pairs = span // QRY
    total = batch * span
    chunks = total // ROWS
    per_seq = span // ROWS
    vocab_all = table_ref.shape[0]
    outs_all = readout_ref.shape[0]
    head_dim = dims // HEADS
    scale = head_dim ** (-0.5)
    exp_scale = scale * math.log2(math.e)
    groups = HEADS // 2
    base = lax.axis_index("seq") * span
    me = lax.axis_index("seq")
    seq_size = sizes[0]
    right = lax.rem(me + 1, seq_size)
    left = lax.rem(me + seq_size - 1, seq_size)

    ex = Exchange(*sizes, buckets, grads_ref, out_ref, *exchange_refs)
    ex.greet()
    ex.squares[...] = jnp.zeros_like(ex.squares)

    loads = [
        pltpu.make_async_copy(table_ref, table_f, load_sem.at[0]),
        pltpu.make_async_copy(readout_ref, readout_f, load_sem.at[1]),
    ]
    blocks = []
    for layer in range(layers):
        for j in range(3):
            blocks.append((attn_in_ref, wq, layer, slice(0, 256), slice(j * 256, j * 256 + 256)))
        blocks.append((attn_out_ref, wo, layer, slice(0, 256), slice(0, 256)))
        for j in range(ff // 256):
            blocks.append((ffn_in_ref, wu, layer, slice(0, 256), slice(j * 256, j * 256 + 256)))
        for j in range(ff // 256):
            blocks.append((ffn_out_ref, wd, layer, slice(j * 256, j * 256 + 256), slice(0, 256)))

    def place_of(k):
        at = (k + (2 * layers - 2) * chunks) % (2 * layers * chunks)
        return 1 + at // chunks, slice(256 * (at % chunks), 256 * (at % chunks) + 256)

    for k, (source, _, layer, rows, cols) in enumerate(blocks):
        plane, there = place_of(k)
        loads.append(
            pltpu.make_async_copy(source.at[layer, rows, cols], xs.at[plane, there, :], load_sem.at[2 + k])
        )
    for load in loads:
        load.start()

    def convert(low, high):
        for k in range(low, high):
            _, dest, layer, rows, cols = blocks[k]
            plane, there = place_of(k)
            loads[2 + k].wait()
            dest[layer, rows, cols] = xs[plane, there, :].astype(BF)

    tb[...] = jnp.zeros_like(tb)
    rt[...] = jnp.zeros_like(rt)

    ends = []
    for b in range(batch):
        run = jnp.int32(0)
        row = []
        for e in range(lengths_ref.shape[1]):
            run = run + lengths_ref[b, e]
            row.append(run)
        ends.append(row)
    episodes = len(ends[0])

    lane = iota((8, span), 1)
    lam[...] = jnp.zeros_like(lam)
    lam[0, 0:batch, :] = rewards_ref[...]
    lam[1, 0:batch, :] = continues_ref[...]
    lam[2, 0:batch, :] = values_ref[...]
    last = lax.rem(lane, SEG) == SEG - 1
    decay = GAMMA * lam[1]
    value_next = pltpu.roll(lam[2], span - 1, 1)
    add = jnp.where(last, lam[2], lam[0] + decay * ((1.0 - LAMBDA_RET) * value_next))
    mul = jnp.where(last, 0.0, decay * LAMBDA_RET)
    step = 1
    while step < SEG:
        add = add + mul * pltpu.roll(add, span - step, 1)
        mul = mul * pltpu.roll(mul, span - step, 1)
        step *= 2
    lam[3] = add
    valid_rows = []
    for b in range(batch):
        after = iota((1, span), 1) + (base + 1)
        final = after == ends[b][0]
        for e in range(1, episodes):
            final = final | (after == ends[b][e])
        valid_rows.append(jnp.where(final, 0.0, 1.0))
    for c in range(chunks):
        b = c // per_seq
        lanes = slice((c % per_seq) * ROWS, (c % per_seq) * ROWS + ROWS)
        for row in range(4):
            tokf[c, row : row + 1, :] = lam[row, b : b + 1, lanes]
        tokf[c, 4:5, :] = valid_rows[b][:, lanes]
        toki[c, 0:1, :] = codes_ref[b : b + 1, lanes]
        toki[c, 1:2, :] = actions_ref[b : b + 1, lanes]
        toki[c, 2:3, :] = next_ref[b : b + 1, lanes]

    half = dims // 2
    in_sin, in_cos = trig_ref[0:SEG, 2, :], trig_ref[0:SEG, 3, :]
    end_sin, end_cos = [], []
    for b in range(batch):
        for e in range(episodes):
            far, near = lax.div(ends[b][e], SEG), lax.rem(ends[b][e], SEG)
            far_sin, far_cos = trig_ref[far, 0:1, :], trig_ref[far, 1:2, :]
            near_sin, near_cos = trig_ref[near, 2:3, :], trig_ref[near, 3:4, :]
            end_sin.append(far_sin * near_cos + far_cos * near_sin)
            end_cos.append(far_cos * near_cos - far_sin * near_sin)

    def marks(tile, carry):
        at = me * tiles + tile
        tile_sin, tile_cos = trig_ref[at, 0:1, :], trig_ref[at, 1:2, :]
        here_sin = in_sin * tile_cos + in_cos * tile_sin
        here_cos = in_cos * tile_cos - in_sin * tile_sin
        place = iota((SEG, half), 0) + (base + tile * SEG)
        for b in range(batch):
            start_sin = jnp.zeros((SEG, half), F32)
            start_cos = jnp.ones((SEG, half), F32)
            for e in range(episodes):
                passed = place >= ends[b][e]
                row = b * episodes + e
                start_sin = jnp.where(passed, end_sin[row], start_sin)
                start_cos = jnp.where(passed, end_cos[row], start_cos)
            rows = pl.ds(pl.multiple_of(b * span + tile * SEG, SEG), SEG)
            xs[0, rows, 0:half] = here_sin * start_cos - here_cos * start_sin
            xs[0, rows, half:dims] = here_cos * start_cos + here_sin * start_sin
        return carry

    lax.fori_loop(0, tiles, marks, 0)

    def lowest(pair, carry):
        within = lax.rem(iota((8, groups * QRY), 1), QRY)
        first = base + pair * QRY - SEG
        place = within + (base + pair * QRY)
        for b in range(batch):
            low = jnp.where(within >= SEG, SEG, 0)
            for e in range(episodes):
                low = jnp.where(place >= ends[b][e], jnp.maximum(low, ends[b][e] - first), low)
            lows[b * pairs + pair] = jnp.maximum(low, -first)
        return carry

    lax.fori_loop(0, pairs, lowest, 0)

    def chunk_rows(c):
        return pl.ds(pl.multiple_of(c * ROWS, ROWS), ROWS)

    def kv_rows(c):
        return pl.ds(pl.multiple_of(lax.rem(c, per_seq) * ROWS + SEG, 16), ROWS)

    loads[0].wait()
    tb[0:vocab_all, :] = table_f[...].astype(BF)

    def onehot(c):
        code = toki[c, 0:1, :]
        act = toki[c, 1:2, :] + VOCAB
        ids = iota((OUTS, ROWS), 0)
        return jnp.where((ids == code) | (ids == act), 1.0, 0.0).astype(BF)

    def three_chunks(i):
        return tuple(3 * i + j for j in range(3))

    def embed(i, carry):
        for c in three_chunks(i):
            xs[0, chunk_rows(c), :] += dot_tn(onehot(c), tb[...])
        return carry

    lax.fori_loop(0, chunks // 3, embed, 0)

    lane_head = iota((1, dims), 1) // head_dim
    group_mask = [jnp.where(lane_head // 2 == g, 1.0, 0.0).astype(BF) for g in range(groups)]
    even_mask = jnp.where(lax.rem(lane_head, 2) == 0, 1.0, 0.0).astype(BF)
    odd_mask = jnp.where(lax.rem(lane_head, 2) == 1, 1.0, 0.0).astype(BF)
    even_f = lax.rem(lane_head, 2) == 0

    def by_group(rows):
        return jnp.concatenate([rows * group_mask[g] for g in range(groups)], axis=0)

    def both(keys):
        return jnp.concatenate([keys * even_mask, keys * odd_mask], axis=0)

    def gather_heads(wide):
        out = wide[0:QRY]
        for g in range(1, groups):
            out = jnp.where(lane_head // 2 == g, wide[g * QRY : g * QRY + QRY], out)
        return out

    def forward_copy(layer):
        return pltpu.make_async_remote_copy(
            src_ref=kvs.at[layer, :, pl.ds(span, SEG), :],
            dst_ref=kvs.at[layer, :, pl.ds(0, SEG), :],
            send_sem=send_sem.at[layer],
            recv_sem=recv_sem.at[layer],
            device_id={"seq": right},
            device_id_type=MESH,
        )

    def backward_copy(layer):
        return pltpu.make_async_remote_copy(
            src_ref=bsend.at[layer],
            dst_ref=brecv.at[layer],
            send_sem=send_sem.at[layers + layer],
            recv_sem=recv_sem.at[layers + layer],
            device_id={"seq": left},
            device_id_type=MESH,
        )

    def project(layer):
        gain = gains_ref[2 * layer : 2 * layer + 1, :]

        def body(i, carry):
            pieces = [(c, chunk_rows(c)) for c in three_chunks(i)]
            normed = [rms_apply(xs[2 * layer, rows, :], gain) for _, rows in pieces]
            wide = [dot_nn(h, wq[layer]).astype(BF) for h in normed]
            for (c, rows), h, qkv in zip(pieces, normed, wide):
                hs[2 * layer, rows, :] = h
                qs[layer, rows, :] = qkv[:, 0:dims]
                kvs[layer, c // per_seq, kv_rows(c), :] = qkv[:, dims:]
            return carry

        lax.fori_loop(0, chunks // 3, body, 0)

    def pair_rows(b, pair):
        return pl.ds(pl.multiple_of(b * span + pair * QRY, 16), QRY)

    def pair_window(pair):
        return pl.ds(pl.multiple_of(pair * QRY, 16), KEY)

    causal = iota((KEY, groups * QRY), 0) <= lax.rem(iota((KEY, groups * QRY), 1), QRY) + SEG
    key_place = iota((KEY, groups * QRY), 0)

    def attend(layer):
        copy = forward_copy(layer)

        def body(i, carry):
            items = [(b, pairs - 1 - PER * i - j) for j in range(PER) for b in range(batch)]
            pl.when(i == pairs // PER - 1)(copy.wait)
            scores = []
            for b, pair in items:
                keys = kvs[layer, b, pair_window(pair), 0:dims]
                scores.append(dot_nt(both(keys), by_group(qs[layer, pair_rows(b, pair), :])))
            weights = []
            for (b, pair), score in zip(items, scores):
                seen = causal & (key_place >= lows[b * pairs + pair, 0:1, :])
                sides = []
                for side in range(2):
                    s = jnp.where(seen, score[side * KEY : side * KEY + KEY], NEG)
                    top = jnp.max(s, axis=0, keepdims=True)
                    e = jnp.exp2((s - top) * exp_scale)
                    sides.append((e * (1.0 / jnp.sum(e, axis=0, keepdims=True))).astype(BF))
                p = jnp.concatenate(sides, axis=0)
                probs[layer, b * pairs + pair] = p
                weights.append(p)
            for (b, pair), p in zip(items, weights):
                values = kvs[layer, b, pair_window(pair), dims:]
                wide = dot_tn(p, both(values))
                mixes[layer, pair_rows(b, pair), :] = gather_heads(wide).astype(BF)
            return carry

        copy.start()
        lax.fori_loop(0, pairs // PER, body, 0)

    def feed(layer):
        gain = gains_ref[2 * layer + 1 : 2 * layer + 2, :]
        c0, c1 = math.sqrt(2.0 / math.pi), 0.044715

        def body(i, carry):
            pieces = [chunk_rows(c) for c in three_chunks(i)]
            mids = [xs[2 * layer, rows, :] + dot_nn(mixes[layer, rows, :], wo[layer]) for rows in pieces]
            normed = [rms_apply(x, gain) for x in mids]
            for rows, x, h in zip(pieces, mids, normed):
                xs[2 * layer + 1, rows, :] = x
                hs[2 * layer + 1, rows, :] = h
            hidden = [[], [], []]
            for j in range(ff // 256):
                cols = slice(j * 256, j * 256 + 256)
                for rows, h, parts in zip(pieces, normed, hidden):
                    up = dot_nn(h, wu[layer, :, cols])
                    square = up * up
                    half_t = 0.5 + 0.5 * jnp.tanh(up * (c0 + (c0 * c1) * square))
                    act = up * half_t
                    slope = half_t + (1.0 - half_t) * act * (2.0 * c0 + (6.0 * c0 * c1) * square)
                    parts.append(act.astype(BF))
                    gds[layer, rows, cols] = slope.astype(BF)
            for rows, x, parts in zip(pieces, mids, hidden):
                act = jnp.concatenate(parts, axis=1)
                acts[layer, rows, :] = act
                xs[2 * layer + 2, rows, :] = x + dot_nn(act, wd[layer])
            return carry

        lax.fori_loop(0, chunks // 3, body, 0)

    per_layer = 4 + 2 * (ff // 256)
    for layer in range(layers):
        if layer == 0:
            convert(0, 3)
        project(layer)
        if layer == 0:
            ex.greeted()
        attend(layer)
        if layer == 0:
            convert(3, layers * per_layer)
        feed(layer)
    loads[1].wait()
    rt[0:outs_all, :] = readout_f[...].astype(BF)

    lossacc[...] = jnp.zeros_like(lossacc)
    dgain[...] = jnp.zeros_like(dgain)
    top_gain = gains_ref[2 * layers : 2 * layers + 1, :]

    def put(at, block):
        for side in range(2):
            cols = slice(side * 128, side * 128 + 128)
            grads_ref[side, at : at + block.shape[0], :] = block[:, cols].astype(BF)

    def loss_grad(c, outs):
        reward, cont = tokf[c, 0:1, :], tokf[c, 1:2, :]
        target, ret, valid = tokf[c, 2:3, :], tokf[c, 3:4, :], tokf[c, 4:5, :]
        action, code = toki[c, 1:2, :], toki[c, 2:3, :]
        logits = outs[0:VOCAB]
        top = jnp.max(logits, axis=0, keepdims=True)
        e = jnp.exp(logits - top)
        esum = jnp.sum(e, axis=0, keepdims=True)
        chosen = iota((VOCAB, ROWS), 0) == code
        picked = jnp.sum(jnp.where(chosen, logits, 0.0), axis=0, keepdims=True)
        loss = jnp.log(esum) + top - picked
        grad_logits = (e * (valid / esum) - jnp.where(chosen, valid, 0.0)).astype(BF)
        small = outs[VOCAB:OUTS]
        place = iota((OUTS - VOCAB, ROWS), 0)
        reward_err = small[0:1] - reward
        end_logit = small[1:2]
        value_err = small[2:3] - ret
        minus = jnp.exp(-jnp.abs(end_logit))
        soft = jnp.maximum(end_logit, 0.0) + jnp.log(1.0 + minus)
        sigmoid = jnp.where(end_logit >= 0.0, 1.0, minus) / (1.0 + minus)
        loss = loss + 0.5 * reward_err * reward_err + soft - cont * end_logit
        loss = loss + 0.5 * value_err * value_err
        actor = (place >= 3) & (place < outs_all - VOCAB)
        act_top = jnp.max(jnp.where(actor, small, NEG), axis=0, keepdims=True)
        act_e = jnp.where(actor, jnp.exp(jnp.where(actor, small - act_top, 0.0)), 0.0)
        act_sum = jnp.sum(act_e, axis=0, keepdims=True)
        log_pi = jnp.where(actor, small - act_top - jnp.log(act_sum), 0.0)
        pi = act_e / act_sum
        neg_entropy = jnp.sum(pi * log_pi, axis=0, keepdims=True)
        taken = place == action + 3
        picked_pi = jnp.sum(jnp.where(taken, log_pi, 0.0), axis=0, keepdims=True)
        gap = ret - target
        loss = loss - gap * picked_pi + ENTROPY_COEF * neg_entropy
        grad = gap * (pi - jnp.where(taken, 1.0, 0.0))
        grad = grad + ENTROPY_COEF * pi * (log_pi - neg_entropy)
        grad = jnp.where(actor, grad, 0.0)
        grad = jnp.where(place == 0, reward_err, grad)
        grad = jnp.where(place == 1, sigmoid - cont, grad)
        grad = jnp.where(place == 2, value_err, grad)
        lossacc[0:1, :] += loss * valid
        lossacc[1:2, :] += valid
        return jnp.concatenate([grad_logits, (grad * valid).astype(BF)], axis=0)

    def losses(i, carry):
        pieces = [(c, chunk_rows(c)) for c in three_chunks(i)]
        hidden = [xs[2 * layers, rows, :] for _, rows in pieces]
        normed = [rms_apply(x, top_gain) for x in hidden]
        outs = [dot_nt(rt[...], h) for h in normed]
        found = [loss_grad(c, out) for (c, _), out in zip(pieces, outs)]
        pulled = [dot_tn(grad, rt[...]) for grad in found]
        for (c, rows), x, h, grad, dh in zip(pieces, hidden, normed, found, pulled):
            hs[2 * layers, rows, :] = h
            gouts[:, rows] = grad
            grad_x, part = rms_pull(dh, x, top_gain)
            gx[rows, :] = grad_x
            gl[rows, :] = grad_x.astype(BF)
            dgain[2 * layers] += part
        return carry

    lax.fori_loop(0, chunks // 3, losses, 0)
    tail_at = VOCAB + layers * 12 * 256 + OUTS
    put(0, dot_nn(gouts[0:VOCAB, :], hs[2 * layers]))
    put(tail_at, dot_nn(gouts[VOCAB:OUTS, :], hs[2 * layers]))
    loss_total = jnp.sum(lossacc[0:1, :])
    count_total = jnp.sum(lossacc[1:2, :])
    place = iota(scal_ref.shape, 0)
    ex.tile_out[0, 0] = jnp.where(place == 0, loss_total, jnp.where(place == 1, count_total, 0.0))
    ex.begin(len(buckets))

    def spread(count, spent, body):
        plans = [ex.plan(spent / count) for _ in range(count)]

        def run(i, carry):
            body(i)
            for k, todo in enumerate(plans):
                if todo:
                    pl.when(i == k)(functools.partial(ex.run, todo))
            return carry

        lax.fori_loop(0, count, run, 0)

    def feed_back(layer):
        gain = gains_ref[2 * layer + 1 : 2 * layer + 2, :]

        def body(i):
            pieces = [chunk_rows(c) for c in three_chunks(i)]
            hidden = [[], [], []]
            for j in range(ff // 256):
                cols = slice(j * 256, j * 256 + 256)
                for rows, parts in zip(pieces, hidden):
                    da = dot_nt(gl[rows, :], wd[layer, cols, :])
                    parts.append((da * gds[layer, rows, cols].astype(F32)).astype(BF))
            hidden = [jnp.concatenate(parts, axis=1) for parts in hidden]
            pulled = [dot_nt(du, wu[layer]) for du in hidden]
            for rows, du, dh in zip(pieces, hidden, pulled):
                gds[layer, rows, :] = du
                grad_x, part = rms_pull(dh, xs[2 * layer + 1, rows, :], gain)
                dgain[2 * layer + 1] += part
                grad = gx[rows, :] + grad_x
                gx[rows, :] = grad
                low = grad.astype(BF)
                gl[rows, :] = low
                dmix[rows, :] = dot_nt(low, wo[layer]).astype(BF)

        spread(chunks // 3, 3.3, body)

    def attend_back(layer):
        def steps(i):
            items = [(b, PER * i + j) for j in range(PER) for b in range(batch)]
            keys, values, queries, douts = [], [], [], []
            for b, pair in items:
                window, rows = pair_window(pair), pair_rows(b, pair)
                keys.append(both(kvs[layer, b, window, 0:dims]))
                values.append(both(kvs[layer, b, window, dims:]))
                queries.append(by_group(qs[layer, rows, :]))
                douts.append(by_group(dmix[rows, :]))
            weights = [probs[layer, b * pairs + pair] for b, pair in items]
            pulled = [dot_nt(value, dout) for value, dout in zip(values, douts)]
            slopes = []
            for p, dp in zip(weights, pulled):
                sides = []
                for side in range(2):
                    part = slice(side * KEY, side * KEY + KEY)
                    pf = p[part].astype(F32)
                    d = dp[part]
                    sides.append((pf * (d - jnp.sum(d * pf, axis=0, keepdims=True))).astype(BF))
                slopes.append(jnp.concatenate(sides, axis=0))
            for (b, pair), ds, key in zip(items, slopes, keys):
                dqkv[pair_rows(b, pair), 0:dims] = (gather_heads(dot_tn(ds, key)) * scale).astype(BF)
            wide = []
            for ds, query, p, dout in zip(slopes, queries, weights, douts):
                dk = dot_nn(ds, query) * scale
                dv = dot_nn(p, dout)
                dk = jnp.where(even_f, dk[0:KEY], dk[KEY:])
                wide.append(jnp.concatenate([dk, jnp.where(even_f, dv[0:KEY], dv[KEY:])], axis=1))
            return items, wide

        def keep(items, wide):
            before = [carried[b] + wide[b][0:SEG] for b in range(batch)]
            for at, (b, pair) in enumerate(items):
                rows = pl.multiple_of(b * span + pair * QRY, 16)
                if QRY > SEG:
                    dqkv[pl.ds(rows, QRY - SEG), dims:] = wide[at][SEG:QRY].astype(BF)
                if at + batch < len(items):
                    ending = wide[at][QRY:] + wide[at + batch][0:SEG]
                    dqkv[pl.ds(pl.multiple_of(rows + QRY - SEG, 16), SEG), dims:] = ending.astype(BF)
                else:
                    carried[b] = wide[at][QRY:]
            return before

        copy = backward_copy(layer)

        def body(i):
            before = [rows.astype(BF) for rows in keep(*steps(i))]

            @pl.when(i == 0)
            def _():
                for b in range(batch):
                    bsend[layer, b] = before[b]
                copy.start()

            @pl.when(i > 0)
            def _():
                for b in range(batch):
                    rows = pl.ds(pl.multiple_of(b * span + i * PER * QRY - SEG, 16), SEG)
                    dqkv[rows, dims:] = before[b]

        carried[...] = jnp.zeros_like(carried)
        spread(pairs // PER, 6.0, body)
        copy.wait()
        for b in range(batch):
            final = carried[b] + brecv[layer, b].astype(F32)
            dqkv[b * span + span - SEG : b * span + span, dims:] = final.astype(BF)

    def project_back(layer):
        gain = gains_ref[2 * layer : 2 * layer + 1, :]

        def body(i):
            pieces = [chunk_rows(c) for c in three_chunks(i)]
            pulled = [dot_nt(dqkv[rows, :], wq[layer]) for rows in pieces]
            for rows, dh in zip(pieces, pulled):
                grad_x, part = rms_pull(dh, xs[2 * layer, rows, :], gain)
                dgain[2 * layer] += part
                grad = gx[rows, :] + grad_x
                gx[rows, :] = grad
                gl[rows, :] = grad.astype(BF)

        spread(chunks // 3, 1.5, body)

    at = VOCAB
    bucket = 0
    for layer in reversed(range(layers)):
        for j in range(ff // 256):
            cols = slice(j * 256, j * 256 + 256)
            put(at, dot_tn(acts[layer, :, cols], gl[...]))
            at += 256
        ex.begin(bucket)
        ex.tick(1.2)
        feed_back(layer)
        for j in range(ff // 256):
            cols = slice(j * 256, j * 256 + 256)
            put(at, dot_tn(hs[2 * layer + 1], gds[layer, :, cols]))
            at += 256
            if j % 2:
                ex.tick(0.4)
        put(at, dot_tn(mixes[layer], gl[...]))
        at += 256
        ex.begin(bucket + 1)
        ex.tick(0.2)
        attend_back(layer)
        for j in range(3):
            cols = slice(j * 256, j * 256 + 256)
            put(at, dot_tn(hs[2 * layer], dqkv[:, cols]))
            at += 256
        bucket += 2
        if layer == 0:
            ex.begin(bucket)
        ex.tick(0.7)
        project_back(layer)

    def mark(c, carry):
        gouts[:, chunk_rows(c)] = onehot(c)
        return carry

    lax.fori_loop(0, chunks, mark, 0)
    put(at, dot_nn(gouts[...], gl[...]))
    ex.tick(1.6)
    at = tail_at + OUTS - VOCAB
    place = iota((16, dims), 0)
    gain_rows = jnp.zeros((16, dims), F32)
    for index in range(2 * layers + 1):
        gain_rows = jnp.where(place == index, jnp.sum(dgain[index], axis=0, keepdims=True), gain_rows)
    put(at, gain_rows)
    at += 16
    put(at, jnp.zeros((grads_ref.shape[1] - at, dims), F32))
    ex.begin(len(buckets) - 1)
    ex.drain()
    count = ex.tile_out[0, 3, 1:2, 0:1]
    norm = jnp.sqrt(jnp.sum(ex.tile_out[1, 3]) / (count * count))
    place = iota(scal_ref.shape, 0)
    scal = jnp.where(place == 2, norm, ex.tile_out[0, 3])
    scal_ref[...] = jnp.where(place == 3, jnp.minimum(1.0, CLIP_NORM / norm) / count, scal)
    for n in range(len(buckets)):
        ex.wait(ex.out_copies(n))


def gradients(codes, actions, next_codes, lengths, rewards, continues, values, weights, sizes):
    table, attn_in, attn_out, ffn_in, ffn_out, gains, readout = weights
    batch, span = codes.shape
    layers, dims, ff = ffn_in.shape
    total = batch * span
    tiles = span // SEG
    chunks = total // ROWS
    grad_rows = grad_row_count(layers)
    buckets = buckets_of(layers)
    seq_size, dp_size = sizes
    shares = [(b[1] - b[0]) // seq_size // owners_of(b, seq_size, dp_size // 2) for b in buckets]
    slots = exchange_slots(dp_size)
    hbm = pl.BlockSpec(memory_space=pltpu.HBM)
    steps = np.arange(lax.axis_size("seq") * tiles + 1, dtype=np.float64)[:, None]
    freq = np.exp(np.arange(dims // 2) * (-2.0 * math.log(10000.0) / dims))
    trig = np.zeros((steps.shape[0], 8, dims // 2), np.float32)
    trig[:, 0], trig[:, 1] = np.sin(steps * SEG * freq), np.cos(steps * SEG * freq)
    trig[:, 2], trig[:, 3] = np.sin(steps * freq), np.cos(steps * freq)
    trig = jnp.asarray(trig)
    vmem = pl.BlockSpec(memory_space=pltpu.VMEM)
    smem = pl.BlockSpec(memory_space=pltpu.SMEM)
    return pl.pallas_call(
        functools.partial(step_kernel, layers, sizes, buckets),
        out_shape=(
            jax.ShapeDtypeStruct((2, grad_rows, dims // 2), BF),
            jax.ShapeDtypeStruct((8, 128), F32),
        ),
        in_specs=[vmem] * 3 + [smem] + [vmem] * 4 + [hbm] * 5 + [vmem, hbm],
        out_specs=(hbm, vmem),
        scratch_shapes=[
            pltpu.VMEM((layers, dims, 3 * dims), BF),
            pltpu.VMEM((layers, dims, dims), BF),
            pltpu.VMEM((layers, dims, ff), BF),
            pltpu.VMEM((layers, ff, dims), BF),
            pltpu.VMEM((OUTS, dims), BF),
            pltpu.VMEM((OUTS, dims), BF),
            pltpu.VMEM((2 * layers + 1, total, dims), F32),
            pltpu.VMEM((2 * layers + 1, total, dims), BF),
            pltpu.VMEM((layers, total, dims), BF),
            pltpu.VMEM((layers, batch, SEG + span, 2 * dims), BF),
            pltpu.VMEM((layers, total // QRY, 2 * KEY, HEADS // 2 * QRY), BF),
            pltpu.VMEM((layers, total, ff), BF),
            pltpu.VMEM((layers, total, ff), BF),
            pltpu.VMEM((layers, total, dims), BF),
            pltpu.VMEM((total // QRY, 8, HEADS // 2 * QRY), jnp.int32),
            pltpu.VMEM((chunks, 8, ROWS), F32),
            pltpu.VMEM((chunks, 8, ROWS), jnp.int32),
            pltpu.VMEM((OUTS, total), BF),
            pltpu.VMEM((total, dims), F32),
            pltpu.VMEM((total, dims), BF),
            pltpu.VMEM((total, dims), BF),
            pltpu.VMEM((total, 3 * dims), BF),
            pltpu.VMEM((batch, SEG, 2 * dims), F32),
            pltpu.VMEM((2 * layers + 1, 8, dims), F32),
            pltpu.VMEM((8, ROWS), F32),
            pltpu.VMEM((4, 8, span), F32),
            pltpu.VMEM((layers, batch, SEG, 2 * dims), BF),
            pltpu.VMEM((layers, batch, SEG, 2 * dims), BF),
            pltpu.SemaphoreType.DMA((2 * layers,)),
            pltpu.SemaphoreType.DMA((2 * layers,)),
            pltpu.SemaphoreType.DMA((2 + 12 * layers,)),
            pltpu.VMEM(table.shape, F32),
            pltpu.VMEM(readout.shape, F32),
            pltpu.VMEM((2, grad_rows, dims // 2), BF),
            pltpu.VMEM((grad_rows, dims // 2), BF),
            pltpu.VMEM((seq_size - 1, grad_rows // seq_size, dims // 2), BF),
            pltpu.VMEM((grad_rows // seq_size, dims // 2), BF),
            pltpu.VMEM((dp_size // 2 - 1, sum(shares), dims // 2), BF),
            pltpu.VMEM((8, dims // 2), F32),
            pltpu.VMEM((2, 4, 8, 128), F32),
            pltpu.VMEM((2, slots // 2, 8, 128), F32),
            pltpu.SemaphoreType.DMA((len(buckets) + 2, slots)),
            pltpu.SemaphoreType.DMA((len(buckets) + 2, slots)),
            pltpu.SemaphoreType.DMA((len(buckets), 2)),
        ],
        compiler_params=pltpu.CompilerParams(
            collective_id=0, has_side_effects=True, vmem_limit_bytes=63 * 1024 * 1024
        ),
        name="train_step",
    )(
        codes,
        actions,
        next_codes,
        lengths,
        rewards,
        continues,
        values,
        trig,
        table,
        attn_in,
        attn_out,
        ffn_in,
        ffn_out,
        gains,
        readout,
    )


def adam_update(weight, first_mom, second_mom, clipped, rate):
    new_first = BETA_ONE * first_mom + (1.0 - BETA_ONE) * clipped
    new_second = BETA_TWO * second_mom + (1.0 - BETA_TWO) * clipped * clipped
    root = jnp.sqrt(new_second * (1.0 / (1.0 - BETA_TWO**STEP))) + ADAM_EPS
    ratio = new_first * (rate / (1.0 - BETA_ONE**STEP)) / root
    return (weight * (1.0 - rate * DECAY) - ratio, new_first, new_second)


AHEAD = 5


def update_kernel(layers, scal_ref, sums_ref, *refs):
    ins, outs, scalars, here = refs[0:21], refs[21:42], refs[42:45], refs[45:66]
    load_sem, store_sem, sum_sem, grads_ref = refs[66:]
    scale = scal_ref[3, 0]
    for k, ref in enumerate(scalars):
        ref[0, 0] = scal_ref[k, 0]
    pieces = [(slot, layer) for slot in (4, 3, 1, 2) for layer in range(layers)]
    pieces += [(0, None), (5, None), (6, None)]

    offset = VOCAB
    starts = {}
    for layer in reversed(range(layers)):
        starts[4, layer] = offset
        starts[3, layer] = offset + 4 * 256
        starts[2, layer] = offset + 8 * 256
        starts[1, layer] = offset + 9 * 256
        offset += 12 * 256
    table_at, tail_at = offset, offset + OUTS
    gains_at = tail_at + OUTS - VOCAB

    def view(ref, layer):
        return ref if layer is None else ref.at[layer]

    def moves(n, kind):
        slot, layer = pieces[n]
        for part in range(3):
            index = 3 * slot + part
            inside = view(here[index], layer)
            if kind == 0:
                yield pltpu.make_async_copy(view(ins[index], layer), inside, load_sem.at[n, part])
            else:
                yield pltpu.make_async_copy(inside, view(outs[index], layer), store_sem.at[n, part])

    def fetch(n):
        slot, layer = pieces[n]
        rows = {0: (table_at, OUTS), 6: (0, VOCAB), 5: (tail_at, sums_ref.shape[1] - tail_at)}
        if layer is not None:
            rows[slot] = (starts[slot, layer], here[3 * slot].shape[1] * here[3 * slot].shape[2] // 256)
        at, count = rows[slot]
        part = pl.ds(at, count)
        return pltpu.make_async_copy(sums_ref.at[:, part], grads_ref.at[:, part], sum_sem.at[n])

    def begin(n):
        for move in moves(n, 0):
            move.start()
        fetch(n).start()

    for n in range(AHEAD):
        begin(n)

    def renew(slot, layer, rows, cols, grad):
        refs = [view(here[3 * slot + part], layer) for part in range(3)]
        new = adam_update(*[ref[rows, cols] for ref in refs], grad.astype(F32) * scale, RATES[slot])
        for ref, value in zip(refs, new):
            ref[rows, cols] = value

    for n, (slot, layer) in enumerate(pieces):
        if n + AHEAD < len(pieces):
            begin(n + AHEAD)
        for move in moves(n, 0):
            move.wait()
        fetch(n).wait()
        if layer is not None:
            rows_all, cols_all = here[3 * slot].shape[1:]
            at = starts[slot, layer]
            for j in range(rows_all // 256):
                for i in range(cols_all // 256):
                    for side in range(2):
                        cols = slice(i * 256 + side * 128, i * 256 + side * 128 + 128)

                        def body(k, carry):
                            rows = pl.ds(pl.multiple_of(j * 256 + k * 64, 64), 64)
                            block = at + (j + i) * 256 + k * 64
                            grad = grads_ref[side, pl.ds(pl.multiple_of(block, 64), 64), :]
                            renew(slot, layer, rows, cols, grad)
                            return carry

                        lax.fori_loop(0, 4, body, 0)
        elif slot == 0:
            rows_all = here[0].shape[0]
            for side in range(2):
                cols = slice(side * 128, side * 128 + 128)

                def body(k, carry):
                    rows = pl.ds(pl.multiple_of(k * 64, 64), 64)
                    block = pl.ds(pl.multiple_of(table_at + k * 64, 64), 64)
                    renew(0, None, rows, cols, grads_ref[side, block, :])
                    return carry

                full = rows_all // 64
                lax.fori_loop(0, full, body, 0)
                if rows_all % 64:
                    last = slice(full * 64, rows_all)
                    block = grads_ref[side, table_at + full * 64 : tail_at, :]
                    renew(0, None, last, cols, block.astype(F32)[0 : rows_all % 64])
        elif slot == 6:
            outs_all = here[18].shape[0]
            for side in range(2):
                cols = slice(side * 128, side * 128 + 128)

                def body(k, carry):
                    rows = pl.ds(pl.multiple_of(k * 64, 64), 64)
                    renew(6, None, rows, cols, grads_ref[side, rows, :])
                    return carry

                lax.fori_loop(0, VOCAB // 64, body, 0)
                rest = grads_ref[side, tail_at : tail_at + OUTS - VOCAB, :].astype(F32)
                renew(6, None, slice(VOCAB, outs_all), cols, rest[0 : outs_all - VOCAB])
        else:
            count = here[15].shape[0]
            for side in range(2):
                cols = slice(side * 128, side * 128 + 128)
                grad = grads_ref[side, gains_at : gains_at + 16, :].astype(F32)[0:count]
                renew(5, None, slice(0, count), cols, grad)
        for move in moves(n, 1):
            move.start()
    for n in range(len(pieces)):
        for move in moves(n, 1):
            move.wait()


def update(grads, scal, state):
    layers = state[3].shape[0]
    anywhere = pl.BlockSpec(memory_space=pltpu.HBM)
    pieces = 4 * layers + 3
    return pl.pallas_call(
        functools.partial(update_kernel, layers),
        out_shape=tuple(jax.ShapeDtypeStruct(x.shape, F32) for x in state)
        + (jax.ShapeDtypeStruct((1, 1), F32),) * 3,
        in_specs=[
            pl.BlockSpec(memory_space=pltpu.SMEM),
            anywhere,
        ]
        + [anywhere] * 21,
        out_specs=(anywhere,) * 21 + (pl.BlockSpec(memory_space=pltpu.SMEM),) * 3,
        scratch_shapes=[pltpu.VMEM(x.shape, F32) for x in state]
        + [
            pltpu.SemaphoreType.DMA((pieces, 3)),
            pltpu.SemaphoreType.DMA((pieces, 3)),
            pltpu.SemaphoreType.DMA((pieces,)),
            pltpu.VMEM(grads.shape, BF),
        ],
        compiler_params=pltpu.CompilerParams(vmem_limit_bytes=62 * 1024 * 1024),
        name="update",
    )(scal, grads, *state)


def local(codes, actions, next_codes, lengths, rewards, continues, target_values, *state):
    state = state[0:18] + tuple(value.T for value in state[18:21])
    params = state[0::3]
    seq_size, dp_size = lax.axis_size("seq"), lax.axis_size("dp")
    sizes = (seq_size, dp_size)
    grads, scal = gradients(
        codes, actions, next_codes, lengths, rewards, continues, target_values, params, sizes
    )
    results = list(update(grads, scal, state))
    results[18:21] = [value.T for value in results[18:21]]
    results[21:24] = [value.reshape(()) for value in results[21:24]]
    return tuple(results)


def solution(mesh):
    rows, whole = P("dp", "seq"), P()
    return jax.shard_map(
        local,
        mesh=mesh,
        in_specs=(rows, rows, rows, P("dp", None), rows, rows, rows) + (whole,) * 21,
        out_specs=(whole,) * 24,
        check_vma=False,
    )
```

```python
import functools
import math

import jax
import jax.numpy as jnp
import numpy as np
from jax import lax
from jax.experimental import pallas as pl
from jax.experimental.pallas import tpu as pltpu
from jax.sharding import PartitionSpec as P

HEADS = 8
VOCAB = 512
SEG = 48
STEP = 5

EPS_NORM = 1e-06
BETA_ONE = 0.9
BETA_TWO = 0.999
RATES = (0.25, 0.02, 0.08, 0.02, 0.02, 0.25, 0.02)
DECAY = 0.01
ADAM_EPS = 1e-08
CLIP_NORM = 0.05
GAMMA = 0.985
LAMBDA_RET = 0.95
ENTROPY_COEF = 0.05

BF = jnp.bfloat16
F32 = jnp.float32
ROWS = 256
QRY = SEG
KEY = QRY + SEG
PER = 4
OUTS = 544
NEG = -1e30
MESH = pl.DeviceIdType.MESH
PER_ROW = 256 / 92e3
TRANSFERS = {
    "core": ("core", PER_ROW / 5.4, 1.1),
    "seq": ("seq", PER_ROW, 3.3),
    "deep": ("deep", PER_ROW / 2, 3.5),
    "tile": ("tile", 0.0, 3.6),
}
PATH = ("core", "seq", "deep", "back_deep", "back_seq", "back_core")
STAGE_TIME = 0.35


def dot_nn(left, right):
    return jnp.dot(left, right, preferred_element_type=F32)


def dot_tn(left, right):
    return lax.dot_general(left, right, (((0,), (0,)), ((), ())), preferred_element_type=F32)


def dot_nt(left, right):
    return lax.dot_general(left, right, (((1,), (1,)), ((), ())), preferred_element_type=F32)


def iota(shape, dim):
    return lax.broadcasted_iota(jnp.int32, shape, dim)


def rms_apply(x, gain):
    inv = lax.rsqrt(jnp.mean(x * x, axis=-1, keepdims=True) + EPS_NORM)
    return (x * inv * gain).astype(BF)


def rms_pull(grad, x, gain):
    inv = lax.rsqrt(jnp.mean(x * x, axis=-1, keepdims=True) + EPS_NORM)
    unit = x * inv
    weighted = grad * gain
    grad_x = inv * (weighted - unit * jnp.mean(weighted * unit, axis=-1, keepdims=True))
    rows, dims = x.shape
    return grad_x, jnp.sum((grad * unit).reshape(rows // 8, 8, dims), axis=0)


def grad_row_count(layers):
    rows = VOCAB + layers * 12 * 256 + OUTS + (OUTS - VOCAB) + 16
    return -(-rows // 256) * 256


def buckets_of(layers):
    cuts = [0, VOCAB + 4 * 256]
    for layer in range(layers):
        cuts.append(cuts[-1] + 5 * 256)
        cuts.append(cuts[-1] + (3 if layer == layers - 1 else 7) * 256)
    cuts.append(grad_row_count(layers))
    return list(zip(cuts[:-1], cuts[1:]))


def owners_of(bucket, seq_size, deep):
    quarter = (bucket[1] - bucket[0]) // seq_size
    return max(k for k in range(1, deep + 1) if quarter % (16 * k) == 0)


class Exchange:
    def __init__(self, seq_size, dp_size, buckets, grads, out, core_in, seq_in, seq_out, deep_in,
                 squares, tile_out, tile_in, send_sem, recv_sem, out_sem):
        self.deep = dp_size // 2
        self.seq_size = seq_size
        self.buckets = buckets
        self.grads, self.out = grads, out
        self.core_in, self.seq_in, self.seq_out, self.deep_in = core_in, seq_in, seq_out, deep_in
        self.squares = squares
        self.tile_out, self.tile_in = tile_out, tile_in
        self.send_sem, self.recv_sem, self.out_sem = send_sem, recv_sem, out_sem
        self.slots = exchange_slots(dp_size)
        me = lax.axis_index("seq")
        at_dp = lax.axis_index("dp")
        self.me, self.core, self.at_deep = me, lax.rem(at_dp, 2), lax.div(at_dp, 2)
        self.sibling = {"dp": self.at_deep * 2 + 1 - self.core}
        self.stage, self.due, self.free, self.now, self.summed = {}, {}, {}, 0.0, 0

    def deep_peer(self, k):
        return {"dp": lax.rem(self.at_deep + k, self.deep) * 2 + self.core}

    def peers(self):
        found = [self.sibling]
        found += [{"seq": lax.rem(self.me + k, self.seq_size)} for k in range(1, self.seq_size)]
        return found + [self.deep_peer(k) for k in range(1, self.deep)]

    def greet(self):
        for peer in self.peers():
            pl.semaphore_signal(
                pltpu.get_barrier_semaphore(), inc=1, device_id=peer, device_id_type=MESH
            )

    def greeted(self):
        pl.semaphore_wait(pltpu.get_barrier_semaphore(), len(self.peers()))

    def copy(self, src, dst, n, slot, peer):
        return pltpu.make_async_remote_copy(
            src_ref=src,
            dst_ref=dst,
            send_sem=self.send_sem.at[n, slot],
            recv_sem=self.recv_sem.at[n, slot],
            device_id=peer,
            device_id_type=MESH,
        )

    def only(self, n, index, act):
        owners = owners_of(self.buckets[n], self.seq_size, self.deep)
        if owners == self.deep:
            act()
        else:
            pl.when(index < owners)(act)

    def parts(self, n):
        r0, r1 = self.buckets[n]
        quarter = (r1 - r0) // self.seq_size
        return r0, r1 - r0, quarter, quarter // owners_of(self.buckets[n], self.seq_size, self.deep)

    def place(self, n, index):
        return lax.rem(index, owners_of(self.buckets[n], self.seq_size, self.deep))

    def deep_rows(self, n):
        at = sum(self.parts(k)[3] for k in range(n))
        return pl.ds(at, self.parts(n)[3])

    def quarter_rows(self, n, index):
        r0, _, quarter, _ = self.parts(n)
        return pl.ds(pl.multiple_of(r0 + index * quarter, 16), quarter)

    def packed_rows(self, n):
        r0, _, quarter, _ = self.parts(n)
        return pl.ds(r0 // self.seq_size, quarter)

    def share_rows(self, n, index):
        r0, _, _, share = self.parts(n)
        return pl.ds(pl.multiple_of(r0 // self.seq_size + index * share, 16), share)

    def own_rows(self, n):
        r0, _, quarter, share = self.parts(n)
        at = r0 + self.me * quarter + self.place(n, self.at_deep) * share
        return pl.ds(pl.multiple_of(at, 16), share)

    def blocks(self, n, index, work):
        r0, _, quarter, _ = self.parts(n)
        size = quarter // 2 if quarter > 256 else quarter
        for at in range(0, quarter, size):
            wide = pl.ds(pl.multiple_of(r0 + index * quarter + at, 16), size)
            work(wide, pl.ds(r0 // self.seq_size + at, size))

    def core_copies(self, n):
        r0, rows, _, _ = self.parts(n)
        part = pl.ds(r0, rows)
        return [self.copy(self.grads.at[1 - self.core, part], self.core_in.at[part], n, 0, self.sibling)]

    def seq_copies(self, n):
        packed = self.packed_rows(n)
        found = []
        for k in range(1, self.seq_size):
            peer = lax.rem(self.me + k, self.seq_size)
            source = self.core_in.at[self.quarter_rows(n, peer)]
            found.append(self.copy(source, self.seq_in.at[k - 1, packed], n, k, {"seq": peer}))
        return found

    def deep_copy(self, n, k):
        target = self.place(n, lax.rem(self.at_deep + k, self.deep))
        dest = self.deep_in.at[k - 1, self.deep_rows(n)]
        return self.copy(self.seq_out.at[self.share_rows(n, target)], dest, n, 3 + k, self.deep_peer(k))

    def back_copy(self, n, rows, slot, peer):
        there = self.grads.at[self.core, rows]
        return self.copy(there, there, n, self.slots // 2 + slot, peer)

    def back_seq(self, n):
        rows = self.quarter_rows(n, self.me)
        return [
            self.back_copy(n, rows, k, {"seq": lax.rem(self.me + k, self.seq_size)})
            for k in range(1, self.seq_size)
        ]

    def back_core(self, n):
        r0, rows, _, _ = self.parts(n)
        return [self.back_copy(n, pl.ds(r0, rows), 0, self.sibling)]

    def out_copies(self, n):
        r0, rows, _, _ = self.parts(n)
        part = pl.ds(r0, rows)
        return [
            pltpu.make_async_copy(self.grads.at[side, part], self.out.at[side, part], self.out_sem.at[n, side])
            for side in range(2)
        ]

    def start(self, copies):
        for copy in copies:
            copy.start()

    def wait(self, copies):
        for copy in copies:
            copy.wait()

    def own_sum(self, wide, packed):
        both = self.grads[self.core, wide, :].astype(F32) + self.core_in[wide, :].astype(F32)
        for k in range(self.seq_size - 1):
            both = both + self.seq_in[k, packed, :].astype(F32)
        return both

    def after_core(self, n):
        def work(wide, packed):
            both = self.grads[self.core, wide, :].astype(F32) + self.core_in[wide, :].astype(F32)
            self.core_in[wide, :] = both.astype(BF)

        for k in range(1, self.seq_size):
            self.blocks(n, lax.rem(self.me + k, self.seq_size), work)

    def after_seq(self, n):
        def work(wide, packed):
            self.seq_out[packed, :] = self.own_sum(wide, packed).astype(BF)

        self.blocks(n, self.me, work)

    def after_deep(self, n):
        share = self.parts(n)[3]

        def act():
            rows = self.own_rows(n)
            both = self.own_sum(rows, self.share_rows(n, self.place(n, self.at_deep)))
            part = self.deep_rows(n)
            for k in range(self.deep - 1):
                both = both + self.deep_in[k, part, :].astype(F32)
            self.grads[self.core, rows, :] = both.astype(BF)
            self.squares[...] += jnp.sum((both * both).reshape(share // 8, 8, both.shape[1]), axis=0)

        self.only(n, self.at_deep, act)

    def begin_deep(self, n):
        for k in range(1, self.deep):
            target = lax.rem(self.at_deep + k, self.deep)
            self.only(n, target, self.deep_copy(n, k).start)

    def end_deep(self, n):
        for k in range(1, self.deep):
            target = lax.rem(self.at_deep + k, self.deep)
            self.only(n, target, self.deep_copy(n, k).wait_send)

        def act():
            for k in range(1, self.deep):
                self.deep_copy(n, k).wait_recv()

        self.only(n, self.at_deep, act)

    def begin_back_deep(self, n):
        rows = self.own_rows(n)

        def act():
            for k in range(1, self.deep):
                self.back_copy(n, rows, 3 + k, self.deep_peer(k)).start()

        self.only(n, self.at_deep, act)

    def end_back_deep(self, n):
        rows = self.own_rows(n)

        def act():
            for k in range(1, self.deep):
                self.back_copy(n, rows, 3 + k, self.deep_peer(k)).wait_send()

        self.only(n, self.at_deep, act)
        for k in range(1, self.deep):
            origin = lax.rem(self.at_deep + self.deep - k, self.deep)
            self.only(n, origin, self.back_copy(n, rows, 3 + k, self.deep_peer(k)).wait_recv)

    def begin_transfer(self, n, name):
        if name == "deep":
            self.begin_deep(n)
        elif name == "back_deep":
            self.begin_back_deep(n)
        else:
            self.start(getattr(self, name if "back" in name else name + "_copies")(n))

    def end_transfer(self, n, name):
        if name == "deep":
            self.end_deep(n)
        elif name == "back_deep":
            self.end_back_deep(n)
        else:
            self.wait(getattr(self, name if "back" in name else name + "_copies")(n))
        if name == "core":
            self.after_core(n)
        elif name == "seq":
            self.after_seq(n)
        elif name == "deep":
            self.after_deep(n)
        elif name == "back_core":
            self.start(self.out_copies(n))

    def plan_launch(self, n):
        if n < len(self.buckets):
            name, rows = PATH[self.stage[n]], self.buckets[n][1] - self.buckets[n][0]
        else:
            name, rows = "tile", 0
        link, share, latency = TRANSFERS[name.replace("back_", "")]
        self.free[link] = max(self.now, self.free.get(link, 0.0)) + rows * share
        self.due[n] = self.free[link] + latency

    def plan_begin(self, n):
        self.stage[n] = 0
        self.plan_launch(n)
        return (n, None, 0)

    def plan_advance(self, n):
        step = self.stage[n]
        self.now = max(self.now, self.due.pop(n)) + STAGE_TIME
        self.stage[n] += 1
        last = (len(PATH) if n < len(self.buckets) else 3) - 1
        if step < last:
            self.plan_launch(n)
        todo = [(n, step, step + 1 if step < last else None)]
        if n < len(self.buckets):
            self.summed += PATH[step] == "deep"
        norm = len(self.buckets) + 1
        if self.summed == len(self.buckets) and norm not in self.stage:
            todo.append(self.plan_begin(norm))
        return todo

    def plan(self, spent):
        self.now += spent
        todo = []
        for n in sorted(self.due):
            if self.due[n] + 0.8 <= self.now:
                todo += self.plan_advance(n)
        return todo

    def run(self, todo):
        for n, ended, begun in todo:
            if n < len(self.buckets):
                if ended is not None:
                    self.end_transfer(n, PATH[ended])
                if begun is not None:
                    self.begin_transfer(n, PATH[begun])
            else:
                tile = n - len(self.buckets)
                if tile == 1 and ended is None:
                    self.tile_out[1, 0] = self.squares[...]
                if ended is not None:
                    self.tile_finish(tile, ended)
                if begun is not None:
                    self.tile_start(tile, begun)

    def begin(self, n):
        self.run([self.plan_begin(n)])

    def tick(self, spent):
        self.run(self.plan(spent))

    def drain(self):
        while self.due:
            self.run(self.plan_advance(min(self.due, key=lambda n: (self.due[n], n))))

    def tile_copies(self, tile, phase):
        if phase == 0:
            slots, peers = [0], [self.sibling]
        elif phase == 1:
            slots = list(range(1, self.seq_size))
            peers = [{"seq": lax.rem(self.me + k, self.seq_size)} for k in slots]
        else:
            slots = [3 + k for k in range(1, self.deep)]
            peers = [self.deep_peer(k) for k in range(1, self.deep)]
        n = len(self.buckets) + tile
        return [
            self.copy(self.tile_out.at[tile, phase], self.tile_in.at[tile, slot], n, slot, peer)
            for slot, peer in zip(slots, peers)
        ], slots

    def tile_start(self, tile, phase):
        self.start(self.tile_copies(tile, phase)[0])

    def tile_finish(self, tile, phase):
        copies, slots = self.tile_copies(tile, phase)
        self.wait(copies)
        both = self.tile_out[tile, phase]
        for slot in slots:
            both = both + self.tile_in[tile, slot]
        self.tile_out[tile, phase + 1] = both


def exchange_slots(dp_size):
    return 2 * (4 + dp_size // 2 - 1)


def step_kernel(
    layers,
    sizes,
    buckets,
    codes_ref,
    actions_ref,
    next_ref,
    lengths_ref,
    rewards_ref,
    continues_ref,
    values_ref,
    trig_ref,
    table_ref,
    attn_in_ref,
    attn_out_ref,
    ffn_in_ref,
    ffn_out_ref,
    gains_ref,
    readout_ref,
    out_ref,
    scal_ref,
    wq,
    wo,
    wu,
    wd,
    rt,
    tb,
    xs,
    hs,
    qs,
    kvs,
    probs,
    acts,
    gds,
    mixes,
    lows,
    tokf,
    toki,
    gouts,
    gx,
    gl,
    dmix,
    dqkv,
    carried,
    dgain,
    lossacc,
    lam,
    bsend,
    brecv,
    send_sem,
    recv_sem,
    load_sem,
    table_f,
    readout_f,
    grads_ref,
    *exchange_refs,
):
    batch, span = codes_ref.shape
    dims = gains_ref.shape[1]
    ff = ffn_in_ref.shape[2]
    tiles = span // SEG
    pairs = span // QRY
    total = batch * span
    chunks = total // ROWS
    per_seq = span // ROWS
    vocab_all = table_ref.shape[0]
    outs_all = readout_ref.shape[0]
    head_dim = dims // HEADS
    scale = head_dim ** (-0.5)
    exp_scale = scale * math.log2(math.e)
    groups = HEADS // 2
    base = lax.axis_index("seq") * span
    me = lax.axis_index("seq")
    seq_size = sizes[0]
    right = lax.rem(me + 1, seq_size)
    left = lax.rem(me + seq_size - 1, seq_size)

    ex = Exchange(*sizes, buckets, grads_ref, out_ref, *exchange_refs)
    ex.greet()
    ex.squares[...] = jnp.zeros_like(ex.squares)

    loads = [
        pltpu.make_async_copy(table_ref, table_f, load_sem.at[0]),
        pltpu.make_async_copy(readout_ref, readout_f, load_sem.at[1]),
    ]
    blocks = []
    for layer in range(layers):
        for j in range(3):
            blocks.append((attn_in_ref, wq, layer, slice(0, 256), slice(j * 256, j * 256 + 256)))
        blocks.append((attn_out_ref, wo, layer, slice(0, 256), slice(0, 256)))
        for j in range(ff // 256):
            blocks.append((ffn_in_ref, wu, layer, slice(0, 256), slice(j * 256, j * 256 + 256)))
        for j in range(ff // 256):
            blocks.append((ffn_out_ref, wd, layer, slice(j * 256, j * 256 + 256), slice(0, 256)))

    def place_of(k):
        at = (k + (2 * layers - 2) * chunks) % (2 * layers * chunks)
        return 1 + at // chunks, slice(256 * (at % chunks), 256 * (at % chunks) + 256)

    for k, (source, _, layer, rows, cols) in enumerate(blocks):
        plane, there = place_of(k)
        loads.append(
            pltpu.make_async_copy(source.at[layer, rows, cols], xs.at[plane, there, :], load_sem.at[2 + k])
        )
    for load in loads:
        load.start()

    def convert(low, high):
        for k in range(low, high):
            _, dest, layer, rows, cols = blocks[k]
            plane, there = place_of(k)
            loads[2 + k].wait()
            dest[layer, rows, cols] = xs[plane, there, :].astype(BF)

    tb[...] = jnp.zeros_like(tb)
    rt[...] = jnp.zeros_like(rt)

    ends = []
    for b in range(batch):
        run = jnp.int32(0)
        row = []
        for e in range(lengths_ref.shape[1]):
            run = run + lengths_ref[b, e]
            row.append(run)
        ends.append(row)
    episodes = len(ends[0])

    lane = iota((8, span), 1)
    lam[...] = jnp.zeros_like(lam)
    lam[0, 0:batch, :] = rewards_ref[...]
    lam[1, 0:batch, :] = continues_ref[...]
    lam[2, 0:batch, :] = values_ref[...]
    last = lax.rem(lane, SEG) == SEG - 1
    decay = GAMMA * lam[1]
    value_next = pltpu.roll(lam[2], span - 1, 1)
    add = jnp.where(last, lam[2], lam[0] + decay * ((1.0 - LAMBDA_RET) * value_next))
    mul = jnp.where(last, 0.0, decay * LAMBDA_RET)
    step = 1
    while step < SEG:
        add = add + mul * pltpu.roll(add, span - step, 1)
        mul = mul * pltpu.roll(mul, span - step, 1)
        step *= 2
    lam[3] = add
    valid_rows = []
    for b in range(batch):
        after = iota((1, span), 1) + (base + 1)
        final = after == ends[b][0]
        for e in range(1, episodes):
            final = final | (after == ends[b][e])
        valid_rows.append(jnp.where(final, 0.0, 1.0))
    for c in range(chunks):
        b = c // per_seq
        lanes = slice((c % per_seq) * ROWS, (c % per_seq) * ROWS + ROWS)
        for row in range(4):
            tokf[c, row : row + 1, :] = lam[row, b : b + 1, lanes]
        tokf[c, 4:5, :] = valid_rows[b][:, lanes]
        toki[c, 0:1, :] = codes_ref[b : b + 1, lanes]
        toki[c, 1:2, :] = actions_ref[b : b + 1, lanes]
        toki[c, 2:3, :] = next_ref[b : b + 1, lanes]

    half = dims // 2
    in_sin, in_cos = trig_ref[0:SEG, 2, :], trig_ref[0:SEG, 3, :]
    end_sin, end_cos = [], []
    for b in range(batch):
        for e in range(episodes):
            far, near = lax.div(ends[b][e], SEG), lax.rem(ends[b][e], SEG)
            far_sin, far_cos = trig_ref[far, 0:1, :], trig_ref[far, 1:2, :]
            near_sin, near_cos = trig_ref[near, 2:3, :], trig_ref[near, 3:4, :]
            end_sin.append(far_sin * near_cos + far_cos * near_sin)
            end_cos.append(far_cos * near_cos - far_sin * near_sin)

    def marks(tile, carry):
        at = me * tiles + tile
        tile_sin, tile_cos = trig_ref[at, 0:1, :], trig_ref[at, 1:2, :]
        here_sin = in_sin * tile_cos + in_cos * tile_sin
        here_cos = in_cos * tile_cos - in_sin * tile_sin
        place = iota((SEG, half), 0) + (base + tile * SEG)
        for b in range(batch):
            start_sin = jnp.zeros((SEG, half), F32)
            start_cos = jnp.ones((SEG, half), F32)
            for e in range(episodes):
                passed = place >= ends[b][e]
                row = b * episodes + e
                start_sin = jnp.where(passed, end_sin[row], start_sin)
                start_cos = jnp.where(passed, end_cos[row], start_cos)
            rows = pl.ds(pl.multiple_of(b * span + tile * SEG, SEG), SEG)
            xs[0, rows, 0:half] = here_sin * start_cos - here_cos * start_sin
            xs[0, rows, half:dims] = here_cos * start_cos + here_sin * start_sin
        return carry

    lax.fori_loop(0, tiles, marks, 0, unroll=4)

    def lowest(pair, carry):
        within = lax.rem(iota((8, groups * QRY), 1), QRY)
        first = base + pair * QRY - SEG
        place = within + (base + pair * QRY)
        for b in range(batch):
            low = jnp.where(within >= SEG, SEG, 0)
            for e in range(episodes):
                low = jnp.where(place >= ends[b][e], jnp.maximum(low, ends[b][e] - first), low)
            lows[b * pairs + pair] = jnp.maximum(low, -first)
        return carry

    lax.fori_loop(0, pairs, lowest, 0, unroll=4)

    def chunk_rows(c):
        return pl.ds(pl.multiple_of(c * ROWS, ROWS), ROWS)

    def kv_rows(c):
        return pl.ds(pl.multiple_of(lax.rem(c, per_seq) * ROWS + SEG, 16), ROWS)

    loads[0].wait()
    tb[0:vocab_all, :] = table_f[...].astype(BF)

    def onehot(c):
        code = toki[c, 0:1, :]
        act = toki[c, 1:2, :] + VOCAB
        ids = iota((OUTS, ROWS), 0)
        return jnp.where((ids == code) | (ids == act), 1.0, 0.0).astype(BF)

    def three_chunks(i):
        return tuple(3 * i + j for j in range(3))

    def embed(i, carry):
        for c in range(chunks):
            xs[0, chunk_rows(c), :] += dot_tn(onehot(c), tb[...])
        return carry

    lax.fori_loop(0, 1, embed, 0)

    lane_head = iota((1, dims), 1) // head_dim
    group_mask = [jnp.where(lane_head // 2 == g, 1.0, 0.0).astype(BF) for g in range(groups)]
    even_mask = jnp.where(lax.rem(lane_head, 2) == 0, 1.0, 0.0).astype(BF)
    odd_mask = jnp.where(lax.rem(lane_head, 2) == 1, 1.0, 0.0).astype(BF)
    even_f = lax.rem(lane_head, 2) == 0

    def by_group(rows):
        return jnp.concatenate([rows * group_mask[g] for g in range(groups)], axis=0)

    def both(keys):
        return jnp.concatenate([keys * even_mask, keys * odd_mask], axis=0)

    def gather_heads(wide):
        out = wide[0:QRY]
        for g in range(1, groups):
            out = jnp.where(lane_head // 2 == g, wide[g * QRY : g * QRY + QRY], out)
        return out

    def forward_copy(layer):
        return pltpu.make_async_remote_copy(
            src_ref=kvs.at[layer, :, pl.ds(span, SEG), :],
            dst_ref=kvs.at[layer, :, pl.ds(0, SEG), :],
            send_sem=send_sem.at[layer],
            recv_sem=recv_sem.at[layer],
            device_id={"seq": right},
            device_id_type=MESH,
        )

    def backward_copy(layer):
        return pltpu.make_async_remote_copy(
            src_ref=bsend.at[layer],
            dst_ref=brecv.at[layer],
            send_sem=send_sem.at[layers + layer],
            recv_sem=recv_sem.at[layers + layer],
            device_id={"seq": left},
            device_id_type=MESH,
        )

    def project(layer):
        gain = gains_ref[2 * layer : 2 * layer + 1, :]

        def body(i, carry):
            pieces = [(c, chunk_rows(c)) for c in range(chunks)]
            normed = [rms_apply(xs[2 * layer, rows, :], gain) for _, rows in pieces]
            wide = [dot_nn(h, wq[layer]).astype(BF) for h in normed]
            for (c, rows), h, qkv in zip(pieces, normed, wide):
                hs[2 * layer, rows, :] = h
                qs[layer, rows, :] = qkv[:, 0:dims]
                kvs[layer, c // per_seq, kv_rows(c), :] = qkv[:, dims:]
            return carry

        lax.fori_loop(0, 1, body, 0)

    def pair_rows(b, pair):
        return pl.ds(pl.multiple_of(b * span + pair * QRY, 16), QRY)

    def pair_window(pair):
        return pl.ds(pl.multiple_of(pair * QRY, 16), KEY)

    causal = iota((KEY, groups * QRY), 0) <= lax.rem(iota((KEY, groups * QRY), 1), QRY) + SEG
    key_place = iota((KEY, groups * QRY), 0)

    def attend(layer):
        copy = forward_copy(layer)

        def body(i, carry):
            items = [(b, pairs - 1 - PER * i - j) for j in range(PER) for b in range(batch)]
            pl.when(i == pairs // PER - 1)(copy.wait)
            scores = []
            for b, pair in items:
                keys = kvs[layer, b, pair_window(pair), 0:dims]
                scores.append(dot_nt(both(keys), by_group(qs[layer, pair_rows(b, pair), :])))
            weights = []
            for (b, pair), score in zip(items, scores):
                seen = causal & (key_place >= lows[b * pairs + pair, 0:1, :])
                sides = []
                for side in range(2):
                    s = jnp.where(seen, score[side * KEY : side * KEY + KEY], NEG)
                    top = jnp.max(s, axis=0, keepdims=True)
                    e = jnp.exp2((s - top) * exp_scale)
                    sides.append((e * (1.0 / jnp.sum(e, axis=0, keepdims=True))).astype(BF))
                p = jnp.concatenate(sides, axis=0)
                probs[layer, b * pairs + pair] = p
                weights.append(p)
            for (b, pair), p in zip(items, weights):
                values = kvs[layer, b, pair_window(pair), dims:]
                wide = dot_tn(p, both(values))
                mixes[layer, pair_rows(b, pair), :] = gather_heads(wide).astype(BF)
            return carry

        copy.start()
        lax.fori_loop(0, pairs // PER, body, 0)

    def feed(layer):
        gain = gains_ref[2 * layer + 1 : 2 * layer + 2, :]
        c0, c1 = math.sqrt(2.0 / math.pi), 0.044715

        def body(i, carry):
            pieces = [chunk_rows(c) for c in three_chunks(i)]
            mids = [xs[2 * layer, rows, :] + dot_nn(mixes[layer, rows, :], wo[layer]) for rows in pieces]
            normed = [rms_apply(x, gain) for x in mids]
            for rows, x, h in zip(pieces, mids, normed):
                xs[2 * layer + 1, rows, :] = x
                hs[2 * layer + 1, rows, :] = h
            hidden = [[], [], []]
            for j in range(ff // 256):
                cols = slice(j * 256, j * 256 + 256)
                for rows, h, parts in zip(pieces, normed, hidden):
                    up = dot_nn(h, wu[layer, :, cols])
                    square = up * up
                    half_t = 0.5 + 0.5 * jnp.tanh(up * (c0 + (c0 * c1) * square))
                    act = up * half_t
                    slope = half_t + (1.0 - half_t) * act * (2.0 * c0 + (6.0 * c0 * c1) * square)
                    parts.append(act.astype(BF))
                    gds[layer, rows, cols] = slope.astype(BF)
            for rows, x, parts in zip(pieces, mids, hidden):
                act = jnp.concatenate(parts, axis=1)
                acts[layer, rows, :] = act
                xs[2 * layer + 2, rows, :] = x + dot_nn(act, wd[layer])
            return carry

        lax.fori_loop(0, chunks // 3, body, 0)

    per_layer = 4 + 2 * (ff // 256)
    for layer in range(layers):
        if layer == 0:
            convert(0, 3)
        project(layer)
        if layer == 0:
            ex.greeted()
        attend(layer)
        if layer == 0:
            convert(3, layers * per_layer)
        feed(layer)
    loads[1].wait()
    rt[0:outs_all, :] = readout_f[...].astype(BF)

    lossacc[...] = jnp.zeros_like(lossacc)
    dgain[...] = jnp.zeros_like(dgain)
    top_gain = gains_ref[2 * layers : 2 * layers + 1, :]

    def put(at, block):
        for side in range(2):
            cols = slice(side * 128, side * 128 + 128)
            grads_ref[side, at : at + block.shape[0], :] = block[:, cols].astype(BF)

    def loss_grad(c, outs):
        reward, cont = tokf[c, 0:1, :], tokf[c, 1:2, :]
        target, ret, valid = tokf[c, 2:3, :], tokf[c, 3:4, :], tokf[c, 4:5, :]
        action, code = toki[c, 1:2, :], toki[c, 2:3, :]
        logits = outs[0:VOCAB]
        top = jnp.max(logits, axis=0, keepdims=True)
        e = jnp.exp(logits - top)
        esum = jnp.sum(e, axis=0, keepdims=True)
        chosen = iota((VOCAB, ROWS), 0) == code
        picked = jnp.sum(jnp.where(chosen, logits, 0.0), axis=0, keepdims=True)
        loss = jnp.log(esum) + top - picked
        grad_logits = (e * (valid / esum) - jnp.where(chosen, valid, 0.0)).astype(BF)
        small = outs[VOCAB:OUTS]
        place = iota((OUTS - VOCAB, ROWS), 0)
        reward_err = small[0:1] - reward
        end_logit = small[1:2]
        value_err = small[2:3] - ret
        minus = jnp.exp(-jnp.abs(end_logit))
        soft = jnp.maximum(end_logit, 0.0) + jnp.log(1.0 + minus)
        sigmoid = jnp.where(end_logit >= 0.0, 1.0, minus) / (1.0 + minus)
        loss = loss + 0.5 * reward_err * reward_err + soft - cont * end_logit
        loss = loss + 0.5 * value_err * value_err
        actor = (place >= 3) & (place < outs_all - VOCAB)
        act_top = jnp.max(jnp.where(actor, small, NEG), axis=0, keepdims=True)
        act_e = jnp.where(actor, jnp.exp(jnp.where(actor, small - act_top, 0.0)), 0.0)
        act_sum = jnp.sum(act_e, axis=0, keepdims=True)
        log_pi = jnp.where(actor, small - act_top - jnp.log(act_sum), 0.0)
        pi = act_e / act_sum
        neg_entropy = jnp.sum(pi * log_pi, axis=0, keepdims=True)
        taken = place == action + 3
        picked_pi = jnp.sum(jnp.where(taken, log_pi, 0.0), axis=0, keepdims=True)
        gap = ret - target
        loss = loss - gap * picked_pi + ENTROPY_COEF * neg_entropy
        grad = gap * (pi - jnp.where(taken, 1.0, 0.0))
        grad = grad + ENTROPY_COEF * pi * (log_pi - neg_entropy)
        grad = jnp.where(actor, grad, 0.0)
        grad = jnp.where(place == 0, reward_err, grad)
        grad = jnp.where(place == 1, sigmoid - cont, grad)
        grad = jnp.where(place == 2, value_err, grad)
        lossacc[0:1, :] += loss * valid
        lossacc[1:2, :] += valid
        return jnp.concatenate([grad_logits, (grad * valid).astype(BF)], axis=0)

    def losses(i, carry):
        pieces = [(c, chunk_rows(c)) for c in three_chunks(i)]
        hidden = [xs[2 * layers, rows, :] for _, rows in pieces]
        normed = [rms_apply(x, top_gain) for x in hidden]
        outs = [dot_nt(rt[...], h) for h in normed]
        found = [loss_grad(c, out) for (c, _), out in zip(pieces, outs)]
        pulled = [dot_tn(grad, rt[...]) for grad in found]
        for (c, rows), x, h, grad, dh in zip(pieces, hidden, normed, found, pulled):
            hs[2 * layers, rows, :] = h
            gouts[:, rows] = grad
            grad_x, part = rms_pull(dh, x, top_gain)
            gx[rows, :] = grad_x
            gl[rows, :] = grad_x.astype(BF)
            dgain[2 * layers] += part
        return carry

    lax.fori_loop(0, chunks // 3, losses, 0)
    tail_at = VOCAB + layers * 12 * 256 + OUTS
    put(0, dot_nn(gouts[0:VOCAB, :], hs[2 * layers]))
    put(tail_at, dot_nn(gouts[VOCAB:OUTS, :], hs[2 * layers]))
    loss_total = jnp.sum(lossacc[0:1, :])
    count_total = jnp.sum(lossacc[1:2, :])
    place = iota(scal_ref.shape, 0)
    ex.tile_out[0, 0] = jnp.where(place == 0, loss_total, jnp.where(place == 1, count_total, 0.0))
    ex.begin(len(buckets))

    def spread(count, spent, body):
        plans = [ex.plan(spent / count) for _ in range(count)]

        def run(i, carry):
            body(i)
            for k, todo in enumerate(plans):
                if todo:
                    pl.when(i == k)(functools.partial(ex.run, todo))
            return carry

        lax.fori_loop(0, count, run, 0)

    def feed_back(layer):
        gain = gains_ref[2 * layer + 1 : 2 * layer + 2, :]

        def body(i):
            pieces = [chunk_rows(c) for c in three_chunks(i)]
            hidden = [[], [], []]
            for j in range(ff // 256):
                cols = slice(j * 256, j * 256 + 256)
                for rows, parts in zip(pieces, hidden):
                    da = dot_nt(gl[rows, :], wd[layer, cols, :])
                    parts.append((da * gds[layer, rows, cols].astype(F32)).astype(BF))
            hidden = [jnp.concatenate(parts, axis=1) for parts in hidden]
            pulled = [dot_nt(du, wu[layer]) for du in hidden]
            for rows, du, dh in zip(pieces, hidden, pulled):
                gds[layer, rows, :] = du
                grad_x, part = rms_pull(dh, xs[2 * layer + 1, rows, :], gain)
                dgain[2 * layer + 1] += part
                grad = gx[rows, :] + grad_x
                gx[rows, :] = grad
                low = grad.astype(BF)
                gl[rows, :] = low
                dmix[rows, :] = dot_nt(low, wo[layer]).astype(BF)

        spread(chunks // 3, 3.3, body)

    def attend_back(layer):
        def steps(i):
            items = [(b, PER * i + j) for j in range(PER) for b in range(batch)]
            keys, values, queries, douts = [], [], [], []
            for b, pair in items:
                window, rows = pair_window(pair), pair_rows(b, pair)
                keys.append(both(kvs[layer, b, window, 0:dims]))
                values.append(both(kvs[layer, b, window, dims:]))
                queries.append(by_group(qs[layer, rows, :]))
                douts.append(by_group(dmix[rows, :]))
            weights = [probs[layer, b * pairs + pair] for b, pair in items]
            pulled = [dot_nt(value, dout) for value, dout in zip(values, douts)]
            slopes = []
            for p, dp in zip(weights, pulled):
                sides = []
                for side in range(2):
                    part = slice(side * KEY, side * KEY + KEY)
                    pf = p[part].astype(F32)
                    d = dp[part]
                    sides.append((pf * (d - jnp.sum(d * pf, axis=0, keepdims=True))).astype(BF))
                slopes.append(jnp.concatenate(sides, axis=0))
            for (b, pair), ds, key in zip(items, slopes, keys):
                dqkv[pair_rows(b, pair), 0:dims] = (gather_heads(dot_tn(ds, key)) * scale).astype(BF)
            wide = []
            for ds, query, p, dout in zip(slopes, queries, weights, douts):
                dk = dot_nn(ds, query) * scale
                dv = dot_nn(p, dout)
                dk = jnp.where(even_f, dk[0:KEY], dk[KEY:])
                wide.append(jnp.concatenate([dk, jnp.where(even_f, dv[0:KEY], dv[KEY:])], axis=1))
            return items, wide

        def keep(items, wide):
            before = [carried[b] + wide[b][0:SEG] for b in range(batch)]
            for at, (b, pair) in enumerate(items):
                rows = pl.multiple_of(b * span + pair * QRY, 16)
                if QRY > SEG:
                    dqkv[pl.ds(rows, QRY - SEG), dims:] = wide[at][SEG:QRY].astype(BF)
                if at + batch < len(items):
                    ending = wide[at][QRY:] + wide[at + batch][0:SEG]
                    dqkv[pl.ds(pl.multiple_of(rows + QRY - SEG, 16), SEG), dims:] = ending.astype(BF)
                else:
                    carried[b] = wide[at][QRY:]
            return before

        copy = backward_copy(layer)

        def body(i):
            before = [rows.astype(BF) for rows in keep(*steps(i))]

            @pl.when(i == 0)
            def _():
                for b in range(batch):
                    bsend[layer, b] = before[b]
                copy.start()

            @pl.when(i > 0)
            def _():
                for b in range(batch):
                    rows = pl.ds(pl.multiple_of(b * span + i * PER * QRY - SEG, 16), SEG)
                    dqkv[rows, dims:] = before[b]

        carried[...] = jnp.zeros_like(carried)
        spread(pairs // PER, 6.0, body)
        copy.wait()
        for b in range(batch):
            final = carried[b] + brecv[layer, b].astype(F32)
            dqkv[b * span + span - SEG : b * span + span, dims:] = final.astype(BF)

    def project_back(layer):
        gain = gains_ref[2 * layer : 2 * layer + 1, :]

        def body(i):
            pieces = [chunk_rows(c) for c in three_chunks(i)]
            pulled = [dot_nt(dqkv[rows, :], wq[layer]) for rows in pieces]
            for rows, dh in zip(pieces, pulled):
                grad_x, part = rms_pull(dh, xs[2 * layer, rows, :], gain)
                dgain[2 * layer] += part
                grad = gx[rows, :] + grad_x
                gx[rows, :] = grad
                gl[rows, :] = grad.astype(BF)

        spread(chunks // 3, 1.5, body)

    at = VOCAB
    bucket = 0
    for layer in reversed(range(layers)):
        for j in range(ff // 256):
            cols = slice(j * 256, j * 256 + 256)
            put(at, dot_tn(acts[layer, :, cols], gl[...]))
            at += 256
        ex.begin(bucket)
        ex.tick(1.2)
        feed_back(layer)
        for j in range(ff // 256):
            cols = slice(j * 256, j * 256 + 256)
            put(at, dot_tn(hs[2 * layer + 1], gds[layer, :, cols]))
            at += 256
            if j % 2:
                ex.tick(0.4)
        put(at, dot_tn(mixes[layer], gl[...]))
        at += 256
        ex.begin(bucket + 1)
        ex.tick(0.2)
        attend_back(layer)
        for j in range(3):
            cols = slice(j * 256, j * 256 + 256)
            put(at, dot_tn(hs[2 * layer], dqkv[:, cols]))
            at += 256
        bucket += 2
        if layer == 0:
            ex.begin(bucket)
        ex.tick(0.7)
        project_back(layer)

    def mark(c, carry):
        gouts[:, chunk_rows(c)] = onehot(c)
        return carry

    lax.fori_loop(0, chunks, mark, 0)
    put(at, dot_nn(gouts[...], gl[...]))
    ex.tick(1.6)
    at = tail_at + OUTS - VOCAB
    place = iota((16, dims), 0)
    gain_rows = jnp.zeros((16, dims), F32)
    for index in range(2 * layers + 1):
        gain_rows = jnp.where(place == index, jnp.sum(dgain[index], axis=0, keepdims=True), gain_rows)
    put(at, gain_rows)
    at += 16
    put(at, jnp.zeros((grads_ref.shape[1] - at, dims), F32))
    ex.begin(len(buckets) - 1)
    ex.drain()
    count = ex.tile_out[0, 3, 1:2, 0:1]
    norm = jnp.sqrt(jnp.sum(ex.tile_out[1, 3]) / (count * count))
    place = iota(scal_ref.shape, 0)
    scal = jnp.where(place == 2, norm, ex.tile_out[0, 3])
    scal_ref[...] = jnp.where(place == 3, jnp.minimum(1.0, CLIP_NORM / norm) / count, scal)
    for n in range(len(buckets)):
        ex.wait(ex.out_copies(n))


def gradients(codes, actions, next_codes, lengths, rewards, continues, values, weights, sizes):
    table, attn_in, attn_out, ffn_in, ffn_out, gains, readout = weights
    batch, span = codes.shape
    layers, dims, ff = ffn_in.shape
    total = batch * span
    tiles = span // SEG
    chunks = total // ROWS
    grad_rows = grad_row_count(layers)
    buckets = buckets_of(layers)
    seq_size, dp_size = sizes
    shares = [(b[1] - b[0]) // seq_size // owners_of(b, seq_size, dp_size // 2) for b in buckets]
    slots = exchange_slots(dp_size)
    hbm = pl.BlockSpec(memory_space=pltpu.HBM)
    steps = np.arange(lax.axis_size("seq") * tiles + 1, dtype=np.float64)[:, None]
    freq = np.exp(np.arange(dims // 2) * (-2.0 * math.log(10000.0) / dims))
    trig = np.zeros((steps.shape[0], 8, dims // 2), np.float32)
    trig[:, 0], trig[:, 1] = np.sin(steps * SEG * freq), np.cos(steps * SEG * freq)
    trig[:, 2], trig[:, 3] = np.sin(steps * freq), np.cos(steps * freq)
    trig = jnp.asarray(trig)
    vmem = pl.BlockSpec(memory_space=pltpu.VMEM)
    smem = pl.BlockSpec(memory_space=pltpu.SMEM)
    return pl.pallas_call(
        functools.partial(step_kernel, layers, sizes, buckets),
        out_shape=(
            jax.ShapeDtypeStruct((2, grad_rows, dims // 2), BF),
            jax.ShapeDtypeStruct((8, 128), F32),
        ),
        in_specs=[vmem] * 3 + [smem] + [vmem] * 4 + [hbm] * 5 + [vmem, hbm],
        out_specs=(hbm, vmem),
        scratch_shapes=[
            pltpu.VMEM((layers, dims, 3 * dims), BF),
            pltpu.VMEM((layers, dims, dims), BF),
            pltpu.VMEM((layers, dims, ff), BF),
            pltpu.VMEM((layers, ff, dims), BF),
            pltpu.VMEM((OUTS, dims), BF),
            pltpu.VMEM((OUTS, dims), BF),
            pltpu.VMEM((2 * layers + 1, total, dims), F32),
            pltpu.VMEM((2 * layers + 1, total, dims), BF),
            pltpu.VMEM((layers, total, dims), BF),
            pltpu.VMEM((layers, batch, SEG + span, 2 * dims), BF),
            pltpu.VMEM((layers, total // QRY, 2 * KEY, HEADS // 2 * QRY), BF),
            pltpu.VMEM((layers, total, ff), BF),
            pltpu.VMEM((layers, total, ff), BF),
            pltpu.VMEM((layers, total, dims), BF),
            pltpu.VMEM((total // QRY, 8, HEADS // 2 * QRY), jnp.int32),
            pltpu.VMEM((chunks, 8, ROWS), F32),
            pltpu.VMEM((chunks, 8, ROWS), jnp.int32),
            pltpu.VMEM((OUTS, total), BF),
            pltpu.VMEM((total, dims), F32),
            pltpu.VMEM((total, dims), BF),
            pltpu.VMEM((total, dims), BF),
            pltpu.VMEM((total, 3 * dims), BF),
            pltpu.VMEM((batch, SEG, 2 * dims), F32),
            pltpu.VMEM((2 * layers + 1, 8, dims), F32),
            pltpu.VMEM((8, ROWS), F32),
            pltpu.VMEM((4, 8, span), F32),
            pltpu.VMEM((layers, batch, SEG, 2 * dims), BF),
            pltpu.VMEM((layers, batch, SEG, 2 * dims), BF),
            pltpu.SemaphoreType.DMA((2 * layers,)),
            pltpu.SemaphoreType.DMA((2 * layers,)),
            pltpu.SemaphoreType.DMA((2 + 12 * layers,)),
            pltpu.VMEM(table.shape, F32),
            pltpu.VMEM(readout.shape, F32),
            pltpu.VMEM((2, grad_rows, dims // 2), BF),
            pltpu.VMEM((grad_rows, dims // 2), BF),
            pltpu.VMEM((seq_size - 1, grad_rows // seq_size, dims // 2), BF),
            pltpu.VMEM((grad_rows // seq_size, dims // 2), BF),
            pltpu.VMEM((dp_size // 2 - 1, sum(shares), dims // 2), BF),
            pltpu.VMEM((8, dims // 2), F32),
            pltpu.VMEM((2, 4, 8, 128), F32),
            pltpu.VMEM((2, slots // 2, 8, 128), F32),
            pltpu.SemaphoreType.DMA((len(buckets) + 2, slots)),
            pltpu.SemaphoreType.DMA((len(buckets) + 2, slots)),
            pltpu.SemaphoreType.DMA((len(buckets), 2)),
        ],
        compiler_params=pltpu.CompilerParams(
            collective_id=0, has_side_effects=True, vmem_limit_bytes=63 * 1024 * 1024
        ),
        name="train_step",
    )(
        codes,
        actions,
        next_codes,
        lengths,
        rewards,
        continues,
        values,
        trig,
        table,
        attn_in,
        attn_out,
        ffn_in,
        ffn_out,
        gains,
        readout,
    )


def adam_update(weight, first_mom, second_mom, clipped, rate):
    new_first = BETA_ONE * first_mom + (1.0 - BETA_ONE) * clipped
    new_second = BETA_TWO * second_mom + (1.0 - BETA_TWO) * clipped * clipped
    root = jnp.sqrt(new_second * (1.0 / (1.0 - BETA_TWO**STEP))) + ADAM_EPS
    ratio = new_first * (rate / (1.0 - BETA_ONE**STEP)) / root
    return (weight * (1.0 - rate * DECAY) - ratio, new_first, new_second)


AHEAD = 5


def update_kernel(layers, scal_ref, sums_ref, *refs):
    ins, outs, scalars, here = refs[0:21], refs[21:42], refs[42:45], refs[45:66]
    load_sem, store_sem, sum_sem, grads_ref = refs[66:]
    scale = scal_ref[3, 0]
    for k, ref in enumerate(scalars):
        ref[0, 0] = scal_ref[k, 0]
    pieces = [(slot, layer) for slot in (4, 3, 1, 2) for layer in range(layers)]
    pieces += [(0, None), (5, None), (6, None)]

    offset = VOCAB
    starts = {}
    for layer in reversed(range(layers)):
        starts[4, layer] = offset
        starts[3, layer] = offset + 4 * 256
        starts[2, layer] = offset + 8 * 256
        starts[1, layer] = offset + 9 * 256
        offset += 12 * 256
    table_at, tail_at = offset, offset + OUTS
    gains_at = tail_at + OUTS - VOCAB

    def view(ref, layer):
        return ref if layer is None else ref.at[layer]

    def moves(n, kind):
        slot, layer = pieces[n]
        for part in range(3):
            index = 3 * slot + part
            inside = view(here[index], layer)
            if kind == 0:
                yield pltpu.make_async_copy(view(ins[index], layer), inside, load_sem.at[n, part])
            else:
                yield pltpu.make_async_copy(inside, view(outs[index], layer), store_sem.at[n, part])

    def fetch(n):
        slot, layer = pieces[n]
        rows = {0: (table_at, OUTS), 6: (0, VOCAB), 5: (tail_at, sums_ref.shape[1] - tail_at)}
        if layer is not None:
            rows[slot] = (starts[slot, layer], here[3 * slot].shape[1] * here[3 * slot].shape[2] // 256)
        at, count = rows[slot]
        part = pl.ds(at, count)
        return pltpu.make_async_copy(sums_ref.at[:, part], grads_ref.at[:, part], sum_sem.at[n])

    def begin(n):
        for move in moves(n, 0):
            move.start()
        fetch(n).start()

    for n in range(AHEAD):
        begin(n)

    def renew(slot, layer, rows, cols, grad):
        refs = [view(here[3 * slot + part], layer) for part in range(3)]
        new = adam_update(*[ref[rows, cols] for ref in refs], grad.astype(F32) * scale, RATES[slot])
        for ref, value in zip(refs, new):
            ref[rows, cols] = value

    for n, (slot, layer) in enumerate(pieces):
        if n + AHEAD < len(pieces):
            begin(n + AHEAD)
        for move in moves(n, 0):
            move.wait()
        fetch(n).wait()
        if layer is not None:
            rows_all, cols_all = here[3 * slot].shape[1:]
            at = starts[slot, layer]
            for j in range(rows_all // 256):
                for i in range(cols_all // 256):
                    for side in range(2):
                        cols = slice(i * 256 + side * 128, i * 256 + side * 128 + 128)

                        def body(k, carry):
                            rows = pl.ds(pl.multiple_of(j * 256 + k * 64, 64), 64)
                            block = at + (j + i) * 256 + k * 64
                            grad = grads_ref[side, pl.ds(pl.multiple_of(block, 64), 64), :]
                            renew(slot, layer, rows, cols, grad)
                            return carry

                        lax.fori_loop(0, 4, body, 0)
        elif slot == 0:
            rows_all = here[0].shape[0]
            for side in range(2):
                cols = slice(side * 128, side * 128 + 128)

                def body(k, carry):
                    rows = pl.ds(pl.multiple_of(k * 64, 64), 64)
                    block = pl.ds(pl.multiple_of(table_at + k * 64, 64), 64)
                    renew(0, None, rows, cols, grads_ref[side, block, :])
                    return carry

                full = rows_all // 64
                lax.fori_loop(0, full, body, 0)
                if rows_all % 64:
                    last = slice(full * 64, rows_all)
                    block = grads_ref[side, table_at + full * 64 : tail_at, :]
                    renew(0, None, last, cols, block.astype(F32)[0 : rows_all % 64])
        elif slot == 6:
            outs_all = here[18].shape[0]
            for side in range(2):
                cols = slice(side * 128, side * 128 + 128)

                def body(k, carry):
                    rows = pl.ds(pl.multiple_of(k * 64, 64), 64)
                    renew(6, None, rows, cols, grads_ref[side, rows, :])
                    return carry

                lax.fori_loop(0, VOCAB // 64, body, 0)
                rest = grads_ref[side, tail_at : tail_at + OUTS - VOCAB, :].astype(F32)
                renew(6, None, slice(VOCAB, outs_all), cols, rest[0 : outs_all - VOCAB])
        else:
            count = here[15].shape[0]
            for side in range(2):
                cols = slice(side * 128, side * 128 + 128)
                grad = grads_ref[side, gains_at : gains_at + 16, :].astype(F32)[0:count]
                renew(5, None, slice(0, count), cols, grad)
        for move in moves(n, 1):
            move.start()
    for n in range(len(pieces)):
        for move in moves(n, 1):
            move.wait()


def update(grads, scal, state):
    layers = state[3].shape[0]
    anywhere = pl.BlockSpec(memory_space=pltpu.HBM)
    pieces = 4 * layers + 3
    return pl.pallas_call(
        functools.partial(update_kernel, layers),
        out_shape=tuple(jax.ShapeDtypeStruct(x.shape, F32) for x in state)
        + (jax.ShapeDtypeStruct((1, 1), F32),) * 3,
        in_specs=[
            pl.BlockSpec(memory_space=pltpu.SMEM),
            anywhere,
        ]
        + [anywhere] * 21,
        out_specs=(anywhere,) * 21 + (pl.BlockSpec(memory_space=pltpu.SMEM),) * 3,
        scratch_shapes=[pltpu.VMEM(x.shape, F32) for x in state]
        + [
            pltpu.SemaphoreType.DMA((pieces, 3)),
            pltpu.SemaphoreType.DMA((pieces, 3)),
            pltpu.SemaphoreType.DMA((pieces,)),
            pltpu.VMEM(grads.shape, BF),
        ],
        compiler_params=pltpu.CompilerParams(vmem_limit_bytes=62 * 1024 * 1024),
        name="update",
    )(scal, grads, *state)


def local(codes, actions, next_codes, lengths, rewards, continues, target_values, *state):
    state = state[0:18] + tuple(value.T for value in state[18:21])
    params = state[0::3]
    seq_size, dp_size = lax.axis_size("seq"), lax.axis_size("dp")
    sizes = (seq_size, dp_size)
    grads, scal = gradients(
        codes, actions, next_codes, lengths, rewards, continues, target_values, params, sizes
    )
    results = list(update(grads, scal, state))
    results[18:21] = [value.T for value in results[18:21]]
    results[21:24] = [value.reshape(()) for value in results[21:24]]
    return tuple(results)


def solution(mesh):
    rows, whole = P("dp", "seq"), P()
    return jax.shard_map(
        local,
        mesh=mesh,
        in_specs=(rows, rows, rows, P("dp", None), rows, rows, rows) + (whole,) * 21,
        out_specs=(whole,) * 24,
        check_vma=False,
    )
```
